32 devices in a mesh: ctx: 8 (over y, x, core), fsdp: 4 (over z).
Axes of the slice: x: 2, y: 2, z: 4, core: 2. Of those that a mesh axis runs over, the one named last changes fastest.
Arguments:
- x_stream: float32 [4, 3, 2048, 512], P('fsdp', None, 'ctx'), may hold values from -6 to 6
- y_stream: float32 [4, 3, 2048, 512], P('fsdp', None, 'ctx'), may hold values from -6 to 6
- grad_x: float32 [4, 3, 2048, 512], P('fsdp', None, 'ctx'), may hold values from -6 to 6
- grad_y: float32 [4, 3, 2048, 512], P('fsdp', None, 'ctx'), may hold values from -6 to 6
- doc_start: int32 [4, 3, 2048], P('fsdp'), may hold values from 0 to 2047, as said below
- query_weight: bfloat16 [512, 512], P('fsdp'), may hold values from -0.25 to 0.25
- query_bias: bfloat16 [512], P('fsdp'), may hold values from -1.5 to 1.5
- key_weight: bfloat16 [512, 512], P('fsdp'), may hold values from -0.25 to 0.25
- value_weight: bfloat16 [512, 512], P('fsdp'), may hold values from -0.25 to 0.25
- value_bias: bfloat16 [512], P('fsdp'), may hold values from -0.14941406 to 0.14941406
- output_weight: bfloat16 [512, 512], P('fsdp'), may hold values from -6 to 6
- output_bias: bfloat16 [512], P('fsdp'), may hold values from -1.5 to 1.5
- first_gain: bfloat16 [512], P('fsdp'), may hold values from 0.5 to 1.5
- first_shift: bfloat16 [512], P('fsdp'), may hold values from -1.5 to 1.5
- hidden_weight: bfloat16 [512, 2048], P('fsdp'), may hold values from -0.25 to 0.25
- hidden_bias: bfloat16 [2048], P('fsdp'), may hold values from -1.5 to 1.5
- reduce_weight: bfloat16 [2048, 512], P('fsdp'), may hold values from -0.125 to 0.125
- reduce_bias: bfloat16 [512], P('fsdp'), may hold values from -1.5 to 1.5
- second_gain: bfloat16 [512], P('fsdp'), may hold values from 0.5 to 1.5
- second_shift: bfloat16 [512], P('fsdp'), may hold values from -1.5 to 1.5
Outputs:
- x_next: float32 [4, 3, 2048, 512], P('fsdp', None, 'ctx')
- y_next: float32 [4, 3, 2048, 512], P('fsdp', None, 'ctx')
- x_grad: float32 [4, 3, 2048, 512], P('fsdp', None, 'ctx')
- query_weight_grad: float32 [512, 512], P('fsdp')
- query_bias_grad: float32 [512], P('fsdp')
- key_weight_grad: float32 [512, 512], P('fsdp')
- value_weight_grad: float32 [512, 512], P('fsdp')
- value_bias_grad: float32 [512], P('fsdp')
- output_weight_grad: float32 [512, 512], P('fsdp')
- output_bias_grad: float32 [512], P('fsdp')
- first_gain_grad: float32 [512], P('fsdp')
- first_shift_grad: float32 [512], P('fsdp')
- hidden_weight_grad: float32 [512, 2048], P('fsdp')
- hidden_bias_grad: float32 [2048], P('fsdp')
- reduce_weight_grad: float32 [2048, 512], P('fsdp')
- reduce_bias_grad: float32 [512], P('fsdp')
- second_gain_grad: float32 [512], P('fsdp')
- second_shift_grad: float32 [512], P('fsdp')
The draws below stay inside these ranges and needn't reach their ends.
Inputs may be any that keep to these rules, and one draw needn't show every extreme that they name: doc_start[s, b, p] is the position, within micro-batch b of stream s, of the first token of the document that holds position p: it never falls along p, it is at most p, and it equals p where a document begins. In each stream one micro-batch holds one document of more than 2048 tokens that begins within the first 256 positions and runs to the last position; the documents before it hold 1 to 255 tokens together. In the other micro-batches the first document holds 1 to 2048 tokens, the last one is cut by the micro-batch's end, and every other one holds 1024 to 2048 tokens.
All inputs are finite; a program needn't handle non-finite values.
Results may differ from the reference program's by a relative error of at most 0.015.
Values may be sent and summed in bfloat16 or wider, within the bound.
A program may use at most 448 MiB of HBM per device.

```python
import math
import jax
import jax.numpy as jnp
from jax import lax

D = 512
HEADS = 8
HEAD = 64
FF = 2048
SEQ_DEV = 256
MB = 3
DOC_MIN = 1024
DOC_MAX = 2048
STREAMS = 4
LEN = 2048
N_CTX = 8


def doc_stream(key):
    key_long, key_lens, key_shift, key_first = jax.random.split(key, 4)
    long_pick = jax.random.randint(key_long, (), 0, MB)
    doc_slots = LEN // DOC_MIN + 2
    lengths = jax.random.randint(key_lens, (MB, doc_slots), DOC_MIN, DOC_MAX + 1)
    shifts = jax.random.randint(key_shift, (MB, 1), 0, DOC_MIN)
    begins = jnp.maximum(jnp.cumsum(lengths, axis=1) - lengths - shifts, 0)
    positions = jnp.arange(LEN, dtype=jnp.int32)
    short_starts = jnp.max(jnp.where(begins[:, :, None] <= positions[None, None, :], begins[:, :, None], 0), axis=1)
    first_cut = jax.random.randint(key_first, (), 1, SEQ_DEV)
    long_starts = jnp.where(positions >= first_cut, first_cut, 0)
    micro_rows = jnp.arange(MB)
    return jnp.where(micro_rows[:, None] == long_pick, long_starts[None, :], short_starts).astype(jnp.int32)


def draw_doc_start(key, part):
    stream_keys = jax.random.split(key, STREAMS)
    return jax.vmap(doc_stream)(stream_keys)


def block_levels(own_key, extent, pieces, smallest, largest):
    loudness, own = 1.0, jax.random.fold_in(own_key, 6)
    for dim, blocks in pieces:
        draws = jnp.exp(jax.random.uniform(jax.random.fold_in(own, dim), (blocks,), jnp.float32, smallest / len(pieces), largest / len(pieces)))
        loudness = loudness * jnp.repeat(draws, extent[dim] // blocks).reshape([-1 if axis == dim else 1 for axis in range(len(extent))])
    return loudness


def noise(key, extent, deviation, bound, cuts=(), kind=jnp.bfloat16):
    result = jax.random.normal(key, extent, jnp.float32) * deviation
    if len(cuts) > 0:
        result = block_levels(key, extent, cuts, -0.22, 0.18) * result
    return jnp.clip(result, min=-bound, max=bound).astype(kind)


def setup_inputs(seed: int = 0) -> dict:
    seeds = jax.random.split(jax.random.key(seed), 21)
    x_stream = noise(seeds[0], (STREAMS, MB, LEN, D), 1.0, 6.0, ((0, 4), (2, 8)), jnp.float32)
    y_stream = noise(seeds[1], (STREAMS, MB, LEN, D), 1.0, 6.0, ((0, 4), (2, 8)), jnp.float32)
    grad_x = noise(seeds[2], (STREAMS, MB, LEN, D), 1.0, 6.0, ((0, 4), (2, 8)), jnp.float32)
    grad_y = noise(seeds[3], (STREAMS, MB, LEN, D), 1.0, 6.0, ((0, 4), (2, 8)), jnp.float32)
    doc_start = draw_doc_start(jax.random.fold_in(seeds[20], 71), 0)
    query_weight = noise(seeds[5], (D, D), D ** -0.5, 0.25, ((0, 4),))
    query_bias = noise(seeds[6], (D,), 0.3, 1.5, ((0, 4),))
    key_weight = noise(seeds[7], (D, D), D ** -0.5, 0.25, ((0, 4),))
    value_weight = noise(seeds[8], (D, D), D ** -0.5, 0.25, ((0, 4),))
    value_bias = noise(seeds[9], (D,), 0.03, 0.14941406, ((0, 4),))
    output_weight = noise(seeds[10], (D, D), 1 ** -0.5, 6.0, ((0, 4),))
    output_bias = noise(seeds[11], (D,), 0.3, 1.5, ((0, 4),))
    first_gain = jnp.clip(1.0 + 0.1 * jax.random.normal(seeds[12], (D,), jnp.float32), 0.5, 1.5).astype(jnp.bfloat16)
    first_shift = noise(seeds[13], (D,), 0.3, 1.5, ((0, 4),))
    hidden_weight = noise(seeds[14], (D, FF), D ** -0.5, 0.25, ((0, 4),))
    hidden_bias = noise(seeds[15], (FF,), 0.3, 1.5, ((0, 4),))
    reduce_weight = noise(seeds[16], (FF, D), FF ** -0.5, 0.125, ((0, 4),))
    reduce_bias = noise(seeds[17], (D,), 0.3, 1.5, ((0, 4),))
    second_gain = jnp.clip(1.0 + 0.1 * jax.random.normal(seeds[18], (D,), jnp.float32), 0.5, 1.5).astype(jnp.bfloat16)
    second_shift = noise(seeds[19], (D,), 0.3, 1.5, ((0, 4),))
    return {"x_stream": x_stream, "y_stream": y_stream, "grad_x": grad_x, "grad_y": grad_y, "doc_start": doc_start, "query_weight": query_weight, "query_bias": query_bias, "key_weight": key_weight, "value_weight": value_weight, "value_bias": value_bias, "output_weight": output_weight, "output_bias": output_bias, "first_gain": first_gain, "first_shift": first_shift, "hidden_weight": hidden_weight, "hidden_bias": hidden_bias, "reduce_weight": reduce_weight, "reduce_bias": reduce_bias, "second_gain": second_gain, "second_shift": second_shift}


@jax.custom_vjp
def low(v):
    return lax.optimization_barrier(v.astype(jnp.bfloat16)).astype(jnp.float32)

@jax.custom_vjp
def low_back(v):
    return v

def low_keep(v):
    return (low(v), None)

def low_pass(kept, grad):
    return (grad,)

def back_keep(v):
    return (v, None)

def back_low(kept, grad):
    return (low(grad),)
low.defvjp(low_keep, low_pass)
low_back.defvjp(back_keep, back_low)

def highest(left, right):
    return jnp.dot(left, right, precision=lax.Precision.HIGHEST)

def layer_norm(total, gain, shift):
    mean_val = lax.optimization_barrier(jnp.mean(total, axis=-1, keepdims=True))
    centered = total - mean_val
    variance = lax.optimization_barrier(jnp.mean(centered * centered, axis=-1, keepdims=True))
    return centered * lax.rsqrt(variance + 1e-05) * gain + shift

def gelu_exact(hidden):
    return hidden * 0.5 * (1.0 + jax.scipy.special.erf(hidden * 0.7071067811865476))

def attend(query_seq, key_seq, value_seq, starts_seq):
    positions = jnp.arange(LEN, dtype=jnp.int32)
    scale_factor = 1.0 / math.sqrt(HEAD)

    def one_block(block_args):
        query_block, query_pos, query_start = block_args
        scores = jnp.einsum('qhd,khd->hqk', query_block, key_seq, precision=lax.Precision.HIGHEST) * scale_factor
        scores = low_back(scores)
        allowed = (positions[None, :] <= query_pos[:, None]) & (positions[None, :] >= query_start[:, None])
        scores = jnp.where(allowed[None], scores, -jnp.inf)
        weights = low(jax.nn.softmax(scores, axis=-1))
        return jnp.einsum('hqk,khd->qhd', weights, value_seq, precision=lax.Precision.HIGHEST)
    blocks = (query_seq.reshape(N_CTX, SEQ_DEV, HEADS, HEAD), positions.reshape(N_CTX, SEQ_DEV), starts_seq.reshape(N_CTX, SEQ_DEV))
    return lax.map(jax.checkpoint(one_block), blocks).reshape(LEN, HEADS, HEAD)

def forward(params, x_all, y_all, starts_all):
    w_query, b_query, w_key, w_value, b_value, w_output, b_output, gain_one, shift_one, w_hidden, b_hidden, w_reduce, b_reduce, gain_two, shift_two = params
    x_rows = x_all.reshape(-1, D)
    y_rows = y_all.reshape(-1, D)
    x_low = low(x_rows)
    query = low(low_back(highest(x_low, w_query) + b_query))
    keys = low(low_back(highest(x_low, w_key)))
    values = low(low_back(highest(x_low, w_value) + b_value))
    seq_count = STREAMS * MB

    def one_seq(seq_args):
        return attend(seq_args[0], seq_args[1], seq_args[2], seq_args[3])
    mixed_all = lax.map(one_seq, (query.reshape(seq_count, LEN, HEADS, HEAD), keys.reshape(seq_count, LEN, HEADS, HEAD), values.reshape(seq_count, LEN, HEADS, HEAD), starts_all.reshape(seq_count, LEN)))
    attended_low = low(low_back(mixed_all.reshape(-1, D)))
    branch = low_back(highest(attended_low, w_output) + b_output)
    x_first = layer_norm(x_rows + branch, gain_one, shift_one)
    y_first = y_rows + branch
    hidden_pre = low_back(highest(low(x_first), w_hidden) + b_hidden)
    hidden_low = low(gelu_exact(hidden_pre))
    second = low_back(highest(hidden_low, w_reduce) + b_reduce)
    x_next = layer_norm(x_first + second, gain_two, shift_two)
    y_next = y_first + second
    return (x_next.reshape(x_all.shape), y_next.reshape(y_all.shape))

def reference(x_stream, y_stream, grad_x, grad_y, doc_start, query_weight, query_bias, key_weight, value_weight, value_bias, output_weight, output_bias, first_gain, first_shift, hidden_weight, hidden_bias, reduce_weight, reduce_bias, second_gain, second_shift):
    raw_params = (query_weight, query_bias, key_weight, value_weight, value_bias, output_weight, output_bias, first_gain, first_shift, hidden_weight, hidden_bias, reduce_weight, reduce_bias, second_gain, second_shift)
    params = tuple((member.astype(jnp.float32) for member in raw_params))

    def run_layer(params_in, x_in):
        return forward(params_in, x_in, y_stream, doc_start)
    outputs, pullback = jax.vjp(run_layer, params, x_stream)
    param_grads, x_grad = pullback((grad_x, grad_y))
    return (outputs[0], outputs[1], x_grad, param_grads[0], param_grads[1], param_grads[2], param_grads[3], param_grads[4], param_grads[5], param_grads[6], param_grads[7], param_grads[8], param_grads[9], param_grads[10], param_grads[11], param_grads[12], param_grads[13], param_grads[14])
```

```python
import math
import jax
import jax.numpy as jnp
from jax import lax
from jax.experimental import pallas as pl
from jax.experimental.pallas import tpu as pltpu
from jax.sharding import PartitionSpec as P

HEADS = 8
NEG = -1e30
bf16 = jnp.bfloat16
f32 = jnp.float32
MESH = pl.DeviceIdType.MESH
VMEM_LIMIT = 60 << 20


def dots(left, right, left_dim, right_dim):
    return lax.dot_general(
        left, right, (((left_dim,), (right_dim,)), ((), ())), preferred_element_type=f32
    )


def turned(block):
    return jnp.transpose(block.astype(f32)).astype(bf16)


class Place:
    def __init__(self):
        self.c = lax.axis_index("ctx")
        self.z = lax.axis_index("fsdp")
        self.core = lax.rem(self.c, 2)
        self.x = lax.rem(lax.div(self.c, 2), 2)
        self.y = lax.div(self.c, 4)
        self.sibling = self.c + 1 - 2 * self.core
        self.x_next = self.c + 2 - 4 * self.x
        self.y_next = self.c + 4 - 8 * self.y

    def ring(self, k):
        return lax.rem(self.c + k, 8)

    def source(self, k):
        return lax.rem(self.c + 8 - k, 8)

    def up(self, d):
        return lax.rem(self.z + d, 4)

    def down(self, d):
        return lax.rem(self.z + 4 - d, 4)


def enter(place):
    barrier = pltpu.get_barrier_semaphore()
    for k in range(1, 8):
        pl.semaphore_signal(barrier, inc=1, device_id=(place.ring(k), place.z), device_id_type=MESH)
    for d in range(1, 4):
        pl.semaphore_signal(barrier, inc=1, device_id=(place.c, place.up(d)), device_id_type=MESH)
    pl.semaphore_wait(barrier, 10)


def remote(src, dst, send_sem, recv_sem, device):
    return pltpu.make_async_remote_copy(
        src_ref=src, dst_ref=dst, send_sem=send_sem, recv_sem=recv_sem,
        device_id=device, device_id_type=MESH,
    )


def aligned(start, size, unit):
    return pl.ds(pl.multiple_of(start, unit), size)


class Gather:
    def __init__(self, place, shard, full, axis, sems):
        self.place, self.shard, self.full, self.axis = place, shard, full, axis
        self.rows = shard.shape[0]
        self.side = place.x if axis == "x" else place.y
        self.pair = place.x_next if axis == "x" else place.y_next
        self.piece = self.rows // (4 if axis else 2)
        self.zs, self.zr, self.ps, self.pr, self.ss, self.sr, self.ts, self.tr, self.own = sems

    def at(self, z, half, core):
        start = z * self.rows + core * self.piece
        if self.axis:
            start = start + half * (2 * self.piece)
        return self.full.at[aligned(start, self.piece, 16)]

    def start(self):
        p = self.place
        begin = p.core * self.piece
        if self.axis:
            begin = begin + self.side * (2 * self.piece)
        mine = self.shard.at[aligned(begin, self.piece, 16)]
        self.out = []
        for d in (1, 3, 2):
            copy = remote(mine, self.at(p.z, self.side, p.core), self.zs.at[d - 1], self.zr.at[d - 1], (p.c, p.up(d)))
            copy.start()
            self.out.append(copy)
        self.local = pltpu.make_async_copy(
            self.shard, self.full.at[aligned(p.z * self.rows, self.rows, 16)], self.own
        )
        self.local.start()
        self.moved = []

    def spread(self):
        p = self.place
        for d in (1, 3, 2):
            block = self.at(p.down(d), self.side, p.core)
            remote(block, block, self.zs.at[d - 1], self.zr.at[d - 1], (p.c, p.up(d))).wait_recv()
            if self.axis:
                copy = remote(block, block, self.ps.at[d - 1], self.pr.at[d - 1], (self.pair, p.z))
                copy.start()
                self.moved.append(copy)
            copy = remote(block, block, self.ss.at[d - 1], self.sr.at[d - 1], (p.sibling, p.z))
            copy.start()
            self.moved.append(copy)

    def relay(self):
        p = self.place
        for d in (1, 3, 2):
            block = self.at(p.down(d), 1 - self.side, p.core)
            remote(block, block, self.ps.at[d - 1], self.pr.at[d - 1], (self.pair, p.z)).wait_recv()
            copy = remote(block, block, self.ts.at[d - 1], self.tr.at[d - 1], (p.sibling, p.z))
            copy.start()
            self.moved.append(copy)

    def finish(self):
        p = self.place
        for d in (1, 3, 2):
            block = self.at(p.down(d), self.side, 1 - p.core)
            remote(block, block, self.ss.at[d - 1], self.sr.at[d - 1], (p.sibling, p.z)).wait_recv()
            if self.axis:
                block = self.at(p.down(d), 1 - self.side, 1 - p.core)
                remote(block, block, self.ts.at[d - 1], self.tr.at[d - 1], (p.sibling, p.z)).wait_recv()
        for copy in self.out + self.moved:
            copy.wait_send()
        self.local.wait()


def attend_kernel(
    x_ref, starts_ref, wq_ref, wk_ref, wv_ref, vec_ref, wo_ref, wh_ref, wr_ref,
    qkv_ref, head_ref, log_ref, mixed_ref, wt_ref, vecs_ref, wo_full, wh_full, wr_full,
    x_turned, stage, q_rows, v_rows, start_cols,
    wz_s, wz_r, wc_s, wc_r, vz_s, vz_r, a_s, a_r, o_s, o_r, g_sems, own_sems,
):
    place = Place()
    c, z, core = place.c, place.z, place.core
    mbs, seq = x_ref.shape[0], x_ref.shape[1]
    width = x_ref.shape[2]
    column = aligned(z * 128, 128, 128)
    for m, w_ref in enumerate((wq_ref, wk_ref, wv_ref)):
        wt_ref[m * width:(m + 1) * width, column] = turned(w_ref[...])
    vecs_ref[z] = vec_ref[...]
    enter(place)

    def weight_part(m, zz, half):
        rows = aligned(m * width + half * (width // 2), width // 2, 16)
        return wt_ref.at[rows, aligned(zz * 128, 128, 128)]

    sends = []
    for d in (1, 3, 2):
        copy = remote(vecs_ref.at[z], vecs_ref.at[z], vz_s.at[d - 1], vz_r.at[d - 1], (c, place.up(d)))
        copy.start()
        sends.append(copy)
    for m in range(3):
        for d in (1, 3, 2):
            part = weight_part(m, z, core)
            copy = remote(part, part, wz_s.at[m, d - 1], wz_r.at[m, d - 1], (c, place.up(d)))
            copy.start()
            sends.append(copy)
    for mb in range(mbs):
        x_turned[:, mb * seq:(mb + 1) * seq] = jnp.transpose(x_ref[mb]).astype(bf16)
        for i in range(8):
            start_cols[mb, i * seq:(i + 1) * seq, :] = jnp.transpose(starts_ref[mb, :, i * seq:(i + 1) * seq])
    for d in (1, 3, 2):
        slot = vecs_ref.at[place.down(d)]
        remote(slot, slot, vz_s.at[d - 1], vz_r.at[d - 1], (c, place.up(d))).wait_recv()
    q_bias = jnp.transpose(jnp.concatenate([vecs_ref[zz, 0:1, :] for zz in range(4)], axis=1).astype(f32))
    v_bias = jnp.transpose(jnp.concatenate([vecs_ref[zz, 1:2, :] for zz in range(4)], axis=1).astype(f32))

    gathers = [
        Gather(place, wo_ref, wo_full, None, [g_sems.at[0, i] for i in range(8)] + [own_sems.at[0]]),
        Gather(place, wh_ref, wh_full, "y", [g_sems.at[1, i] for i in range(8)] + [own_sems.at[1]]),
        Gather(place, wr_ref, wr_full, "x", [g_sems.at[2, i] for i in range(8)] + [own_sems.at[2]]),
    ]

    def weights_ready(m):
        for d in (1, 3, 2):
            part = weight_part(m, place.down(d), core)
            remote(part, part, wz_s.at[m, d - 1], wz_r.at[m, d - 1], (c, place.up(d))).wait_recv()
            copy = remote(part, part, wc_s.at[m, d - 1], wc_r.at[m, d - 1], (place.sibling, z))
            copy.start()
            sends.append(copy)
        for d in (1, 3, 2):
            part = weight_part(m, place.down(d), 1 - core)
            remote(part, part, wc_s.at[m, d - 1], wc_r.at[m, d - 1], (place.sibling, z)).wait_recv()

    def project(m, mb):
        made = jnp.dot(
            wt_ref[m * width:(m + 1) * width, :], x_turned[:, mb * seq:(mb + 1) * seq],
            preferred_element_type=f32,
        )
        if m == 0:
            made = (made + q_bias).astype(bf16).astype(f32) * 0.125
        if m == 2:
            made = made + v_bias
        stage[m, mb] = made.astype(bf16).reshape(8, width // 8, seq)
        qkv_ref[m, mb, c] = stage[m, mb, c]
        for k in range(1, 8):
            copy = remote(
                stage.at[m, mb, place.ring(k)], qkv_ref.at[m, mb, c],
                a_s.at[m, mb, k - 1], a_r.at[m, mb, k - 1], (place.ring(k), z),
            )
            copy.start()
            sends.append(copy)

    weights_ready(0)
    for mb in range(mbs):
        project(0, mb)
    weights_ready(1)
    weights_ready(2)
    for gather in gathers:
        gather.start()
    for mb in range(mbs):
        project(1, mb)
        project(2, mb)

    for mb in range(mbs):
        for k in range(1, 8):
            for m in range(3):
                slot = qkv_ref.at[m, mb, place.source(k)]
                remote(slot, slot, a_s.at[m, mb, k - 1], a_r.at[m, mb, k - 1], (place.ring(k), z)).wait_recv()
        for j in range(8):
            q_rows[j * seq:(j + 1) * seq, :] = turned(qkv_ref[0, mb, j])
            v_rows[j * seq:(j + 1) * seq, :] = turned(qkv_ref[2, mb, j])
        for i in range(8):
            span = (i + 1) * seq
            keys = jnp.concatenate([qkv_ref[1, mb, j] for j in range(i + 1)], axis=1)
            scores = jnp.dot(q_rows[i * seq:(i + 1) * seq, :], keys, preferred_element_type=f32)
            key_pos = lax.broadcasted_iota(jnp.int32, (1, span), 1)
            query_pos = lax.broadcasted_iota(jnp.int32, (seq, 1), 0) + i * seq
            allowed = (key_pos >= start_cols[mb, i * seq:(i + 1) * seq, :]) & (key_pos <= query_pos)
            scores = jnp.where(allowed, scores, NEG)
            top = jnp.max(scores, axis=1, keepdims=True)
            weights = jnp.exp(scores - top)
            total = jnp.sum(weights, axis=1, keepdims=True)
            mixed = jnp.dot(weights.astype(bf16), v_rows[0:span, :], preferred_element_type=f32)
            head_ref[mb, i] = jnp.transpose(mixed / total).astype(bf16)
            log_ref[mb, :, i * seq:(i + 1) * seq] = jnp.transpose(top + jnp.log(total))
        mixed_ref[mb, c] = head_ref[mb, c]
        for k in range(1, 8):
            copy = remote(
                head_ref.at[mb, place.ring(k)], mixed_ref.at[mb, c],
                o_s.at[mb, k - 1], o_r.at[mb, k - 1], (place.ring(k), z),
            )
            copy.start()
            sends.append(copy)
        if mb == 0:
            gathers[0].spread()
        if mb == 1:
            gathers[1].spread()
        if mb == 2:
            gathers[1].relay()
            gathers[2].spread()
            gathers[2].relay()
    for mb in range(mbs):
        for k in range(1, 8):
            slot = mixed_ref.at[mb, place.source(k)]
            remote(slot, slot, o_s.at[mb, k - 1], o_r.at[mb, k - 1], (place.ring(k), z)).wait_recv()
    for gather in gathers:
        gather.finish()
    for copy in sends:
        copy.wait_send()


def attend_call(x, starts, wq, wk, wv, vec, wo, wh, wr):
    mbs, seq, width = x.shape
    hidden = wh.shape[1]
    feat = width // HEADS
    count = HEADS * seq
    vm = pl.BlockSpec(memory_space=pltpu.VMEM)
    anym = pl.BlockSpec(memory_space=pl.ANY)
    dma = pltpu.SemaphoreType.DMA
    sds = jax.ShapeDtypeStruct
    return pl.pallas_call(
        attend_kernel,
        out_shape=(
            sds((3, mbs, 8, feat, seq), bf16), sds((mbs, 8, feat, seq), bf16), sds((mbs, 1, count), f32),
            sds((mbs, 8, feat, seq), bf16), sds((3 * width, width), bf16), sds((4, 16, 128), bf16),
            sds((width, width), bf16), sds((width, hidden), bf16), sds((hidden, width), bf16),
        ),
        in_specs=[vm] * 6 + [anym] * 3,
        out_specs=[vm] * 6 + [anym] * 3,
        scratch_shapes=[
            pltpu.VMEM((width, mbs * seq), bf16), pltpu.VMEM((3, mbs, 8, feat, seq), bf16),
            pltpu.VMEM((count, feat), bf16), pltpu.VMEM((count, feat), bf16), pltpu.VMEM((mbs, count, 1), jnp.int32),
            dma((3, 3)), dma((3, 3)), dma((3, 3)), dma((3, 3)), dma((3,)), dma((3,)),
            dma((3, mbs, 7)), dma((3, mbs, 7)), dma((mbs, 7)), dma((mbs, 7)), dma((3, 8, 3)), dma((3,)),
        ],
        compiler_params=pltpu.CompilerParams(collective_id=1, has_side_effects=True, vmem_limit_bytes=VMEM_LIMIT),
        name="attend",
    )(x, starts, wq, wk, wv, vec, wo, wh, wr)


def pack_vec(qb, vb, ob, fg, fs, rb, sg, ss, hb):
    rows = [v.reshape(-1, 128) for v in (qb, vb, ob, fg, fs, rb, sg, ss, hb)]
    return jnp.concatenate(rows + [jnp.zeros((4, 128), bf16)], axis=0)


neg_big = -1e30
norm_eps = 1e-05
root_half = 0.7071067811865476
inv_root_tau = 0.3989422804014327


def swapped(block, axis, stride):
    count = lax.axis_size(axis)
    route = []
    for low in range(count):
        high = low | 1 << stride
        if high != low and high < count:
            route += [(low, high), (high, low)]
    return lax.ppermute(block, axis, route)


def matmul(left, right):
    return jnp.dot(left, right, preferred_element_type=jnp.float32)


def matmul_left_t(left, right):
    return lax.dot_general(
        left, right, (((0,), (0,)), ((), ())), preferred_element_type=jnp.float32
    )


def matmul_right_t(left, right):
    return lax.dot_general(
        left, right, (((1,), (1,)), ((), ())), preferred_element_type=jnp.float32
    )


def gelu_value(hidden):
    return hidden * 0.5 * (1.0 + jax.scipy.special.erf(hidden * root_half))


def gelu_slope(hidden):
    return 0.5 * (
        1.0 + jax.scipy.special.erf(hidden * root_half)
    ) + hidden * inv_root_tau * jnp.exp(-0.5 * hidden * hidden)


def norm_forward(total, gain, shift):
    mean_val = jnp.mean(total, axis=-1, keepdims=True)
    centered = total - mean_val
    inv_std = lax.rsqrt(jnp.mean(centered * centered, axis=-1, keepdims=True) + norm_eps)
    normed = centered * inv_std
    return (normed * gain + shift, normed, inv_std)


def norm_backward(upstream, normed, inv_std, gain):
    scaled = upstream * gain
    first_mean = jnp.mean(scaled, axis=-1, keepdims=True)
    second_mean = jnp.mean(scaled * normed, axis=-1, keepdims=True)
    return inv_std * (scaled - first_mean - normed * second_mean)


def allowed_pairs(query_pos, query_start, key_pos):
    return (key_pos[None, :] <= query_pos[:, None]) & (key_pos[None, :] >= query_start[:, None])


def pair_needed(key_lo, query_lo, span):
    needed = key_lo <= query_lo + span - 1
    return needed


def half_firsts(device, seq_dev, cycle_size):
    half = seq_dev // 2
    first = device * seq_dev
    second = (cycle_size - 1 - device) * seq_dev + half
    return (first, second)


def mirror_inputs(members, cycle_size):
    moved = members
    for bit in range(cycle_size.bit_length() - 1):
        moved = swapped((moved[0], moved[1], moved[2], moved[3]), "ctx", bit)
    return moved


def mirror_outputs(members, cycle_size):
    moved = members
    for bit in range(cycle_size.bit_length() - 1):
        moved = swapped((moved[0], moved[1], moved[2]), "ctx", bit)
    return moved


def block_scores(query_three, key_three, allowed, scale_factor):
    scores = (
        jnp.einsum("qhd,khd->hqk", query_three, key_three, preferred_element_type=jnp.float32)
        * scale_factor
    )
    return jnp.where(allowed[None], scores, neg_big)


def forward_update(state_mb, query_three, key_three, value_three, allowed, scale_factor):
    run_max, run_sum, run_acc = state_mb
    scores = block_scores(query_three, key_three, allowed, scale_factor)
    new_max = jnp.maximum(run_max, jnp.max(scores, axis=-1))
    rescale = jnp.exp(run_max - new_max)
    weights = jnp.where(allowed[None], jnp.exp(scores - new_max[:, :, None]), 0.0)
    new_sum = run_sum * rescale + jnp.sum(weights, axis=-1)
    mixed_sum = jnp.einsum(
        "hqk,khd->qhd",
        weights.astype(jnp.bfloat16),
        value_three,
        preferred_element_type=jnp.float32,
    )
    new_acc = run_acc * jnp.transpose(rescale)[:, :, None] + mixed_sum
    return (new_max, new_sum, new_acc)


def pair_grads(
    query_three, dout_three, key_three, value_three, allowed, log_total, row_delta, scale_factor
):
    scores = block_scores(query_three, key_three, allowed, scale_factor)
    prob_table = jnp.where(allowed[None], jnp.exp(scores - log_total[:, :, None]), 0.0)
    dprobs = jnp.einsum("qhd,khd->hqk", dout_three, value_three, preferred_element_type=jnp.float32)
    score_grad = (prob_table * (dprobs - row_delta[:, :, None])).astype(jnp.bfloat16)
    return (prob_table, score_grad)


def fold_blocks(pieces, state_all, update, base_rows):
    rows_in = pieces[0].shape[1]
    step_rows = min(rows_in, base_rows)

    def one_step(block_index, state_inner):
        offset = block_index * step_rows
        sliced = tuple(
            (lax.dynamic_slice_in_dim(member, offset, step_rows, 1) for member in pieces)
        )
        return update(state_inner, sliced, offset)

    return lax.fori_loop(0, rows_in // step_rows, one_step, state_all)


def shards(
    x_stream,
    y_stream,
    grad_x,
    grad_y,
    doc_start,
    query_weight,
    query_bias,
    key_weight,
    value_weight,
    value_bias,
    output_weight,
    output_bias,
    first_gain,
    first_shift,
    hidden_weight,
    hidden_bias,
    reduce_weight,
    reduce_bias,
    second_gain,
    second_shift,
):
    gathered = (
        lax.all_gather(query_weight, "fsdp", axis=0, tiled=True),
        lax.all_gather(query_bias, "fsdp", axis=0, tiled=True),
        lax.all_gather(key_weight, "fsdp", axis=0, tiled=True),
        lax.all_gather(value_weight, "fsdp", axis=0, tiled=True),
        lax.all_gather(value_bias, "fsdp", axis=0, tiled=True),
        lax.all_gather(output_weight, "fsdp", axis=0, tiled=True),
        lax.all_gather(output_bias, "fsdp", axis=0, tiled=True),
        lax.all_gather(first_gain, "fsdp", axis=0, tiled=True),
        lax.all_gather(first_shift, "fsdp", axis=0, tiled=True),
        lax.all_gather(hidden_weight, "fsdp", axis=0, tiled=True),
        lax.all_gather(hidden_bias, "fsdp", axis=0, tiled=True),
        lax.all_gather(reduce_weight, "fsdp", axis=0, tiled=True),
        lax.all_gather(reduce_bias, "fsdp", axis=0, tiled=True),
        lax.all_gather(second_gain, "fsdp", axis=0, tiled=True),
        lax.all_gather(second_shift, "fsdp", axis=0, tiled=True),
    )
    (
        w_query,
        b_query,
        w_key,
        w_value,
        b_value,
        w_output,
        b_output,
        gain_one,
        shift_one,
        w_hidden,
        b_hidden,
        w_reduce,
        b_reduce,
        gain_two,
        shift_two,
    ) = gathered
    b_query = b_query.astype(jnp.float32)
    b_value = b_value.astype(jnp.float32)
    b_output = b_output.astype(jnp.float32)
    gain_one = gain_one.astype(jnp.float32)
    shift_one = shift_one.astype(jnp.float32)
    b_hidden = b_hidden.astype(jnp.float32)
    b_reduce = b_reduce.astype(jnp.float32)
    gain_two = gain_two.astype(jnp.float32)
    shift_two = shift_two.astype(jnp.float32)
    micro_count, seq_dev, model_width = (x_stream.shape[1], x_stream.shape[2], x_stream.shape[3])
    half = seq_dev // 2
    head_count = HEADS
    head_dim = model_width // head_count
    scale_factor = 1.0 / math.sqrt(head_dim)
    token_rows = micro_count * seq_dev
    cycle_size = lax.axis_size("ctx")
    my_index = lax.axis_index("ctx")
    half_range = jnp.arange(half, dtype=jnp.int32)
    own_firsts = half_firsts(my_index, seq_dev, cycle_size)
    own_pos = [own_firsts[0] + half_range, own_firsts[1] + half_range]
    positions_own = jnp.concatenate(own_pos)
    doc_all = doc_start[0]
    starts_own = jnp.take(doc_all, positions_own, axis=1)
    own_starts = [
        [starts_own[micro_index, part * half : (part + 1) * half] for part in range(2)]
        for micro_index in range(micro_count)
    ]
    x_mb, y_mb, gx_mb, gy_mb = (x_stream[0], y_stream[0], grad_x[0], grad_y[0])
    moved = mirror_inputs(
        (x_mb[:, half:], y_mb[:, half:], gx_mb[:, half:], gy_mb[:, half:]), cycle_size
    )
    x_mb = jnp.concatenate([x_mb[:, :half], moved[0]], axis=1)
    y_mb = jnp.concatenate([y_mb[:, :half], moved[1]], axis=1)
    gx_mb = jnp.concatenate([gx_mb[:, :half], moved[2]], axis=1)
    gy_mb = jnp.concatenate([gy_mb[:, :half], moved[3]], axis=1)
    x_rows = x_mb.reshape(token_rows, model_width)
    y_rows = y_mb.reshape(token_rows, model_width)
    gx_rows = gx_mb.reshape(token_rows, model_width)
    gy_rows = gy_mb.reshape(token_rows, model_width)
    x_low = x_rows.astype(jnp.bfloat16)
    query_low = (matmul(x_low, w_query) + b_query).astype(jnp.bfloat16)
    key_low = matmul(x_low, w_key).astype(jnp.bfloat16)
    value_low = (matmul(x_low, w_value) + b_value).astype(jnp.bfloat16)
    query_mb = query_low.reshape(micro_count, seq_dev, model_width)
    key_mb = key_low.reshape(micro_count, seq_dev, model_width)
    value_mb = value_low.reshape(micro_count, seq_dev, model_width)
    query_three = [
        query_mb[micro_index].reshape(seq_dev, head_count, head_dim)
        for micro_index in range(micro_count)
    ]
    key_own = [
        key_mb[micro_index].reshape(seq_dev, head_count, head_dim)
        for micro_index in range(micro_count)
    ]
    value_own = [
        value_mb[micro_index].reshape(seq_dev, head_count, head_dim)
        for micro_index in range(micro_count)
    ]

    def forward_step(state_inner, sliced, key_first):
        key_block, value_block = sliced
        source = key_first // seq_dev
        key_firsts = half_firsts(source, seq_dev, cycle_size)
        updated = []
        for micro_index in range(micro_count):
            key_three = key_block[micro_index].reshape(seq_dev, head_count, head_dim)
            value_three = value_block[micro_index].reshape(seq_dev, head_count, head_dim)
            states = list(state_inner[micro_index])
            for query_part in range(2):
                query_piece = query_three[micro_index][query_part * half : (query_part + 1) * half]
                for key_part in range(2):
                    key_piece = key_three[key_part * half : (key_part + 1) * half]
                    value_piece = value_three[key_part * half : (key_part + 1) * half]
                    allowed = allowed_pairs(
                        own_pos[query_part],
                        own_starts[micro_index][query_part],
                        key_firsts[key_part] + half_range,
                    )
                    needed = pair_needed(key_firsts[key_part], own_firsts[query_part], half)

                    def forward_compute(state_mb):
                        return forward_update(
                            state_mb, query_piece, key_piece, value_piece, allowed, scale_factor
                        )

                    def forward_unchanged(state_mb):
                        return state_mb

                    states[query_part] = lax.cond(
                        needed, forward_compute, forward_unchanged, states[query_part]
                    )
            updated.append(tuple(states))
        return tuple(updated)

    def empty_state():
        return (
            jnp.full((head_count, half), neg_big, jnp.float32),
            jnp.zeros((head_count, half), jnp.float32),
            jnp.zeros((half, head_count, head_dim), jnp.float32),
        )

    forward_init = tuple(((empty_state(), empty_state()) for micro_index in range(micro_count)))
    attend_state = fold_blocks(
        (
            lax.all_gather(key_mb, "ctx", axis=1, tiled=True),
            lax.all_gather(value_mb, "ctx", axis=1, tiled=True),
        ),
        forward_init,
        forward_step,
        seq_dev,
    )
    out_parts = []
    log_parts = []
    for micro_index in range(micro_count):
        out_halves = []
        log_halves = []
        for query_part in range(2):
            run_max, run_sum, run_acc = attend_state[micro_index][query_part]
            out_halves.append(run_acc / jnp.transpose(run_sum)[:, :, None])
            log_halves.append(run_max + jnp.log(run_sum))
        out_parts.append(jnp.concatenate(out_halves, axis=0))
        log_parts.append(jnp.concatenate(log_halves, axis=1))
    out_raw = jnp.stack(out_parts)
    log_total_all = jnp.stack(log_parts)
    out_low = out_raw.reshape(token_rows, model_width).astype(jnp.bfloat16)
    branch = matmul(out_low, w_output) + b_output
    x_first, normed_one, inv_one = norm_forward(x_rows + branch, gain_one, shift_one)
    y_first = y_rows + branch
    x_first_low = x_first.astype(jnp.bfloat16)
    hidden_pre = matmul(x_first_low, w_hidden) + b_hidden
    hidden_low = gelu_value(hidden_pre).astype(jnp.bfloat16)
    second = matmul(hidden_low, w_reduce) + b_reduce
    x_next, normed_two, inv_two = norm_forward(x_first + second, gain_two, shift_two)
    y_next = y_first + second
    total_two_grad = norm_backward(gx_rows, normed_two, inv_two, gain_two)
    second_gain_grad = jnp.sum(gx_rows * normed_two, axis=0)
    second_shift_grad = jnp.sum(gx_rows, axis=0)
    second_grad = (total_two_grad + gy_rows).astype(jnp.bfloat16)
    reduce_weight_grad = matmul_left_t(hidden_low, second_grad)
    reduce_bias_grad = jnp.sum(second_grad.astype(jnp.float32), axis=0)
    hidden_grad = (matmul_right_t(second_grad, w_reduce) * gelu_slope(hidden_pre)).astype(
        jnp.bfloat16
    )
    hidden_weight_grad = matmul_left_t(x_first_low, hidden_grad)
    hidden_bias_grad = jnp.sum(hidden_grad.astype(jnp.float32), axis=0)
    first_up = total_two_grad + matmul_right_t(hidden_grad, w_hidden)
    total_one_grad = norm_backward(first_up, normed_one, inv_one, gain_one)
    first_gain_grad = jnp.sum(first_up * normed_one, axis=0)
    first_shift_grad = jnp.sum(first_up, axis=0)
    branch_grad = (total_one_grad + gy_rows).astype(jnp.bfloat16)
    output_weight_grad = matmul_left_t(out_low, branch_grad)
    output_bias_grad = jnp.sum(branch_grad.astype(jnp.float32), axis=0)
    dout_low = matmul_right_t(branch_grad, w_output).astype(jnp.bfloat16)
    dout_mb = dout_low.reshape(micro_count, seq_dev, head_count, head_dim)
    delta_all = jnp.einsum("bqhd,bqhd->bhq", dout_mb.astype(jnp.float32), out_raw)
    dout_three = [dout_mb[micro_index] for micro_index in range(micro_count)]
    dout_rows = dout_low.reshape(micro_count, seq_dev, model_width)

    def zero_query():
        return jnp.zeros((half, head_count, head_dim), jnp.float32)

    query_init = tuple(((zero_query(), zero_query()) for micro_index in range(micro_count)))

    def query_step(state_inner, sliced, key_first):
        key_block, value_block = sliced
        source = key_first // seq_dev
        key_firsts = half_firsts(source, seq_dev, cycle_size)
        updated = []
        for micro_index in range(micro_count):
            key_three = key_block[micro_index].reshape(seq_dev, head_count, head_dim)
            value_three = value_block[micro_index].reshape(seq_dev, head_count, head_dim)
            query_accs = list(state_inner[micro_index])
            for query_part in range(2):
                rows = slice(query_part * half, (query_part + 1) * half)
                query_piece = query_three[micro_index][rows]
                dout_piece = dout_three[micro_index][rows]
                log_piece = log_total_all[micro_index][:, rows]
                delta_piece = delta_all[micro_index][:, rows]
                for key_part in range(2):
                    key_piece = key_three[key_part * half : (key_part + 1) * half]
                    value_piece = value_three[key_part * half : (key_part + 1) * half]
                    allowed = allowed_pairs(
                        own_pos[query_part],
                        own_starts[micro_index][query_part],
                        key_firsts[key_part] + half_range,
                    )
                    needed = pair_needed(key_firsts[key_part], own_firsts[query_part], half)

                    def query_compute(query_acc):
                        prob_table, score_grad = pair_grads(
                            query_piece,
                            dout_piece,
                            key_piece,
                            value_piece,
                            allowed,
                            log_piece,
                            delta_piece,
                            scale_factor,
                        )
                        return (
                            query_acc
                            + jnp.einsum(
                                "hqk,khd->qhd",
                                score_grad,
                                key_piece,
                                preferred_element_type=jnp.float32,
                            )
                            * scale_factor
                        )

                    def query_unchanged(query_acc):
                        return query_acc

                    query_accs[query_part] = lax.cond(
                        needed, query_compute, query_unchanged, query_accs[query_part]
                    )
            updated.append(tuple(query_accs))
        return tuple(updated)

    query_parts = fold_blocks(
        (
            lax.all_gather(key_mb, "ctx", axis=1, tiled=True),
            lax.all_gather(value_mb, "ctx", axis=1, tiled=True),
        ),
        query_init,
        query_step,
        seq_dev,
    )
    stats_all = (
        lax.all_gather(log_total_all, "ctx", axis=2, tiled=True),
        lax.all_gather(delta_all, "ctx", axis=2, tiled=True),
    )

    def key_step(state_inner, sliced, query_begin):
        query_block, dout_block = sliced
        source = query_begin // seq_dev
        query_firsts = half_firsts(source, seq_dev, cycle_size)
        updated = []
        for micro_index in range(micro_count):
            log_block = lax.dynamic_slice_in_dim(stats_all[0][micro_index], query_begin, seq_dev, 1)
            delta_block = lax.dynamic_slice_in_dim(
                stats_all[1][micro_index], query_begin, seq_dev, 1
            )
            query_whole = query_block[micro_index].reshape(seq_dev, head_count, head_dim)
            dout_whole = dout_block[micro_index].reshape(seq_dev, head_count, head_dim)
            key_accs = [
                state_inner[micro_index][0][part * half : (part + 1) * half] for part in range(2)
            ]
            value_accs = [
                state_inner[micro_index][1][part * half : (part + 1) * half] for part in range(2)
            ]
            for query_part in range(2):
                rows = slice(query_part * half, (query_part + 1) * half)
                query_pos = query_firsts[query_part] + half_range
                starts_block = jnp.take(doc_all[micro_index], query_pos)
                query_piece = query_whole[rows]
                dout_piece = dout_whole[rows]
                log_piece = log_block[:, rows]
                delta_piece = delta_block[:, rows]
                for key_part in range(2):
                    key_piece = key_own[micro_index][key_part * half : (key_part + 1) * half]
                    value_piece = value_own[micro_index][key_part * half : (key_part + 1) * half]
                    allowed = allowed_pairs(query_pos, starts_block, own_pos[key_part])
                    needed = pair_needed(own_firsts[key_part], query_firsts[query_part], half)

                    def key_compute(operands):
                        key_acc, value_acc = operands
                        prob_table, score_grad = pair_grads(
                            query_piece,
                            dout_piece,
                            key_piece,
                            value_piece,
                            allowed,
                            log_piece,
                            delta_piece,
                            scale_factor,
                        )
                        key_add = (
                            jnp.einsum(
                                "hqk,qhd->khd",
                                score_grad,
                                query_piece,
                                preferred_element_type=jnp.float32,
                            )
                            * scale_factor
                        )
                        value_add = jnp.einsum(
                            "hqk,qhd->khd",
                            prob_table.astype(jnp.bfloat16),
                            dout_piece,
                            preferred_element_type=jnp.float32,
                        )
                        return (
                            key_acc + key_add.reshape(half, model_width),
                            value_acc + value_add.reshape(half, model_width),
                        )

                    def key_unchanged(operands):
                        return operands

                    result = lax.cond(
                        needed,
                        key_compute,
                        key_unchanged,
                        (key_accs[key_part], value_accs[key_part]),
                    )
                    key_accs[key_part] = result[0]
                    value_accs[key_part] = result[1]
            updated.append((jnp.concatenate(key_accs, axis=0), jnp.concatenate(value_accs, axis=0)))
        return tuple(updated)

    key_init = tuple(
        (
            (
                jnp.zeros((seq_dev, model_width), jnp.float32),
                jnp.zeros((seq_dev, model_width), jnp.float32),
            )
            for micro_index in range(micro_count)
        )
    )
    key_state = fold_blocks(
        (
            lax.all_gather(query_mb, "ctx", axis=1, tiled=True),
            lax.all_gather(dout_rows, "ctx", axis=1, tiled=True),
        ),
        key_init,
        key_step,
        seq_dev,
    )
    key_grad_sum = jnp.stack([key_state[micro_index][0] for micro_index in range(micro_count)])
    value_grad_sum = jnp.stack([key_state[micro_index][1] for micro_index in range(micro_count)])
    query_whole_parts = [
        jnp.concatenate([query_parts[micro_index][0], query_parts[micro_index][1]], axis=0)
        for micro_index in range(micro_count)
    ]
    query_grad_low = (
        jnp.stack(query_whole_parts).reshape(token_rows, model_width).astype(jnp.bfloat16)
    )
    key_grad_low = key_grad_sum.reshape(token_rows, model_width).astype(jnp.bfloat16)
    value_grad_low = value_grad_sum.reshape(token_rows, model_width).astype(jnp.bfloat16)
    query_weight_grad = matmul_left_t(x_low, query_grad_low)
    query_bias_grad = jnp.sum(query_grad_low.astype(jnp.float32), axis=0)
    key_weight_grad = matmul_left_t(x_low, key_grad_low)
    value_weight_grad = matmul_left_t(x_low, value_grad_low)
    value_bias_grad = jnp.sum(value_grad_low.astype(jnp.float32), axis=0)
    x_grad = (
        total_one_grad
        + matmul_right_t(query_grad_low, w_query)
        + matmul_right_t(key_grad_low, w_key)
        + matmul_right_t(value_grad_low, w_value)
    )
    shard_grads = (
        lax.psum_scatter(query_weight_grad, "fsdp", scatter_dimension=0, tiled=True),
        lax.psum_scatter(query_bias_grad, "fsdp", scatter_dimension=0, tiled=True),
        lax.psum_scatter(key_weight_grad, "fsdp", scatter_dimension=0, tiled=True),
        lax.psum_scatter(value_weight_grad, "fsdp", scatter_dimension=0, tiled=True),
        lax.psum_scatter(value_bias_grad, "fsdp", scatter_dimension=0, tiled=True),
        lax.psum_scatter(output_weight_grad, "fsdp", scatter_dimension=0, tiled=True),
        lax.psum_scatter(output_bias_grad, "fsdp", scatter_dimension=0, tiled=True),
        lax.psum_scatter(first_gain_grad, "fsdp", scatter_dimension=0, tiled=True),
        lax.psum_scatter(first_shift_grad, "fsdp", scatter_dimension=0, tiled=True),
        lax.psum_scatter(hidden_weight_grad, "fsdp", scatter_dimension=0, tiled=True),
        lax.psum_scatter(hidden_bias_grad, "fsdp", scatter_dimension=0, tiled=True),
        lax.psum_scatter(reduce_weight_grad, "fsdp", scatter_dimension=0, tiled=True),
        lax.psum_scatter(reduce_bias_grad, "fsdp", scatter_dimension=0, tiled=True),
        lax.psum_scatter(second_gain_grad, "fsdp", scatter_dimension=0, tiled=True),
        lax.psum_scatter(second_shift_grad, "fsdp", scatter_dimension=0, tiled=True),
    )
    summed = lax.psum(
        (
            shard_grads[0],
            shard_grads[1],
            shard_grads[2],
            shard_grads[3],
            shard_grads[4],
            shard_grads[5],
            shard_grads[6],
            shard_grads[7],
            shard_grads[8],
            shard_grads[9],
            shard_grads[10],
            shard_grads[11],
            shard_grads[12],
            shard_grads[13],
            shard_grads[14],
        ),
        "ctx",
    )
    mb_shape = (micro_count, seq_dev, model_width)
    x_next_mb = x_next.reshape(mb_shape)
    y_next_mb = y_next.reshape(mb_shape)
    x_grad_mb = x_grad.reshape(mb_shape)
    back = mirror_outputs(
        (x_next_mb[:, half:], y_next_mb[:, half:], x_grad_mb[:, half:]), cycle_size
    )
    x_next_mb = jnp.concatenate([x_next_mb[:, :half], back[0]], axis=1)
    y_next_mb = jnp.concatenate([y_next_mb[:, :half], back[1]], axis=1)
    x_grad_mb = jnp.concatenate([x_grad_mb[:, :half], back[2]], axis=1)
    out_shape = (1, micro_count, seq_dev, model_width)
    return (
        x_next_mb.reshape(out_shape),
        y_next_mb.reshape(out_shape),
        x_grad_mb.reshape(out_shape),
        summed[0],
        summed[1],
        summed[2],
        summed[3],
        summed[4],
        summed[5],
        summed[6],
        summed[7],
        summed[8],
        summed[9],
        summed[10],
        summed[11],
        summed[12],
        summed[13],
        summed[14],
    )


def dense_kernel(
    mixed_ref, x_ref, y_ref, gx_ref, gy_ref, wo_ref, wh_ref, wr_ref, vecs_ref,
    xn_ref, yn_ref, one_ref, dhead_ref, grad_ref, sums_ref,
    hid, hid_grad, first_low, second_grad, branch_grad, slope, stage,
    d_s, d_r,
):
    place = Place()
    c, z = place.c, place.z
    mbs, seq, width = x_ref.shape
    hidden = wh_ref.shape[1]
    enter(place)

    def vec(row):
        return jnp.concatenate([vecs_ref[zz, row:row + 1, :] for zz in range(4)], axis=1).astype(f32)

    b_output, gain_one, shift_one, b_reduce, gain_two, shift_two = [vec(row) for row in range(2, 8)]
    b_hidden = jnp.concatenate(
        [vecs_ref[zz, 8 + r:9 + r, :] for zz in range(4) for r in range(4)], axis=1
    ).astype(f32)
    sums_ref[...] = jnp.zeros_like(sums_ref)

    def add_row(row, block):
        sums_ref[row:row + 1, :] += jnp.sum(block, axis=0, keepdims=True)

    sends = []
    for mb in range(mbs):
        rows = slice(mb * seq, (mb + 1) * seq)
        branch = dots(mixed_ref[mb].reshape(width, seq), wo_ref[...], 0, 0) + b_output
        x_first, normed_one, inv_one = norm_forward(x_ref[mb] + branch, gain_one, shift_one)
        first_low[rows, :] = x_first.astype(bf16)
        for q in range(4):
            cols = slice(q * (hidden // 4), (q + 1) * (hidden // 4))
            pre = jnp.dot(first_low[rows, :], wh_ref[:, cols], preferred_element_type=f32) + b_hidden[:, cols]
            phi = 0.5 * (1.0 + lax.erf(pre * root_half))
            hid[rows, cols] = (pre * phi).astype(bf16)
            slope[:, cols] = phi + pre * inv_root_tau * jnp.exp(-0.5 * pre * pre)
        second = jnp.dot(hid[rows, :], wr_ref[...], preferred_element_type=f32) + b_reduce
        x_next, normed_two, inv_two = norm_forward(x_first + second, gain_two, shift_two)
        xn_ref[mb] = x_next
        yn_ref[mb] = y_ref[mb] + branch + second
        upstream = gx_ref[mb]
        two_grad = norm_backward(upstream, normed_two, inv_two, gain_two)
        add_row(4, upstream * normed_two)
        add_row(5, upstream)
        second_low = (two_grad + gy_ref[mb]).astype(bf16)
        second_grad[rows, :] = second_low
        add_row(3, second_low.astype(f32))
        first_up = two_grad
        for q in range(4):
            cols = slice(q * (hidden // 4), (q + 1) * (hidden // 4))
            made = dots(second_low, wr_ref[cols, :], 1, 1) * slope[:, cols]
            hid_grad[rows, cols] = made.astype(bf16)
            add_row(6 + q, hid_grad[rows, cols].astype(f32))
        first_up = first_up + dots(hid_grad[rows, :], wh_ref[...], 1, 1)
        one_grad = norm_backward(first_up, normed_one, inv_one, gain_one)
        one_ref[mb] = one_grad
        add_row(1, first_up * normed_one)
        add_row(2, first_up)
        branch_low = (one_grad + gy_ref[mb]).astype(bf16)
        branch_grad[rows, :] = branch_low
        add_row(0, branch_low.astype(f32))
        stage[mb] = dots(wo_ref[...], branch_low, 1, 1).astype(bf16).reshape(8, width // 8, seq)
        dhead_ref[mb, c] = stage[mb, c]
        for k in range(1, 8):
            copy = remote(
                stage.at[mb, place.ring(k)], dhead_ref.at[mb, c],
                d_s.at[mb, k - 1], d_r.at[mb, k - 1], (place.ring(k), z),
            )
            copy.start()
            sends.append(copy)

    first_all = turned(first_low[...])
    second_all = turned(second_grad[...])
    for q in range(4):
        cols = slice(q * (hidden // 4), (q + 1) * (hidden // 4))
        part = jnp.dot(second_all, hid[:, cols], preferred_element_type=f32).astype(bf16)
        for owner in range(8):
            grad_ref[owner % 2, owner // 2, q, 0:64, :] = part[owner * 64:(owner + 1) * 64, :]
        part = jnp.dot(first_all, hid_grad[:, cols], preferred_element_type=f32).astype(bf16)
        for zz in range(4):
            for owner in range(8):
                begin = zz * 128 + owner * 16
                grad_ref[owner % 2, owner // 2, zz, 64 + 16 * q:80 + 16 * q, :] = part[begin:begin + 16, :]
    mixed_all = jnp.concatenate([mixed_ref[mb].reshape(width, seq) for mb in range(mbs)], axis=1)
    part = jnp.dot(mixed_all, branch_grad[...], preferred_element_type=f32).astype(bf16)
    for zz in range(4):
        for owner in range(8):
            begin = zz * 128 + owner * 16
            grad_ref[owner % 2, owner // 2, zz, 128:144, :] = part[begin:begin + 16, :]

    for mb in range(mbs):
        for k in range(1, 8):
            slot = dhead_ref.at[mb, place.source(k)]
            remote(slot, slot, d_s.at[mb, k - 1], d_r.at[mb, k - 1], (place.ring(k), z)).wait_recv()
    for copy in sends:
        copy.wait_send()


def dense_call(mixed, x, y, gx, gy, wo, wh, wr, vecs):
    mbs, seq, width = x.shape
    hidden = wh.shape[1]
    feat = width // HEADS
    tokens = mbs * seq
    vm = pl.BlockSpec(memory_space=pltpu.VMEM)
    dma = pltpu.SemaphoreType.DMA
    sds = jax.ShapeDtypeStruct
    big = sds((mbs, seq, width), f32)
    return pl.pallas_call(
        dense_kernel,
        out_shape=(
            big, big, big, sds((mbs, 8, feat, seq), bf16), sds((2, 4, 4, 144, 512), bf16), sds((16, width), f32),
        ),
        in_specs=[vm] * 9,
        out_specs=[vm] * 6,
        scratch_shapes=[
            pltpu.VMEM((tokens, hidden), bf16), pltpu.VMEM((tokens, hidden), bf16), pltpu.VMEM((tokens, width), bf16),
            pltpu.VMEM((tokens, width), bf16), pltpu.VMEM((tokens, width), bf16), pltpu.VMEM((seq, hidden), f32),
            pltpu.VMEM((mbs, 8, feat, seq), bf16), dma((mbs, 7)), dma((mbs, 7)),
        ],
        compiler_params=pltpu.CompilerParams(collective_id=2, has_side_effects=True, vmem_limit_bytes=VMEM_LIMIT),
        name="dense",
    )(mixed, x, y, gx, gy, wo, wh, wr, vecs)


class Reduction:
    def __init__(self, place, part, pair, half, plane, quarter, column, out, sems):
        self.place = place
        self.part, self.pair, self.half, self.plane = part, pair, half, plane
        self.quarter, self.column, self.out = quarter, column, out
        self.s1, self.r1, self.s2, self.r2, self.s3, self.r3, self.s4, self.r4, self.s5, self.r5 = sems
        self.sent = []
        self.chip = lax.div(place.c, 2)

    def other(self, k):
        return lax.rem(self.chip + k, 4)

    def before(self, k):
        return lax.rem(self.chip + 4 - k, 4)

    def peer(self, k):
        return (2 * self.other(k) + self.place.core, self.place.z)

    def go(self, copy):
        copy.start()
        self.sent.append(copy)

    def pair_start(self):
        p = self.place
        self.go(remote(self.part.at[1 - p.core], self.pair, self.s1, self.r1, (p.sibling, p.z)))

    def plane_start(self):
        p = self.place
        remote(self.pair, self.pair, self.s1, self.r1, (p.sibling, p.z)).wait_recv()

        def add(chip, carry):
            for zz in range(4):
                self.half[chip, zz] = (self.part[p.core, chip, zz].astype(f32) + self.pair[chip, zz].astype(f32)).astype(bf16)
            return carry

        lax.fori_loop(0, 4, add, 0)
        for k in range(1, 4):
            self.go(remote(self.half.at[self.other(k)], self.plane.at[k - 1], self.s2.at[k - 1], self.r2.at[k - 1], self.peer(k)))

    def column_start(self):
        p = self.place
        for k in range(1, 4):
            remote(self.plane.at[k - 1], self.plane.at[k - 1], self.s2.at[k - 1], self.r2.at[k - 1], self.peer(k)).wait_recv()

        def add(zz, carry):
            total = self.half[self.chip, zz].astype(f32)
            for k in range(3):
                total = total + self.plane[k, zz].astype(f32)
            self.quarter[zz] = total.astype(bf16)
            return carry

        lax.fori_loop(0, 4, add, 0)
        for d in (1, 3, 2):
            self.go(remote(self.quarter.at[p.up(d)], self.column.at[d - 1], self.s3.at[d - 1], self.r3.at[d - 1], (p.c, p.up(d))))

    def back_start(self):
        p = self.place
        for d in (1, 3, 2):
            remote(self.column.at[d - 1], self.column.at[d - 1], self.s3.at[d - 1], self.r3.at[d - 1], (p.c, p.up(d))).wait_recv()
        total = self.quarter[p.z].astype(f32)
        for d in range(3):
            total = total + self.column[d].astype(f32)
        self.out[p.c] = total.astype(bf16)
        mine = self.out.at[p.c]
        for k in range(1, 4):
            self.go(remote(mine, mine, self.s4.at[k - 1], self.r4.at[k - 1], self.peer(k)))
        self.go(remote(mine, mine, self.s5.at[0], self.r5.at[0], (p.sibling, p.z)))

    def relay(self):
        p = self.place
        for k in range(1, 4):
            slot = self.out.at[2 * self.before(k) + p.core]
            remote(slot, slot, self.s4.at[k - 1], self.r4.at[k - 1], self.peer(k)).wait_recv()
            self.go(remote(slot, slot, self.s5.at[k], self.r5.at[k], (p.sibling, p.z)))

    def finish(self):
        p = self.place
        for k in range(4):
            slot = self.out.at[2 * self.before(k) + 1 - p.core]
            remote(slot, slot, self.s5.at[k], self.r5.at[k], (p.sibling, p.z)).wait_recv()
        for copy in self.sent:
            copy.wait_send()


def back_kernel(
    qkv_ref, head_ref, log_ref, dhead_ref, starts_ref, x_ref, one_ref, wt_ref, grad_ref, sums_ref,
    xg_ref, wide_ref, thin_ref, vec_ref,
    q_rows, g_rows, dq_turned, delta, made, got, x_low, total_thin,
    wide_pair, wide_half, wide_plane, wide_quarter, wide_column,
    thin_part, thin_pair, thin_half, thin_plane, thin_quarter, thin_column,
    vec_part, vec_column, vec_plane,
    kv_s, kv_r, q_s, q_r, *rest,
):
    wide_sems, thin_sems, (vc_s, vc_r, vp_s, vp_r) = rest[0:10], rest[10:20], rest[20:24]
    place = Place()
    c, z = place.c, place.z
    mbs, seq, width = x_ref.shape
    feat = width // HEADS
    enter(place)
    wide = Reduction(place, grad_ref, wide_pair, wide_half, wide_plane, wide_quarter, wide_column, wide_ref,
                     tuple(s if i > 1 else s.at[0] for i, s in enumerate(wide_sems)))
    thin = Reduction(place, thin_part, thin_pair, thin_half, thin_plane, thin_quarter, thin_column, thin_ref,
                     tuple(s if i > 1 else s.at[0] for i, s in enumerate(thin_sems)))
    wide.pair_start()
    sends = []

    for mb in range(mbs):
        for j in range(8):
            cols = slice(j * seq, (j + 1) * seq)
            q_rows[cols, :] = turned(qkv_ref[0, mb, j])
            g_rows[cols, :] = turned(dhead_ref[mb, j])
            delta[:, cols] = jnp.sum(
                dhead_ref[mb, j].astype(f32) * head_ref[mb, j].astype(f32), axis=0, keepdims=True
            )
        dq_turned[...] = jnp.zeros_like(dq_turned)
        for j in range(8):
            begin = j * seq
            span = 8 * seq - begin
            key_turned = qkv_ref[1, mb, j]
            queries = jnp.concatenate([qkv_ref[0, mb, i] for i in range(j, 8)], axis=1)
            grads = jnp.concatenate([dhead_ref[mb, i] for i in range(j, 8)], axis=1)
            scores = jnp.dot(turned(key_turned), queries, preferred_element_type=f32)
            dprobs = jnp.dot(turned(qkv_ref[2, mb, j]), grads, preferred_element_type=f32)
            key_pos = lax.broadcasted_iota(jnp.int32, (seq, 1), 0) + begin
            query_pos = lax.broadcasted_iota(jnp.int32, (1, span), 1) + begin
            allowed = (key_pos >= starts_ref[mb, :, begin:]) & (key_pos <= query_pos)
            probs = jnp.where(allowed, jnp.exp(scores - log_ref[mb, :, begin:]), 0.0)
            score_grad = (probs * (dprobs - delta[:, begin:])).astype(bf16)
            value_made = jnp.dot(probs.astype(bf16), g_rows[begin:, :], preferred_element_type=f32)
            key_made = jnp.dot(score_grad, q_rows[begin:, :], preferred_element_type=f32)
            dq_turned[:, begin:] += jnp.dot(key_turned, score_grad, preferred_element_type=f32)
            made[1, mb, j] = jnp.transpose(key_made).astype(bf16)
            made[2, mb, j] = jnp.transpose(value_made).astype(bf16)

            @pl.when(c == j)
            def keep():
                got[mb, 1, c] = made[1, mb, j]
                got[mb, 2, c] = made[2, mb, j]

            @pl.when(c != j)
            def send():
                for m in (1, 2):
                    remote(made.at[m, mb, j], got.at[mb, m, c], kv_s.at[m - 1, mb, j], kv_r.at[m - 1, mb, c], (j, z)).start()

        for i in range(8):
            made[0, mb, i] = (dq_turned[:, i * seq:(i + 1) * seq] * 0.125).astype(bf16)
        got[mb, 0, c] = made[0, mb, c]
        for k in range(1, 8):
            copy = remote(made.at[0, mb, place.ring(k)], got.at[mb, 0, c], q_s.at[mb, k - 1], q_r.at[mb, k - 1], (place.ring(k), z))
            copy.start()
            sends.append(copy)
        if mb == 0:
            wide.plane_start()
    x_low[...] = x_ref[...].astype(bf16).reshape(mbs * seq, width)
    wide.column_start()

    ones = jnp.ones((8, seq), bf16)
    bias_q = jnp.zeros((1, width), f32)
    bias_v = jnp.zeros((1, width), f32)
    for mb in range(mbs):
        rows = slice(mb * seq, (mb + 1) * seq)
        for k in range(1, 8):
            src = place.source(k)
            for m in (1, 2):
                slot = got.at[mb, m, src]
                remote(slot, slot, kv_s.at[m - 1, mb, 0], kv_r.at[m - 1, mb, src], (place.ring(k), z)).wait_recv()
            slot = got.at[mb, 0, src]
            remote(slot, slot, q_s.at[mb, k - 1], q_r.at[mb, k - 1], (place.ring(k), z)).wait_recv()
        grads = got[mb].reshape(3 * width, seq)
        xg_ref[mb] = one_ref[mb] + dots(grads, wt_ref[...], 0, 0)
        bias_q = bias_q + dots(ones, grads[0:width], 1, 1)[0:1]
        bias_v = bias_v + dots(ones, grads[2 * width:], 1, 1)[0:1]
        if mb == 1:
            wide.back_start()
        for m in range(3):
            block = jnp.dot(grads[m * width:(m + 1) * width], x_low[rows, :], preferred_element_type=f32)
            span = slice(m * width, (m + 1) * width)
            if mb == 0:
                total_thin[span, :] = block
            elif mb < mbs - 1:
                total_thin[span, :] += block
            else:
                block = (total_thin[span, :] + block).astype(bf16)
                total_thin_low = block
                for part in range(width // 64):
                    row = m * width + part * 64
                    owner, offset = row // 192, row % 192
                    for zz in range(4):
                        thin_part[owner % 2, owner // 2, zz, offset:offset + 64, :] = total_thin_low[
                            part * 64:(part + 1) * 64, zz * 128:(zz + 1) * 128]
    thin.pair_start()
    for zz in range(4):
        cols = slice(zz * 128, (zz + 1) * 128)
        vec_part[zz, 0:1, :] = bias_q[:, cols]
        vec_part[zz, 1:2, :] = bias_v[:, cols]
        vec_part[zz, 2:8, :] = sums_ref[0:6, cols]
        for r in range(4):
            vec_part[zz, 8 + r:9 + r, :] = sums_ref[6 + zz:7 + zz, r * 128:(r + 1) * 128]
        vec_part[zz, 12:16, :] = jnp.zeros((4, 128), f32)
    for d in (1, 3, 2):
        copy = remote(vec_part.at[place.up(d)], vec_column.at[d - 1], vc_s.at[d - 1], vc_r.at[d - 1], (c, place.up(d)))
        copy.start()
        sends.append(copy)
    thin.plane_start()
    for d in (1, 3, 2):
        remote(vec_column.at[d - 1], vec_column.at[d - 1], vc_s.at[d - 1], vc_r.at[d - 1], (c, place.up(d))).wait_recv()
    vec_plane[c] = vec_part[z] + vec_column[0] + vec_column[1] + vec_column[2]
    for k in range(1, 8):
        copy = remote(vec_plane.at[c], vec_plane.at[c], vp_s.at[k - 1], vp_r.at[k - 1], (place.ring(k), z))
        copy.start()
        sends.append(copy)
    wide.relay()
    thin.column_start()
    for k in range(1, 8):
        slot = vec_plane.at[place.source(k)]
        remote(slot, slot, vp_s.at[k - 1], vp_r.at[k - 1], (place.ring(k), z)).wait_recv()
    total = vec_plane[0]
    for k in range(1, 8):
        total = total + vec_plane[k]
    vec_ref[...] = total
    wide.finish()
    thin.back_start()
    thin.relay()
    thin.finish()
    for copy in sends:
        copy.wait_send()
    for j in range(8):
        @pl.when(c != j)
        def sent():
            for mb in range(mbs):
                for m in (1, 2):
                    remote(made.at[m, mb, j], got.at[mb, m, c], kv_s.at[m - 1, mb, j], kv_r.at[m - 1, mb, c], (j, z)).wait_send()


def back_call(qkv, head, log, dhead, starts, x, one, wt, grad, sums):
    mbs, seq, width = x.shape
    feat = width // HEADS
    count = 8 * seq
    vm = pl.BlockSpec(memory_space=pltpu.VMEM)
    dma = pltpu.SemaphoreType.DMA
    sds = jax.ShapeDtypeStruct
    V = pltpu.VMEM
    reduce_sems = [dma((1,)), dma((1,)), dma((3,)), dma((3,)), dma((3,)), dma((3,)), dma((3,)), dma((3,)), dma((4,)), dma((4,))]
    return pl.pallas_call(
        back_kernel,
        out_shape=(
            sds((mbs, seq, width), f32), sds((8, 144, 512), bf16), sds((8, 192, 128), bf16), sds((16, 128), f32),
        ),
        in_specs=[vm] * 10,
        out_specs=[vm] * 4,
        scratch_shapes=[
            V((count, feat), bf16), V((count, feat), bf16), V((feat, count), f32), V((1, count), f32),
            V((3, mbs, 8, feat, seq), bf16), V((mbs, 3, 8, feat, seq), bf16), V((mbs * seq, width), bf16),
            V((3 * width, width), f32),
            V((4, 4, 144, 512), bf16), V((4, 4, 144, 512), bf16), V((3, 4, 144, 512), bf16), V((4, 144, 512), bf16), V((3, 144, 512), bf16),
            V((2, 4, 4, 192, 128), bf16), V((4, 4, 192, 128), bf16), V((4, 4, 192, 128), bf16), V((3, 4, 192, 128), bf16),
            V((4, 192, 128), bf16), V((3, 192, 128), bf16),
            V((4, 16, 128), f32), V((3, 16, 128), f32), V((8, 16, 128), f32),
            dma((2, mbs, 8)), dma((2, mbs, 8)), dma((mbs, 7)), dma((mbs, 7)),
        ] + reduce_sems + reduce_sems + [dma((3,)), dma((3,)), dma((7,)), dma((7,))],
        compiler_params=pltpu.CompilerParams(collective_id=3, has_side_effects=True, vmem_limit_bytes=VMEM_LIMIT),
        name="back",
    )(qkv, head, log, dhead, starts, x, one, wt, grad, sums)


def unpack_kernel(wide_ref, thin_ref, wq_ref, wk_ref, wv_ref, wo_ref, wh_ref, wr_ref):
    wr_ref[...] = jnp.transpose(jnp.concatenate([wide_ref[owner, 0:64, :] for owner in range(8)], axis=0).astype(f32))
    for owner in range(8):
        rows = slice(owner * 16, (owner + 1) * 16)
        for q in range(4):
            wh_ref[rows, q * 512:(q + 1) * 512] = wide_ref[owner, 64 + 16 * q:80 + 16 * q, :].astype(f32)
        wo_ref[rows, :] = wide_ref[owner, 128:144, :].astype(f32)
    stacked = jnp.concatenate([thin_ref[owner] for owner in range(8)], axis=0).astype(f32)
    for m, out in enumerate((wq_ref, wk_ref, wv_ref)):
        out[...] = jnp.transpose(stacked[m * 512:(m + 1) * 512])


def unpack_call(wide, thin):
    vm = pl.BlockSpec(memory_space=pltpu.VMEM)
    sds = jax.ShapeDtypeStruct
    small = sds((128, 512), f32)
    return pl.pallas_call(
        unpack_kernel,
        out_shape=(small, small, small, small, sds((128, 2048), f32), sds((512, 512), f32)),
        in_specs=[vm] * 2,
        out_specs=[vm] * 6,
        compiler_params=pltpu.CompilerParams(vmem_limit_bytes=VMEM_LIMIT),
        name="unpack",
    )(wide, thin)


def head_shards(
    x_stream, y_stream, grad_x, grad_y, doc_start, query_weight, query_bias, key_weight, value_weight, value_bias,
    output_weight, output_bias, first_gain, first_shift, hidden_weight, hidden_bias, reduce_weight, reduce_bias,
    second_gain, second_shift,
):
    mbs = x_stream.shape[1]
    vec = pack_vec(query_bias, value_bias, output_bias, first_gain, first_shift, reduce_bias, second_gain, second_shift, hidden_bias)
    starts = doc_start.reshape(mbs, 1, -1)
    qkv, head, log, mixed, wt, vecs, wo, wh, wr = attend_call(
        x_stream[0], starts, query_weight, key_weight, value_weight, vec, output_weight, hidden_weight, reduce_weight
    )
    xn, yn, one, dhead, grad, sums = dense_call(mixed, x_stream[0], y_stream[0], grad_x[0], grad_y[0], wo, wh, wr, vecs)
    xg, wide, thin, small = back_call(qkv, head, log, dhead, starts, x_stream[0], one, wt, grad, sums)
    g_q, g_k, g_v, g_o, g_h, g_r = unpack_call(wide, thin)
    return (
        xn[None], yn[None], xg[None], g_q, small[0], g_k, g_v, small[1], g_o, small[2], small[3], small[4],
        g_h, small[8:12].reshape(-1), g_r, small[5], small[6], small[7],
    )


def solution(mesh):
    in_specs = (
        P("fsdp", None, "ctx", None),
        P("fsdp", None, "ctx", None),
        P("fsdp", None, "ctx", None),
        P("fsdp", None, "ctx", None),
        P("fsdp", None, None),
        P("fsdp", None),
        P("fsdp"),
        P("fsdp", None),
        P("fsdp", None),
        P("fsdp"),
        P("fsdp", None),
        P("fsdp"),
        P("fsdp"),
        P("fsdp"),
        P("fsdp", None),
        P("fsdp"),
        P("fsdp", None),
        P("fsdp"),
        P("fsdp"),
        P("fsdp"),
    )
    out_specs = (
        P("fsdp", None, "ctx", None),
        P("fsdp", None, "ctx", None),
        P("fsdp", None, "ctx", None),
        P("fsdp", None),
        P("fsdp"),
        P("fsdp", None),
        P("fsdp", None),
        P("fsdp"),
        P("fsdp", None),
        P("fsdp"),
        P("fsdp"),
        P("fsdp"),
        P("fsdp", None),
        P("fsdp"),
        P("fsdp", None),
        P("fsdp"),
        P("fsdp"),
        P("fsdp"),
    )
    body = head_shards if mesh.shape["ctx"] == HEADS and mesh.shape["fsdp"] == 4 else shards
    return jax.shard_map(body, mesh=mesh, in_specs=in_specs, out_specs=out_specs, check_vma=False)
```

```python
import math
import jax
import jax.numpy as jnp
from jax import lax
from jax.experimental import pallas as pl
from jax.experimental.pallas import tpu as pltpu
from jax.sharding import PartitionSpec as P

HEADS = 8
NEG = -1e30
bf16 = jnp.bfloat16
f32 = jnp.float32
MESH = pl.DeviceIdType.MESH
VMEM_LIMIT = 60 << 20


def dots(left, right, left_dim, right_dim):
    return lax.dot_general(
        left, right, (((left_dim,), (right_dim,)), ((), ())), preferred_element_type=f32
    )


def turned(block):
    return jnp.transpose(block.astype(f32)).astype(bf16)


class Place:
    def __init__(self):
        self.c = lax.axis_index("ctx")
        self.z = lax.axis_index("fsdp")
        self.core = lax.rem(self.c, 2)
        self.sibling = self.c + 1 - 2 * self.core
        self.middle = lax.rem(self.z + 1, 4) > 1

    def ring(self, k):
        return lax.rem(self.c + k, 8)

    def source(self, k):
        return lax.rem(self.c + 8 - k, 8)

    def up(self, d):
        return lax.rem(self.z + d, 4)

    def down(self, d):
        return lax.rem(self.z + 4 - d, 4)


def enter(place):
    barrier = pltpu.get_barrier_semaphore()
    for k in range(1, 8):
        pl.semaphore_signal(barrier, inc=1, device_id=(place.ring(k), place.z), device_id_type=MESH)
    for d in range(1, 4):
        pl.semaphore_signal(barrier, inc=1, device_id=(place.c, place.up(d)), device_id_type=MESH)
    pl.semaphore_wait(barrier, 10)


def remote(src, dst, send_sem, recv_sem, device):
    return pltpu.make_async_remote_copy(
        src_ref=src, dst_ref=dst, send_sem=send_sem, recv_sem=recv_sem,
        device_id=device, device_id_type=MESH,
    )


def aligned(start, size, unit):
    return pl.ds(pl.multiple_of(start, unit), size)


neg_big = -1e30
norm_eps = 1e-05
root_half = 0.7071067811865476
inv_root_tau = 0.3989422804014327


def swapped(block, axis, stride):
    count = lax.axis_size(axis)
    route = []
    for low in range(count):
        high = low | 1 << stride
        if high != low and high < count:
            route += [(low, high), (high, low)]
    return lax.ppermute(block, axis, route)


def matmul(left, right):
    return jnp.dot(left, right, preferred_element_type=jnp.float32)


def matmul_left_t(left, right):
    return lax.dot_general(
        left, right, (((0,), (0,)), ((), ())), preferred_element_type=jnp.float32
    )


def matmul_right_t(left, right):
    return lax.dot_general(
        left, right, (((1,), (1,)), ((), ())), preferred_element_type=jnp.float32
    )


def gelu_value(hidden):
    return hidden * 0.5 * (1.0 + jax.scipy.special.erf(hidden * root_half))


def gelu_slope(hidden):
    return 0.5 * (
        1.0 + jax.scipy.special.erf(hidden * root_half)
    ) + hidden * inv_root_tau * jnp.exp(-0.5 * hidden * hidden)


def norm_forward(total, gain, shift):
    mean_val = jnp.mean(total, axis=-1, keepdims=True)
    centered = total - mean_val
    inv_std = lax.rsqrt(jnp.mean(centered * centered, axis=-1, keepdims=True) + norm_eps)
    normed = centered * inv_std
    return (normed * gain + shift, normed, inv_std)


def norm_backward(upstream, normed, inv_std, gain):
    scaled = upstream * gain
    first_mean = jnp.mean(scaled, axis=-1, keepdims=True)
    second_mean = jnp.mean(scaled * normed, axis=-1, keepdims=True)
    return inv_std * (scaled - first_mean - normed * second_mean)


def allowed_pairs(query_pos, query_start, key_pos):
    return (key_pos[None, :] <= query_pos[:, None]) & (key_pos[None, :] >= query_start[:, None])


def pair_needed(key_lo, query_lo, span):
    needed = key_lo <= query_lo + span - 1
    return needed


def half_firsts(device, seq_dev, cycle_size):
    half = seq_dev // 2
    first = device * seq_dev
    second = (cycle_size - 1 - device) * seq_dev + half
    return (first, second)


def mirror_inputs(members, cycle_size):
    moved = members
    for bit in range(cycle_size.bit_length() - 1):
        moved = swapped((moved[0], moved[1], moved[2], moved[3]), "ctx", bit)
    return moved


def mirror_outputs(members, cycle_size):
    moved = members
    for bit in range(cycle_size.bit_length() - 1):
        moved = swapped((moved[0], moved[1], moved[2]), "ctx", bit)
    return moved


def block_scores(query_three, key_three, allowed, scale_factor):
    scores = (
        jnp.einsum("qhd,khd->hqk", query_three, key_three, preferred_element_type=jnp.float32)
        * scale_factor
    )
    return jnp.where(allowed[None], scores, neg_big)


def forward_update(state_mb, query_three, key_three, value_three, allowed, scale_factor):
    run_max, run_sum, run_acc = state_mb
    scores = block_scores(query_three, key_three, allowed, scale_factor)
    new_max = jnp.maximum(run_max, jnp.max(scores, axis=-1))
    rescale = jnp.exp(run_max - new_max)
    weights = jnp.where(allowed[None], jnp.exp(scores - new_max[:, :, None]), 0.0)
    new_sum = run_sum * rescale + jnp.sum(weights, axis=-1)
    mixed_sum = jnp.einsum(
        "hqk,khd->qhd",
        weights.astype(jnp.bfloat16),
        value_three,
        preferred_element_type=jnp.float32,
    )
    new_acc = run_acc * jnp.transpose(rescale)[:, :, None] + mixed_sum
    return (new_max, new_sum, new_acc)


def pair_grads(
    query_three, dout_three, key_three, value_three, allowed, log_total, row_delta, scale_factor
):
    scores = block_scores(query_three, key_three, allowed, scale_factor)
    prob_table = jnp.where(allowed[None], jnp.exp(scores - log_total[:, :, None]), 0.0)
    dprobs = jnp.einsum("qhd,khd->hqk", dout_three, value_three, preferred_element_type=jnp.float32)
    score_grad = (prob_table * (dprobs - row_delta[:, :, None])).astype(jnp.bfloat16)
    return (prob_table, score_grad)


def fold_blocks(pieces, state_all, update, base_rows):
    rows_in = pieces[0].shape[1]
    step_rows = min(rows_in, base_rows)

    def one_step(block_index, state_inner):
        offset = block_index * step_rows
        sliced = tuple(
            (lax.dynamic_slice_in_dim(member, offset, step_rows, 1) for member in pieces)
        )
        return update(state_inner, sliced, offset)

    return lax.fori_loop(0, rows_in // step_rows, one_step, state_all)


def shards(
    x_stream,
    y_stream,
    grad_x,
    grad_y,
    doc_start,
    query_weight,
    query_bias,
    key_weight,
    value_weight,
    value_bias,
    output_weight,
    output_bias,
    first_gain,
    first_shift,
    hidden_weight,
    hidden_bias,
    reduce_weight,
    reduce_bias,
    second_gain,
    second_shift,
):
    gathered = (
        lax.all_gather(query_weight, "fsdp", axis=0, tiled=True),
        lax.all_gather(query_bias, "fsdp", axis=0, tiled=True),
        lax.all_gather(key_weight, "fsdp", axis=0, tiled=True),
        lax.all_gather(value_weight, "fsdp", axis=0, tiled=True),
        lax.all_gather(value_bias, "fsdp", axis=0, tiled=True),
        lax.all_gather(output_weight, "fsdp", axis=0, tiled=True),
        lax.all_gather(output_bias, "fsdp", axis=0, tiled=True),
        lax.all_gather(first_gain, "fsdp", axis=0, tiled=True),
        lax.all_gather(first_shift, "fsdp", axis=0, tiled=True),
        lax.all_gather(hidden_weight, "fsdp", axis=0, tiled=True),
        lax.all_gather(hidden_bias, "fsdp", axis=0, tiled=True),
        lax.all_gather(reduce_weight, "fsdp", axis=0, tiled=True),
        lax.all_gather(reduce_bias, "fsdp", axis=0, tiled=True),
        lax.all_gather(second_gain, "fsdp", axis=0, tiled=True),
        lax.all_gather(second_shift, "fsdp", axis=0, tiled=True),
    )
    (
        w_query,
        b_query,
        w_key,
        w_value,
        b_value,
        w_output,
        b_output,
        gain_one,
        shift_one,
        w_hidden,
        b_hidden,
        w_reduce,
        b_reduce,
        gain_two,
        shift_two,
    ) = gathered
    b_query = b_query.astype(jnp.float32)
    b_value = b_value.astype(jnp.float32)
    b_output = b_output.astype(jnp.float32)
    gain_one = gain_one.astype(jnp.float32)
    shift_one = shift_one.astype(jnp.float32)
    b_hidden = b_hidden.astype(jnp.float32)
    b_reduce = b_reduce.astype(jnp.float32)
    gain_two = gain_two.astype(jnp.float32)
    shift_two = shift_two.astype(jnp.float32)
    micro_count, seq_dev, model_width = (x_stream.shape[1], x_stream.shape[2], x_stream.shape[3])
    half = seq_dev // 2
    head_count = HEADS
    head_dim = model_width // head_count
    scale_factor = 1.0 / math.sqrt(head_dim)
    token_rows = micro_count * seq_dev
    cycle_size = lax.axis_size("ctx")
    my_index = lax.axis_index("ctx")
    half_range = jnp.arange(half, dtype=jnp.int32)
    own_firsts = half_firsts(my_index, seq_dev, cycle_size)
    own_pos = [own_firsts[0] + half_range, own_firsts[1] + half_range]
    positions_own = jnp.concatenate(own_pos)
    doc_all = doc_start[0]
    starts_own = jnp.take(doc_all, positions_own, axis=1)
    own_starts = [
        [starts_own[micro_index, part * half : (part + 1) * half] for part in range(2)]
        for micro_index in range(micro_count)
    ]
    x_mb, y_mb, gx_mb, gy_mb = (x_stream[0], y_stream[0], grad_x[0], grad_y[0])
    moved = mirror_inputs(
        (x_mb[:, half:], y_mb[:, half:], gx_mb[:, half:], gy_mb[:, half:]), cycle_size
    )
    x_mb = jnp.concatenate([x_mb[:, :half], moved[0]], axis=1)
    y_mb = jnp.concatenate([y_mb[:, :half], moved[1]], axis=1)
    gx_mb = jnp.concatenate([gx_mb[:, :half], moved[2]], axis=1)
    gy_mb = jnp.concatenate([gy_mb[:, :half], moved[3]], axis=1)
    x_rows = x_mb.reshape(token_rows, model_width)
    y_rows = y_mb.reshape(token_rows, model_width)
    gx_rows = gx_mb.reshape(token_rows, model_width)
    gy_rows = gy_mb.reshape(token_rows, model_width)
    x_low = x_rows.astype(jnp.bfloat16)
    query_low = (matmul(x_low, w_query) + b_query).astype(jnp.bfloat16)
    key_low = matmul(x_low, w_key).astype(jnp.bfloat16)
    value_low = (matmul(x_low, w_value) + b_value).astype(jnp.bfloat16)
    query_mb = query_low.reshape(micro_count, seq_dev, model_width)
    key_mb = key_low.reshape(micro_count, seq_dev, model_width)
    value_mb = value_low.reshape(micro_count, seq_dev, model_width)
    query_three = [
        query_mb[micro_index].reshape(seq_dev, head_count, head_dim)
        for micro_index in range(micro_count)
    ]
    key_own = [
        key_mb[micro_index].reshape(seq_dev, head_count, head_dim)
        for micro_index in range(micro_count)
    ]
    value_own = [
        value_mb[micro_index].reshape(seq_dev, head_count, head_dim)
        for micro_index in range(micro_count)
    ]

    def forward_step(state_inner, sliced, key_first):
        key_block, value_block = sliced
        source = key_first // seq_dev
        key_firsts = half_firsts(source, seq_dev, cycle_size)
        updated = []
        for micro_index in range(micro_count):
            key_three = key_block[micro_index].reshape(seq_dev, head_count, head_dim)
            value_three = value_block[micro_index].reshape(seq_dev, head_count, head_dim)
            states = list(state_inner[micro_index])
            for query_part in range(2):
                query_piece = query_three[micro_index][query_part * half : (query_part + 1) * half]
                for key_part in range(2):
                    key_piece = key_three[key_part * half : (key_part + 1) * half]
                    value_piece = value_three[key_part * half : (key_part + 1) * half]
                    allowed = allowed_pairs(
                        own_pos[query_part],
                        own_starts[micro_index][query_part],
                        key_firsts[key_part] + half_range,
                    )
                    needed = pair_needed(key_firsts[key_part], own_firsts[query_part], half)

                    def forward_compute(state_mb):
                        return forward_update(
                            state_mb, query_piece, key_piece, value_piece, allowed, scale_factor
                        )

                    def forward_unchanged(state_mb):
                        return state_mb

                    states[query_part] = lax.cond(
                        needed, forward_compute, forward_unchanged, states[query_part]
                    )
            updated.append(tuple(states))
        return tuple(updated)

    def empty_state():
        return (
            jnp.full((head_count, half), neg_big, jnp.float32),
            jnp.zeros((head_count, half), jnp.float32),
            jnp.zeros((half, head_count, head_dim), jnp.float32),
        )

    forward_init = tuple(((empty_state(), empty_state()) for micro_index in range(micro_count)))
    attend_state = fold_blocks(
        (
            lax.all_gather(key_mb, "ctx", axis=1, tiled=True),
            lax.all_gather(value_mb, "ctx", axis=1, tiled=True),
        ),
        forward_init,
        forward_step,
        seq_dev,
    )
    out_parts = []
    log_parts = []
    for micro_index in range(micro_count):
        out_halves = []
        log_halves = []
        for query_part in range(2):
            run_max, run_sum, run_acc = attend_state[micro_index][query_part]
            out_halves.append(run_acc / jnp.transpose(run_sum)[:, :, None])
            log_halves.append(run_max + jnp.log(run_sum))
        out_parts.append(jnp.concatenate(out_halves, axis=0))
        log_parts.append(jnp.concatenate(log_halves, axis=1))
    out_raw = jnp.stack(out_parts)
    log_total_all = jnp.stack(log_parts)
    out_low = out_raw.reshape(token_rows, model_width).astype(jnp.bfloat16)
    branch = matmul(out_low, w_output) + b_output
    x_first, normed_one, inv_one = norm_forward(x_rows + branch, gain_one, shift_one)
    y_first = y_rows + branch
    x_first_low = x_first.astype(jnp.bfloat16)
    hidden_pre = matmul(x_first_low, w_hidden) + b_hidden
    hidden_low = gelu_value(hidden_pre).astype(jnp.bfloat16)
    second = matmul(hidden_low, w_reduce) + b_reduce
    x_next, normed_two, inv_two = norm_forward(x_first + second, gain_two, shift_two)
    y_next = y_first + second
    total_two_grad = norm_backward(gx_rows, normed_two, inv_two, gain_two)
    second_gain_grad = jnp.sum(gx_rows * normed_two, axis=0)
    second_shift_grad = jnp.sum(gx_rows, axis=0)
    second_grad = (total_two_grad + gy_rows).astype(jnp.bfloat16)
    reduce_weight_grad = matmul_left_t(hidden_low, second_grad)
    reduce_bias_grad = jnp.sum(second_grad.astype(jnp.float32), axis=0)
    hidden_grad = (matmul_right_t(second_grad, w_reduce) * gelu_slope(hidden_pre)).astype(
        jnp.bfloat16
    )
    hidden_weight_grad = matmul_left_t(x_first_low, hidden_grad)
    hidden_bias_grad = jnp.sum(hidden_grad.astype(jnp.float32), axis=0)
    first_up = total_two_grad + matmul_right_t(hidden_grad, w_hidden)
    total_one_grad = norm_backward(first_up, normed_one, inv_one, gain_one)
    first_gain_grad = jnp.sum(first_up * normed_one, axis=0)
    first_shift_grad = jnp.sum(first_up, axis=0)
    branch_grad = (total_one_grad + gy_rows).astype(jnp.bfloat16)
    output_weight_grad = matmul_left_t(out_low, branch_grad)
    output_bias_grad = jnp.sum(branch_grad.astype(jnp.float32), axis=0)
    dout_low = matmul_right_t(branch_grad, w_output).astype(jnp.bfloat16)
    dout_mb = dout_low.reshape(micro_count, seq_dev, head_count, head_dim)
    delta_all = jnp.einsum("bqhd,bqhd->bhq", dout_mb.astype(jnp.float32), out_raw)
    dout_three = [dout_mb[micro_index] for micro_index in range(micro_count)]
    dout_rows = dout_low.reshape(micro_count, seq_dev, model_width)

    def zero_query():
        return jnp.zeros((half, head_count, head_dim), jnp.float32)

    query_init = tuple(((zero_query(), zero_query()) for micro_index in range(micro_count)))

    def query_step(state_inner, sliced, key_first):
        key_block, value_block = sliced
        source = key_first // seq_dev
        key_firsts = half_firsts(source, seq_dev, cycle_size)
        updated = []
        for micro_index in range(micro_count):
            key_three = key_block[micro_index].reshape(seq_dev, head_count, head_dim)
            value_three = value_block[micro_index].reshape(seq_dev, head_count, head_dim)
            query_accs = list(state_inner[micro_index])
            for query_part in range(2):
                rows = slice(query_part * half, (query_part + 1) * half)
                query_piece = query_three[micro_index][rows]
                dout_piece = dout_three[micro_index][rows]
                log_piece = log_total_all[micro_index][:, rows]
                delta_piece = delta_all[micro_index][:, rows]
                for key_part in range(2):
                    key_piece = key_three[key_part * half : (key_part + 1) * half]
                    value_piece = value_three[key_part * half : (key_part + 1) * half]
                    allowed = allowed_pairs(
                        own_pos[query_part],
                        own_starts[micro_index][query_part],
                        key_firsts[key_part] + half_range,
                    )
                    needed = pair_needed(key_firsts[key_part], own_firsts[query_part], half)

                    def query_compute(query_acc):
                        prob_table, score_grad = pair_grads(
                            query_piece,
                            dout_piece,
                            key_piece,
                            value_piece,
                            allowed,
                            log_piece,
                            delta_piece,
                            scale_factor,
                        )
                        return (
                            query_acc
                            + jnp.einsum(
                                "hqk,khd->qhd",
                                score_grad,
                                key_piece,
                                preferred_element_type=jnp.float32,
                            )
                            * scale_factor
                        )

                    def query_unchanged(query_acc):
                        return query_acc

                    query_accs[query_part] = lax.cond(
                        needed, query_compute, query_unchanged, query_accs[query_part]
                    )
            updated.append(tuple(query_accs))
        return tuple(updated)

    query_parts = fold_blocks(
        (
            lax.all_gather(key_mb, "ctx", axis=1, tiled=True),
            lax.all_gather(value_mb, "ctx", axis=1, tiled=True),
        ),
        query_init,
        query_step,
        seq_dev,
    )
    stats_all = (
        lax.all_gather(log_total_all, "ctx", axis=2, tiled=True),
        lax.all_gather(delta_all, "ctx", axis=2, tiled=True),
    )

    def key_step(state_inner, sliced, query_begin):
        query_block, dout_block = sliced
        source = query_begin // seq_dev
        query_firsts = half_firsts(source, seq_dev, cycle_size)
        updated = []
        for micro_index in range(micro_count):
            log_block = lax.dynamic_slice_in_dim(stats_all[0][micro_index], query_begin, seq_dev, 1)
            delta_block = lax.dynamic_slice_in_dim(
                stats_all[1][micro_index], query_begin, seq_dev, 1
            )
            query_whole = query_block[micro_index].reshape(seq_dev, head_count, head_dim)
            dout_whole = dout_block[micro_index].reshape(seq_dev, head_count, head_dim)
            key_accs = [
                state_inner[micro_index][0][part * half : (part + 1) * half] for part in range(2)
            ]
            value_accs = [
                state_inner[micro_index][1][part * half : (part + 1) * half] for part in range(2)
            ]
            for query_part in range(2):
                rows = slice(query_part * half, (query_part + 1) * half)
                query_pos = query_firsts[query_part] + half_range
                starts_block = jnp.take(doc_all[micro_index], query_pos)
                query_piece = query_whole[rows]
                dout_piece = dout_whole[rows]
                log_piece = log_block[:, rows]
                delta_piece = delta_block[:, rows]
                for key_part in range(2):
                    key_piece = key_own[micro_index][key_part * half : (key_part + 1) * half]
                    value_piece = value_own[micro_index][key_part * half : (key_part + 1) * half]
                    allowed = allowed_pairs(query_pos, starts_block, own_pos[key_part])
                    needed = pair_needed(own_firsts[key_part], query_firsts[query_part], half)

                    def key_compute(operands):
                        key_acc, value_acc = operands
                        prob_table, score_grad = pair_grads(
                            query_piece,
                            dout_piece,
                            key_piece,
                            value_piece,
                            allowed,
                            log_piece,
                            delta_piece,
                            scale_factor,
                        )
                        key_add = (
                            jnp.einsum(
                                "hqk,qhd->khd",
                                score_grad,
                                query_piece,
                                preferred_element_type=jnp.float32,
                            )
                            * scale_factor
                        )
                        value_add = jnp.einsum(
                            "hqk,qhd->khd",
                            prob_table.astype(jnp.bfloat16),
                            dout_piece,
                            preferred_element_type=jnp.float32,
                        )
                        return (
                            key_acc + key_add.reshape(half, model_width),
                            value_acc + value_add.reshape(half, model_width),
                        )

                    def key_unchanged(operands):
                        return operands

                    result = lax.cond(
                        needed,
                        key_compute,
                        key_unchanged,
                        (key_accs[key_part], value_accs[key_part]),
                    )
                    key_accs[key_part] = result[0]
                    value_accs[key_part] = result[1]
            updated.append((jnp.concatenate(key_accs, axis=0), jnp.concatenate(value_accs, axis=0)))
        return tuple(updated)

    key_init = tuple(
        (
            (
                jnp.zeros((seq_dev, model_width), jnp.float32),
                jnp.zeros((seq_dev, model_width), jnp.float32),
            )
            for micro_index in range(micro_count)
        )
    )
    key_state = fold_blocks(
        (
            lax.all_gather(query_mb, "ctx", axis=1, tiled=True),
            lax.all_gather(dout_rows, "ctx", axis=1, tiled=True),
        ),
        key_init,
        key_step,
        seq_dev,
    )
    key_grad_sum = jnp.stack([key_state[micro_index][0] for micro_index in range(micro_count)])
    value_grad_sum = jnp.stack([key_state[micro_index][1] for micro_index in range(micro_count)])
    query_whole_parts = [
        jnp.concatenate([query_parts[micro_index][0], query_parts[micro_index][1]], axis=0)
        for micro_index in range(micro_count)
    ]
    query_grad_low = (
        jnp.stack(query_whole_parts).reshape(token_rows, model_width).astype(jnp.bfloat16)
    )
    key_grad_low = key_grad_sum.reshape(token_rows, model_width).astype(jnp.bfloat16)
    value_grad_low = value_grad_sum.reshape(token_rows, model_width).astype(jnp.bfloat16)
    query_weight_grad = matmul_left_t(x_low, query_grad_low)
    query_bias_grad = jnp.sum(query_grad_low.astype(jnp.float32), axis=0)
    key_weight_grad = matmul_left_t(x_low, key_grad_low)
    value_weight_grad = matmul_left_t(x_low, value_grad_low)
    value_bias_grad = jnp.sum(value_grad_low.astype(jnp.float32), axis=0)
    x_grad = (
        total_one_grad
        + matmul_right_t(query_grad_low, w_query)
        + matmul_right_t(key_grad_low, w_key)
        + matmul_right_t(value_grad_low, w_value)
    )
    shard_grads = (
        lax.psum_scatter(query_weight_grad, "fsdp", scatter_dimension=0, tiled=True),
        lax.psum_scatter(query_bias_grad, "fsdp", scatter_dimension=0, tiled=True),
        lax.psum_scatter(key_weight_grad, "fsdp", scatter_dimension=0, tiled=True),
        lax.psum_scatter(value_weight_grad, "fsdp", scatter_dimension=0, tiled=True),
        lax.psum_scatter(value_bias_grad, "fsdp", scatter_dimension=0, tiled=True),
        lax.psum_scatter(output_weight_grad, "fsdp", scatter_dimension=0, tiled=True),
        lax.psum_scatter(output_bias_grad, "fsdp", scatter_dimension=0, tiled=True),
        lax.psum_scatter(first_gain_grad, "fsdp", scatter_dimension=0, tiled=True),
        lax.psum_scatter(first_shift_grad, "fsdp", scatter_dimension=0, tiled=True),
        lax.psum_scatter(hidden_weight_grad, "fsdp", scatter_dimension=0, tiled=True),
        lax.psum_scatter(hidden_bias_grad, "fsdp", scatter_dimension=0, tiled=True),
        lax.psum_scatter(reduce_weight_grad, "fsdp", scatter_dimension=0, tiled=True),
        lax.psum_scatter(reduce_bias_grad, "fsdp", scatter_dimension=0, tiled=True),
        lax.psum_scatter(second_gain_grad, "fsdp", scatter_dimension=0, tiled=True),
        lax.psum_scatter(second_shift_grad, "fsdp", scatter_dimension=0, tiled=True),
    )
    summed = lax.psum(
        (
            shard_grads[0],
            shard_grads[1],
            shard_grads[2],
            shard_grads[3],
            shard_grads[4],
            shard_grads[5],
            shard_grads[6],
            shard_grads[7],
            shard_grads[8],
            shard_grads[9],
            shard_grads[10],
            shard_grads[11],
            shard_grads[12],
            shard_grads[13],
            shard_grads[14],
        ),
        "ctx",
    )
    mb_shape = (micro_count, seq_dev, model_width)
    x_next_mb = x_next.reshape(mb_shape)
    y_next_mb = y_next.reshape(mb_shape)
    x_grad_mb = x_grad.reshape(mb_shape)
    back = mirror_outputs(
        (x_next_mb[:, half:], y_next_mb[:, half:], x_grad_mb[:, half:]), cycle_size
    )
    x_next_mb = jnp.concatenate([x_next_mb[:, :half], back[0]], axis=1)
    y_next_mb = jnp.concatenate([y_next_mb[:, :half], back[1]], axis=1)
    x_grad_mb = jnp.concatenate([x_grad_mb[:, :half], back[2]], axis=1)
    out_shape = (1, micro_count, seq_dev, model_width)
    return (
        x_next_mb.reshape(out_shape),
        y_next_mb.reshape(out_shape),
        x_grad_mb.reshape(out_shape),
        summed[0],
        summed[1],
        summed[2],
        summed[3],
        summed[4],
        summed[5],
        summed[6],
        summed[7],
        summed[8],
        summed[9],
        summed[10],
        summed[11],
        summed[12],
        summed[13],
        summed[14],
    )


class Gather:
    def __init__(self, place, mine, at, sems):
        self.place, self.mine, self.at = place, mine, at
        self.zs, self.zr, self.fs, self.cs, self.cr = sems
        self.moved = []

    def direct(self, d):
        place = self.place
        return remote(
            self.mine, self.at(place.z, place.core), self.zs.at[d - 1], self.zr.at[d - 1], (place.c, place.up(d))
        )

    def start(self):
        place = self.place
        self.direct(2).start()

        @pl.when(place.z != 3)
        def above():
            self.direct(1).start()

        @pl.when(place.z != 0)
        def below():
            self.direct(3).start()

    def passed(self):
        place = self.place
        block = self.at(place.up(2), place.core)
        return remote(block, block, self.fs, self.zr.at[2 * (place.z - 1)], (place.c, 3 * (place.z - 1)))

    def arrive(self):
        place = self.place
        for d in (2, 1, 3):
            block = self.at(place.down(d), place.core)
            remote(block, block, self.zs.at[d - 1], self.zr.at[d - 1], (place.c, place.up(d))).wait_recv()
            if d == 2:

                @pl.when(place.middle)
                def onward():
                    self.passed().start()

            copy = remote(block, block, self.cs.at[d - 1], self.cr.at[d - 1], (place.sibling, place.z))
            copy.start()
            self.moved.append(copy)

    def ready(self):
        place = self.place
        for d in (2, 1, 3):
            block = self.at(place.down(d), 1 - place.core)
            remote(block, block, self.cs.at[d - 1], self.cr.at[d - 1], (place.sibling, place.z)).wait_recv()

    def finish(self):
        place = self.place
        for copy in self.moved:
            copy.wait_send()
        self.direct(2).wait_send()

        @pl.when(place.z != 3)
        def above():
            self.direct(1).wait_send()

        @pl.when(place.z != 0)
        def below():
            self.direct(3).wait_send()

        @pl.when(place.middle)
        def onward():
            self.passed().wait_send()


class Reduction:
    def __init__(self, place, part, pair, comb, slots, total, plane, out, sems):
        self.place = place
        self.part, self.pair, self.comb, self.slots = part, pair, comb, slots
        self.total, self.plane, self.out = total, plane, out
        (self.pair_s, self.pair_r, self.col_s, self.col_r, self.comb_r, self.plane_s, self.plane_r,
         self.back_s, self.back_r, self.core_s, self.core_r) = sems
        self.sent = []
        self.chip = lax.div(place.c, 2)

    def peer(self, k):
        return (2 * lax.rem(self.chip + k, 4) + self.place.core, self.place.z)

    def go(self, copy):
        copy.start()
        self.sent.append(copy)

    def pair_start(self):
        place = self.place
        self.go(remote(self.part.at[1 - place.core], self.pair, self.pair_s.at[0], self.pair_r.at[0], (place.sibling, place.z)))

    def own(self, zz):
        return self.part.at[self.place.core, zz]

    def end_copy(self, i):
        place = self.place
        upper = lax.div(place.z, 3)
        near, far = 1 + upper, 2 - upper
        goal = (3 - place.z, near, far)[i]
        target = (self.comb, self.slots.at[0], self.slots.at[2])[i]
        arrival = (self.comb_r.at[0], self.col_r.at[0], self.col_r.at[2])[i]
        return remote(self.own(goal), target, self.col_s.at[i], arrival, (place.c, far if i == 2 else near))

    def middle_copy(self, i):
        place = self.place
        end = 3 * (place.z - 1)
        goal = (end, 3 - place.z, 3 - end)[i]
        return remote(self.own(goal), self.slots.at[i], self.col_s.at[i], self.col_r.at[i], (place.c, goal))

    def column_start(self):
        place = self.place
        core = place.core
        remote(self.pair, self.pair, self.pair_s.at[0], self.pair_r.at[0], (place.sibling, place.z)).wait_recv()

        def add(zz, carry):
            for chip in range(4):
                self.part[core, zz, chip] = (
                    self.part[core, zz, chip].astype(f32) + self.pair[zz, chip].astype(f32)
                ).astype(bf16)
            return carry

        lax.fori_loop(0, 4, add, 0)

        @pl.when(place.middle)
        def inner():
            self.middle_copy(0).start()
            self.middle_copy(1).start()

        @pl.when(jnp.logical_not(place.middle))
        def outer():
            for i in range(3):
                self.end_copy(i).start()

    def column_combine(self):
        place = self.place
        core = place.core

        @pl.when(place.middle)
        def inner():
            self.end_copy(0).wait_recv()
            goal = 3 - 3 * (place.z - 1)
            for chip in range(4):
                self.part[core, goal, chip] = (
                    self.part[core, goal, chip].astype(f32) + self.comb[chip].astype(f32)
                ).astype(bf16)
            self.middle_copy(2).start()

    def plane_start(self):
        place = self.place
        core, z = place.core, place.z
        self.end_copy(1).wait_recv()
        self.end_copy(2).wait_recv()

        @pl.when(place.middle)
        def inner():
            self.middle_copy(1).wait_recv()
            for chip in range(4):
                self.total[chip] = (
                    self.part[core, z, chip].astype(f32) + self.slots[0, chip].astype(f32)
                    + self.slots[1, chip].astype(f32) + self.slots[2, chip].astype(f32)
                ).astype(bf16)

        @pl.when(jnp.logical_not(place.middle))
        def outer():
            for chip in range(4):
                self.total[chip] = (
                    self.part[core, z, chip].astype(f32) + self.slots[0, chip].astype(f32)
                    + self.slots[2, chip].astype(f32)
                ).astype(bf16)

        for k in range(1, 4):
            self.go(remote(
                self.total.at[lax.rem(self.chip + k, 4)], self.plane.at[k - 1],
                self.plane_s.at[k - 1], self.plane_r.at[k - 1], self.peer(k),
            ))

    def back_start(self):
        place = self.place
        for k in range(1, 4):
            slot = self.plane.at[k - 1]
            remote(slot, slot, self.plane_s.at[k - 1], self.plane_r.at[k - 1], self.peer(k)).wait_recv()
        total = self.total[self.chip].astype(f32)
        for k in range(3):
            total = total + self.plane[k].astype(f32)
        self.out[place.c] = total.astype(bf16)
        mine = self.out.at[place.c]
        for k in range(1, 4):
            self.go(remote(mine, mine, self.back_s.at[k - 1], self.back_r.at[k - 1], self.peer(k)))
        self.go(remote(mine, mine, self.core_s.at[0], self.core_r.at[0], (place.sibling, place.z)))

    def relay(self):
        place = self.place
        for k in range(1, 4):
            slot = self.out.at[2 * lax.rem(self.chip + 4 - k, 4) + place.core]
            remote(slot, slot, self.back_s.at[k - 1], self.back_r.at[k - 1], self.peer(k)).wait_recv()
            self.go(remote(slot, slot, self.core_s.at[k], self.core_r.at[k], (place.sibling, place.z)))

    def finish(self):
        place = self.place
        for k in range(4):
            slot = self.out.at[2 * lax.rem(self.chip + 4 - k, 4) + 1 - place.core]
            remote(slot, slot, self.core_s.at[k], self.core_r.at[k], (place.sibling, place.z)).wait_recv()
        for copy in self.sent:
            copy.wait_send()

        @pl.when(place.middle)
        def inner():
            for i in range(3):
                self.middle_copy(i).wait_send()

        @pl.when(jnp.logical_not(place.middle))
        def outer():
            for i in range(3):
                self.end_copy(i).wait_send()


def layer_kernel(
    starts_ref, wq_ref, wk_ref, wv_ref, qb_ref, vb_ref, ob_ref, fg_ref, fs_ref, rb_ref, sg_ref, ss_ref, hb_ref, x_hbm, y_hbm, gx_hbm, gy_hbm, wo_hbm, wh_hbm, wr_hbm,
    xn_hbm, yn_hbm, xg_hbm, red_out, hid_out, thin_out, vec_out,
    x_buf, y_buf, gx_buf, gy_buf, wt, wo, wh, wr, vecs, made, qkv, rows_a, rows_b,
    head, mixed, log_total, hid, hid_grad, first_low, second_grad, branch_grad, slope, dstage, dhead,
    dq_turned, delta, got,
    red_part, red_pair, red_comb, red_slots, red_total, red_plane,
    wide_part, wide_pair, wide_comb, wide_slots, wide_total, wide_plane,
    thin_part, thin_pair, thin_comb, thin_slots, thin_total, thin_plane,
    vec_part, vec_column, vec_plane, sums,
    load_sems, store_sems, own_sems, vz_s, vz_r,
    gz_s, gz_r, gf_s, gc_s, gc_r,
    a_s, a_r, o_s, o_r, d_s, d_r, kv_s, kv_r, q_s, q_r,
    pair_s, pair_r, col_s, col_r, comb_r, plane_s, plane_r, back_s, back_r, core_s, core_r,
    vc_s, vc_r, vp_s, vp_r,
):
    place = Place()
    c, z, core = place.c, place.z, place.core
    mbs, seq, width = x_buf.shape
    hidden = wh.shape[1]
    feat = width // HEADS
    shard = width // 4
    sends = []

    def go(copy):
        copy.start()
        sends.append(copy)

    loads = [
        [pltpu.make_async_copy(src.at[mb], dst.at[mb], load_sems.at[i, mb]) for mb in range(mbs)]
        for i, (src, dst) in enumerate(((x_hbm, x_buf), (y_hbm, y_buf), (gx_hbm, gx_buf), (gy_hbm, gy_buf)))
    ]
    for copy in loads[0]:
        copy.start()
    for m, w_ref in enumerate((wq_ref, wk_ref, wv_ref)):
        wt[m * width:(m + 1) * width, aligned(z * shard, shard, 128)] = turned(w_ref[...])
    shorts = [ref[...].reshape(1, shard) for ref in (qb_ref, vb_ref, ob_ref, fg_ref, fs_ref, rb_ref, sg_ref, ss_ref)]
    shorts += [hb_ref[r * 128:(r + 1) * 128].reshape(1, 128) for r in range(4)]
    for row, short in enumerate(shorts):
        vecs[z, row:row + 1, :] = short.astype(f32)
    vecs[z, 12:16, :] = jnp.zeros((4, 128), f32)
    enter(place)

    for d in (1, 3, 2):
        go(remote(vecs.at[z], vecs.at[z], vz_s.at[d - 1], vz_r.at[d - 1], (c, place.up(d))))

    def sems_of(i):
        return (gz_s.at[i], gz_r.at[i], gf_s.at[i], gc_s.at[i], gc_r.at[i])

    def turned_at(m):
        def at(zz, half):
            return wt.at[aligned(m * width + half * (width // 2), width // 2, 16), aligned(zz * shard, shard, 128)]
        return at

    def rows_at(full, count):
        def at(zz, half):
            return full.at[aligned(zz * count + half * (count // 2), count // 2, 16)]
        return at

    gathers = [Gather(place, turned_at(m)(z, core), turned_at(m), sems_of(m)) for m in range(3)]
    owned = []
    for i, (src, full) in enumerate(((wo_hbm, wo), (wh_hbm, wh), (wr_hbm, wr))):
        count = src.shape[0]
        mine = src.at[aligned(core * (count // 2), count // 2, 16)]
        gathers.append(Gather(place, mine, rows_at(full, count), sems_of(3 + i)))
        owned.append(pltpu.make_async_copy(src, full.at[aligned(z * count, count, 16)], own_sems.at[i]))
    for gather in gathers:
        gather.start()
    for copy in loads[0]:
        copy.wait()
    x_turned = hid
    for mb in range(mbs):
        x_turned[0:width, mb * seq:(mb + 1) * seq] = jnp.transpose(x_buf[mb]).astype(bf16)
    for copy in owned:
        copy.start()
    for group in loads[1:]:
        for copy in group:
            copy.start()
    for d in (1, 3, 2):
        slot = vecs.at[place.down(d)]
        remote(slot, slot, vz_s.at[d - 1], vz_r.at[d - 1], (c, place.up(d))).wait_recv()

    def vec(row):
        return jnp.concatenate([vecs[zz, row:row + 1, :] for zz in range(4)], axis=1)

    q_bias = jnp.transpose(vec(0))
    v_bias = jnp.transpose(vec(1))

    def project(m, mb):
        out = jnp.dot(
            wt[m * width:(m + 1) * width, :], x_turned[0:width, mb * seq:(mb + 1) * seq], preferred_element_type=f32
        )
        if m == 0:
            out = (out + q_bias).astype(bf16).astype(f32) * 0.125
        if m == 2:
            out = out + v_bias
        made[m, mb] = out.astype(bf16).reshape(8, feat, seq)
        qkv[m, mb, c] = made[m, mb, c]
        for k in range(1, 8):
            go(remote(
                made.at[m, mb, place.ring(k)], qkv.at[m, mb, c], a_s.at[m, mb, k - 1], a_r.at[m, mb, k - 1],
                (place.ring(k), z),
            ))

    gathers[0].arrive()
    gathers[0].ready()
    for mb in range(mbs):
        project(0, mb)
    gathers[1].arrive()
    gathers[2].arrive()
    gathers[1].ready()
    project(1, 0)
    gathers[2].ready()
    project(2, 0)
    for mb in range(1, mbs):
        project(1, mb)
        project(2, mb)

    for mb in range(mbs):
        for k in range(1, 8):
            for m in range(3):
                slot = qkv.at[m, mb, place.source(k)]
                remote(slot, slot, a_s.at[m, mb, k - 1], a_r.at[m, mb, k - 1], (place.ring(k), z)).wait_recv()
        for j in range(8):
            rows_a[j * seq:(j + 1) * seq, :] = turned(qkv[0, mb, j])
            rows_b[j * seq:(j + 1) * seq, :] = turned(qkv[2, mb, j])
        for i in range(8):
            span = (i + 1) * seq
            keys = jnp.concatenate([qkv[1, mb, j] for j in range(i + 1)], axis=1)
            scores = jnp.dot(rows_a[i * seq:(i + 1) * seq, :], keys, preferred_element_type=f32)
            key_pos = lax.broadcasted_iota(jnp.int32, (1, span), 1)
            query_pos = lax.broadcasted_iota(jnp.int32, (seq, 1), 0) + i * seq
            first = jnp.transpose(starts_ref[mb, :, i * seq:(i + 1) * seq])
            scores = jnp.where((key_pos >= first) & (key_pos <= query_pos), scores, NEG)
            top = jnp.max(scores, axis=1, keepdims=True)
            weights = jnp.exp(scores - top)
            total = jnp.sum(weights, axis=1, keepdims=True)
            out = jnp.dot(weights.astype(bf16), rows_b[0:span, :], preferred_element_type=f32)
            head[mb, i] = jnp.transpose(out / total).astype(bf16)
            log_total[mb, :, i * seq:(i + 1) * seq] = jnp.transpose(top + jnp.log(total))
        mixed[mb, c] = head[mb, c]
        for k in range(1, 8):
            go(remote(
                head.at[mb, place.ring(k)], mixed.at[mb, c], o_s.at[mb, k - 1], o_r.at[mb, k - 1], (place.ring(k), z)
            ))
        gathers[3 + mb].arrive()

    for copy in owned:
        copy.wait()
    for group in loads[1:]:
        for copy in group:
            copy.wait()
    b_output, gain_one, shift_one, b_reduce, gain_two, shift_two = [vec(row) for row in range(2, 8)]
    b_hidden = jnp.concatenate([vecs[zz, 8 + r:9 + r, :] for zz in range(4) for r in range(4)], axis=1)
    sums[...] = jnp.zeros_like(sums)

    def add_row(row, block):
        sums[row:row + 1, :] += jnp.sum(block, axis=0, keepdims=True)

    quarter = hidden // 4
    stores = []
    for mb in range(mbs):
        rows = slice(mb * seq, (mb + 1) * seq)
        for k in range(1, 8):
            slot = mixed.at[mb, place.source(k)]
            remote(slot, slot, o_s.at[mb, k - 1], o_r.at[mb, k - 1], (place.ring(k), z)).wait_recv()
        if mb == 0:
            gathers[3].ready()
        branch = dots(mixed[mb].reshape(width, seq), wo[...], 0, 0) + b_output
        x_first, normed_one, inv_one = norm_forward(x_buf[mb] + branch, gain_one, shift_one)
        first_low[rows, :] = x_first.astype(bf16)
        if mb == 0:
            gathers[4].ready()
        for q in range(4):
            cols = slice(q * quarter, (q + 1) * quarter)
            pre = jnp.dot(first_low[rows, :], wh[:, cols], preferred_element_type=f32) + b_hidden[:, cols]
            phi = 0.5 * (1.0 + lax.erf(pre * root_half))
            hid[rows, cols] = (pre * phi).astype(bf16)
            slope[:, cols] = phi + pre * inv_root_tau * jnp.exp(-0.5 * pre * pre)
        if mb == 0:
            gathers[5].ready()
        second = jnp.dot(hid[rows, :], wr[...], preferred_element_type=f32) + b_reduce
        x_next, normed_two, inv_two = norm_forward(x_first + second, gain_two, shift_two)
        upstream = gx_buf[mb]
        y_buf[mb] = y_buf[mb] + branch + second
        two_grad = norm_backward(upstream, normed_two, inv_two, gain_two)
        add_row(4, upstream * normed_two)
        add_row(5, upstream)
        gx_buf[mb] = x_next
        for copy in (
            pltpu.make_async_copy(gx_buf.at[mb], xn_hbm.at[mb], store_sems.at[0, mb]),
            pltpu.make_async_copy(y_buf.at[mb], yn_hbm.at[mb], store_sems.at[1, mb]),
        ):
            copy.start()
            stores.append(copy)
        second_low = (two_grad + gy_buf[mb]).astype(bf16)
        second_grad[rows, :] = second_low
        add_row(3, second_low.astype(f32))
        for q in range(4):
            cols = slice(q * quarter, (q + 1) * quarter)
            hid_grad[rows, cols] = (dots(second_low, wr[cols, :], 1, 1) * slope[:, cols]).astype(bf16)
            add_row(6 + q, hid_grad[rows, cols].astype(f32))
        first_up = two_grad + dots(hid_grad[rows, :], wh[...], 1, 1)
        one_grad = norm_backward(first_up, normed_one, inv_one, gain_one)
        add_row(1, first_up * normed_one)
        add_row(2, first_up)
        branch_low = (one_grad + gy_buf[mb]).astype(bf16)
        gy_buf[mb] = one_grad
        branch_grad[rows, :] = branch_low
        add_row(0, branch_low.astype(f32))
        dstage[mb] = dots(wo[...], branch_low, 1, 1).astype(bf16).reshape(8, feat, seq)
        dhead[mb, c] = dstage[mb, c]
        for k in range(1, 8):
            go(remote(
                dstage.at[mb, place.ring(k)], dhead.at[mb, c], d_s.at[mb, k - 1], d_r.at[mb, k - 1], (place.ring(k), z)
            ))

    def reduction(i, part, pair, comb, slots, total, plane, out):
        return Reduction(place, part, pair, comb, slots, total, plane, out, tuple(
            s.at[i] for s in (pair_s, pair_r, col_s, col_r, comb_r, plane_s, plane_r, back_s, back_r, core_s, core_r)
        ))

    red = reduction(0, red_part, red_pair, red_comb, red_slots, red_total, red_plane, red_out)
    wide = reduction(1, wide_part, wide_pair, wide_comb, wide_slots, wide_total, wide_plane, hid_out)
    thin = reduction(2, thin_part, thin_pair, thin_comb, thin_slots, thin_total, thin_plane, thin_out)

    second_all = turned(second_grad[...])
    for q in range(4):
        cols = slice(q * quarter, (q + 1) * quarter)
        part = jnp.dot(second_all, hid[:, cols], preferred_element_type=f32).astype(bf16)
        for owner in range(8):
            red_part[owner % 2, q, owner // 2] = part[owner * 64:(owner + 1) * 64, :]
    red.pair_start()
    first_all = turned(first_low[...])
    for q in range(4):
        cols = slice(q * quarter, (q + 1) * quarter)
        part = jnp.dot(first_all, hid_grad[:, cols], preferred_element_type=f32).astype(bf16)
        for zz in range(4):
            for owner in range(8):
                begin = zz * shard + owner * 16
                wide_part[owner % 2, zz, owner // 2, 16 * q:16 * q + 16, :] = part[begin:begin + 16, :]
    mixed_all = jnp.concatenate([mixed[mb].reshape(width, seq) for mb in range(mbs)], axis=1)
    part = jnp.dot(mixed_all, branch_grad[...], preferred_element_type=f32).astype(bf16)
    for zz in range(4):
        for owner in range(8):
            begin = zz * shard + owner * 16
            wide_part[owner % 2, zz, owner // 2, 64:80, :] = part[begin:begin + 16, :]
    wide.pair_start()
    red.column_start()
    x_low = first_low
    x_low[...] = x_buf[...].astype(bf16).reshape(mbs * seq, width)

    qkv_sent = 3 + 7 * 3 * mbs
    for copy in sends[:qkv_sent]:
        copy.wait_send()
    del sends[:qkv_sent]
    hooks = {
        (0, 0): [wide.column_start],
        (1, 0): [red.column_combine],
        (1, 7): [wide.column_combine],
        (2, 0): [red.plane_start],
        (2, 7): [red.back_start],
    }

    def kv_copy(m, mb, j):
        return remote(made.at[m, mb, j], got.at[mb, m, c], kv_s.at[m - 1, mb, j], kv_r.at[m - 1, mb, c], (j, z))

    for mb in range(mbs):
        for k in range(1, 8):
            slot = dhead.at[mb, place.source(k)]
            remote(slot, slot, d_s.at[mb, k - 1], d_r.at[mb, k - 1], (place.ring(k), z)).wait_recv()
        for j in range(8):
            cols = slice(j * seq, (j + 1) * seq)
            rows_a[cols, :] = turned(qkv[0, mb, j])
            rows_b[cols, :] = turned(dhead[mb, j])
            delta[:, cols] = jnp.sum(dhead[mb, j].astype(f32) * head[mb, j].astype(f32), axis=0, keepdims=True)
        dq_turned[...] = jnp.zeros_like(dq_turned)
        for j in range(8):
            begin = j * seq
            span = 8 * seq - begin
            key_turned = qkv[1, mb, j]
            queries = jnp.concatenate([qkv[0, mb, i] for i in range(j, 8)], axis=1)
            grads = jnp.concatenate([dhead[mb, i] for i in range(j, 8)], axis=1)
            scores = jnp.dot(turned(key_turned), queries, preferred_element_type=f32)
            dprobs = jnp.dot(turned(qkv[2, mb, j]), grads, preferred_element_type=f32)
            key_pos = lax.broadcasted_iota(jnp.int32, (seq, 1), 0) + begin
            query_pos = lax.broadcasted_iota(jnp.int32, (1, span), 1) + begin
            allowed = (key_pos >= starts_ref[mb, :, begin:]) & (key_pos <= query_pos)
            probs = jnp.where(allowed, jnp.exp(scores - log_total[mb, :, begin:]), 0.0)
            score_grad = (probs * (dprobs - delta[:, begin:])).astype(bf16)
            value_made = jnp.dot(probs.astype(bf16), rows_b[begin:, :], preferred_element_type=f32)
            key_made = jnp.dot(score_grad, rows_a[begin:, :], preferred_element_type=f32)
            dq_turned[:, begin:] += jnp.dot(key_turned, score_grad, preferred_element_type=f32)
            made[1, mb, j] = jnp.transpose(key_made).astype(bf16)
            made[2, mb, j] = jnp.transpose(value_made).astype(bf16)

            @pl.when(c == j)
            def keep():
                got[mb, 1, c] = made[1, mb, j]
                got[mb, 2, c] = made[2, mb, j]

            @pl.when(c != j)
            def send():
                kv_copy(1, mb, j).start()
                kv_copy(2, mb, j).start()

            for hook in hooks.get((mb, j), []):
                hook()

        for i in range(8):
            made[0, mb, i] = (dq_turned[:, i * seq:(i + 1) * seq] * 0.125).astype(bf16)
        got[mb, 0, c] = made[0, mb, c]
        for k in range(1, 8):
            go(remote(
                made.at[0, mb, place.ring(k)], got.at[mb, 0, c], q_s.at[mb, k - 1], q_r.at[mb, k - 1], (place.ring(k), z)
            ))

    ones = jnp.ones((8, seq), bf16)
    bias_q = jnp.zeros((1, width), f32)
    bias_v = jnp.zeros((1, width), f32)

    def x_gradient(mb):
        x_buf[mb] = gy_buf[mb] + dots(got[mb].reshape(3 * width, seq), wt[...], 0, 0)
        copy = pltpu.make_async_copy(x_buf.at[mb], xg_hbm.at[mb], store_sems.at[2, mb])
        copy.start()
        stores.append(copy)

    for mb in range(mbs):
        for k in range(1, 8):
            src = place.source(k)
            for m in (1, 2):
                slot = got.at[mb, m, src]
                remote(slot, slot, kv_s.at[m - 1, mb, 0], kv_r.at[m - 1, mb, src], (place.ring(k), z)).wait_recv()
            slot = got.at[mb, 0, src]
            remote(slot, slot, q_s.at[mb, k - 1], q_r.at[mb, k - 1], (place.ring(k), z)).wait_recv()
        bias_q = bias_q + dots(ones, got[mb, 0].reshape(width, seq), 1, 1)[0:1]
        bias_v = bias_v + dots(ones, got[mb, 2].reshape(width, seq), 1, 1)[0:1]
        if mb < mbs - 1:
            x_gradient(mb)
    for m in range(3):
        block = jnp.concatenate([got[mb, m].reshape(width, seq) for mb in range(mbs)], axis=1)
        block = jnp.dot(block, x_low[...], preferred_element_type=f32).astype(bf16)
        for part in range(width // 64):
            row = m * width + part * 64
            owner, offset = row // 192, row % 192
            for zz in range(4):
                thin_part[owner % 2, zz, owner // 2, offset:offset + 64, :] = block[
                    part * 64:(part + 1) * 64, zz * shard:(zz + 1) * shard]
    thin.pair_start()
    for zz in range(4):
        cols = slice(zz * shard, (zz + 1) * shard)
        vec_part[zz, 0:1, :] = bias_q[:, cols]
        vec_part[zz, 1:2, :] = bias_v[:, cols]
        vec_part[zz, 2:8, :] = sums[0:6, cols]
        for r in range(4):
            vec_part[zz, 8 + r:9 + r, :] = sums[6 + zz:7 + zz, r * 128:(r + 1) * 128]
        vec_part[zz, 12:16, :] = jnp.zeros((4, 128), f32)
    for d in (1, 3, 2):
        go(remote(vec_part.at[place.up(d)], vec_column.at[d - 1], vc_s.at[d - 1], vc_r.at[d - 1], (c, place.up(d))))
    thin.column_start()
    x_gradient(mbs - 1)
    thin.column_combine()
    for d in (1, 3, 2):
        slot = vec_column.at[d - 1]
        remote(slot, slot, vc_s.at[d - 1], vc_r.at[d - 1], (c, place.up(d))).wait_recv()
    vec_plane[c] = vec_part[z] + vec_column[0] + vec_column[1] + vec_column[2]
    for k in range(1, 8):
        go(remote(vec_plane.at[c], vec_plane.at[c], vp_s.at[k - 1], vp_r.at[k - 1], (place.ring(k), z)))
    wide.plane_start()
    thin.plane_start()
    red.relay()
    wide.back_start()
    thin.back_start()
    for k in range(1, 8):
        slot = vec_plane.at[place.source(k)]
        remote(slot, slot, vp_s.at[k - 1], vp_r.at[k - 1], (place.ring(k), z)).wait_recv()
    total = vec_plane[0]
    for k in range(1, 8):
        total = total + vec_plane[k]
    vec_out[...] = total
    wide.relay()
    thin.relay()
    for reduced in (red, wide, thin):
        reduced.finish()
    for gather in gathers:
        gather.finish()
    for copy in sends:
        copy.wait_send()
    for copy in stores:
        copy.wait()
    for j in range(8):
        @pl.when(c != j)
        def sent():
            for mb in range(mbs):
                kv_copy(1, mb, j).wait_send()
                kv_copy(2, mb, j).wait_send()


def layer_call(starts, wq, wk, wv, vectors, x, y, gx, gy, wo, wh, wr):
    mbs, seq, width = x.shape
    hidden = wh.shape[1]
    feat = width // HEADS
    count = HEADS * seq
    tokens = mbs * seq
    vm = pl.BlockSpec(memory_space=pltpu.VMEM)
    anym = pl.BlockSpec(memory_space=pl.ANY)
    dma = pltpu.SemaphoreType.DMA
    sds = jax.ShapeDtypeStruct
    V = pltpu.VMEM
    big = sds((mbs, seq, width), f32)

    def reduce_scratch(rows, cols):
        return [
            V((2, 4, 4, rows, cols), bf16), V((4, 4, rows, cols), bf16), V((4, rows, cols), bf16),
            V((3, 4, rows, cols), bf16), V((4, rows, cols), bf16), V((3, rows, cols), bf16),
        ]

    return pl.pallas_call(
        layer_kernel,
        out_shape=(
            big, big, big, sds((8, 64, 512), bf16), sds((8, 80, 512), bf16), sds((8, 192, 128), bf16), sds((16, 128), f32),
        ),
        in_specs=[vm] * 13 + [anym] * 7,
        out_specs=[anym] * 3 + [vm] * 4,
        scratch_shapes=[V((mbs, seq, width), f32)] * 4 + [
            V((3 * width, width), bf16), V((width, width), bf16), V((width, hidden), bf16), V((hidden, width), bf16),
            V((4, 16, 128), f32), V((3, mbs, 8, feat, seq), bf16), V((3, mbs, 8, feat, seq), bf16),
            V((count, feat), bf16), V((count, feat), bf16),
            V((mbs, 8, feat, seq), bf16), V((mbs, 8, feat, seq), bf16), V((mbs, 1, count), f32),
            V((tokens, hidden), bf16), V((tokens, hidden), bf16), V((tokens, width), bf16), V((tokens, width), bf16),
            V((tokens, width), bf16), V((seq, hidden), f32), V((mbs, 8, feat, seq), bf16), V((mbs, 8, feat, seq), bf16),
            V((feat, count), f32), V((1, count), f32), V((mbs, 3, 8, feat, seq), bf16),
        ] + reduce_scratch(64, 512) + reduce_scratch(80, 512) + reduce_scratch(192, 128) + [
            V((4, 16, 128), f32), V((3, 16, 128), f32), V((8, 16, 128), f32), V((16, width), f32),
            dma((4, mbs)), dma((3, mbs)), dma((3,)), dma((3,)), dma((3,)),
            dma((6, 3)), dma((6, 3)), dma((6,)), dma((6, 3)), dma((6, 3)),
            dma((3, mbs, 7)), dma((3, mbs, 7)), dma((mbs, 7)), dma((mbs, 7)), dma((mbs, 7)), dma((mbs, 7)),
            dma((2, mbs, 8)), dma((2, mbs, 8)), dma((mbs, 7)), dma((mbs, 7)),
            dma((3, 1)), dma((3, 1)), dma((3, 3)), dma((3, 3)), dma((3, 1)), dma((3, 3)), dma((3, 3)),
            dma((3, 3)), dma((3, 3)), dma((3, 4)), dma((3, 4)),
            dma((3,)), dma((3,)), dma((7,)), dma((7,)),
        ],
        compiler_params=pltpu.CompilerParams(collective_id=1, has_side_effects=True, vmem_limit_bytes=VMEM_LIMIT),
        name="layer",
    )(starts, wq, wk, wv, *vectors, x, y, gx, gy, wo, wh, wr)


def unpack_kernel(
    red_ref, hid_ref, thin_ref, vec_ref, xn_in, yn_in, xg_in,
    xn_out, yn_out, xg_out, wq_ref, wk_ref, wv_ref, wo_ref, wh_ref, wr_ref,
    qb_ref, vb_ref, ob_ref, fg_ref, fs_ref, rb_ref, sg_ref, ss_ref, hb_ref, held, sems, out_sems,
):
    mbs = held.shape[1]
    big = ((xn_in, xn_out), (yn_in, yn_out), (xg_in, xg_out))
    loads = [
        [pltpu.make_async_copy(src.at[mb], held.at[i, mb], sems.at[i, mb]) for mb in range(mbs)]
        for i, (src, _) in enumerate(big)
    ]
    stores = [
        [pltpu.make_async_copy(held.at[i, mb], dst.at[mb], out_sems.at[i, mb]) for mb in range(mbs)]
        for i, (_, dst) in enumerate(big)
    ]

    def turn_round(i):
        for mb in range(mbs):
            loads[i][mb].wait()
            stores[i][mb].start()

    for group in loads:
        for copy in group:
            copy.start()
    wr_ref[...] = jnp.transpose(jnp.concatenate([red_ref[owner] for owner in range(8)], axis=0).astype(f32))
    turn_round(0)
    for owner in range(8):
        rows = slice(owner * 16, (owner + 1) * 16)
        for q in range(4):
            wh_ref[rows, q * 512:(q + 1) * 512] = hid_ref[owner, 16 * q:16 * q + 16, :].astype(f32)
        wo_ref[rows, :] = hid_ref[owner, 64:80, :].astype(f32)
    turn_round(1)
    stacked = jnp.concatenate([thin_ref[owner] for owner in range(8)], axis=0).astype(f32)
    for m, out in enumerate((wq_ref, wk_ref, wv_ref)):
        out[...] = jnp.transpose(stacked[m * 512:(m + 1) * 512])
    turn_round(2)
    for row, out in enumerate((qb_ref, vb_ref, ob_ref, fg_ref, fs_ref, rb_ref, sg_ref, ss_ref)):
        out[...] = vec_ref[row]
    for r in range(4):
        hb_ref[r * 128:(r + 1) * 128] = vec_ref[8 + r]
    for group in stores:
        for copy in group:
            copy.wait()


def unpack_call(red, hid, thin, vec, xn, yn, xg):
    mbs = xn.shape[0]
    vm = pl.BlockSpec(memory_space=pltpu.VMEM)
    anym = pl.BlockSpec(memory_space=pl.ANY)
    sds = jax.ShapeDtypeStruct
    small = sds((128, 512), f32)
    big = sds(xn.shape, f32)
    dma = pltpu.SemaphoreType.DMA
    return pl.pallas_call(
        unpack_kernel,
        out_shape=(big, big, big, small, small, small, small, sds((128, 2048), f32), sds((512, 512), f32))
        + (sds((128,), f32),) * 8 + (sds((512,), f32),),
        in_specs=[vm] * 4 + [anym] * 3,
        out_specs=[anym] * 3 + [vm] * 15,
        scratch_shapes=[pltpu.VMEM((3,) + xn.shape, f32), dma((3, mbs)), dma((3, mbs))],
        compiler_params=pltpu.CompilerParams(vmem_limit_bytes=VMEM_LIMIT),
        name="unpack",
    )(red, hid, thin, vec, xn, yn, xg)


def head_shards(
    x_stream, y_stream, grad_x, grad_y, doc_start, query_weight, query_bias, key_weight, value_weight, value_bias,
    output_weight, output_bias, first_gain, first_shift, hidden_weight, hidden_bias, reduce_weight, reduce_bias,
    second_gain, second_shift,
):
    mbs = x_stream.shape[1]
    vectors = (query_bias, value_bias, output_bias, first_gain, first_shift, reduce_bias, second_gain, second_shift, hidden_bias)
    starts = doc_start.reshape(mbs, 1, -1)
    xn, yn, xg, red, hid, thin, small = layer_call(
        starts, query_weight, key_weight, value_weight, vectors, x_stream[0], y_stream[0], grad_x[0], grad_y[0],
        output_weight, hidden_weight, reduce_weight,
    )
    xn, yn, xg, g_q, g_k, g_v, g_o, g_h, g_r, qb, vb, ob, fg, fs, rb, sg, ss, hb = unpack_call(
        red, hid, thin, small, xn, yn, xg
    )
    return (
        xn[None], yn[None], xg[None], g_q, qb, g_k, g_v, vb, g_o, ob, fg, fs, g_h, hb, g_r, rb, sg, ss,
    )


def solution(mesh):
    in_specs = (
        P("fsdp", None, "ctx", None),
        P("fsdp", None, "ctx", None),
        P("fsdp", None, "ctx", None),
        P("fsdp", None, "ctx", None),
        P("fsdp", None, None),
        P("fsdp", None),
        P("fsdp"),
        P("fsdp", None),
        P("fsdp", None),
        P("fsdp"),
        P("fsdp", None),
        P("fsdp"),
        P("fsdp"),
        P("fsdp"),
        P("fsdp", None),
        P("fsdp"),
        P("fsdp", None),
        P("fsdp"),
        P("fsdp"),
        P("fsdp"),
    )
    out_specs = (
        P("fsdp", None, "ctx", None),
        P("fsdp", None, "ctx", None),
        P("fsdp", None, "ctx", None),
        P("fsdp", None),
        P("fsdp"),
        P("fsdp", None),
        P("fsdp", None),
        P("fsdp"),
        P("fsdp", None),
        P("fsdp"),
        P("fsdp"),
        P("fsdp"),
        P("fsdp", None),
        P("fsdp"),
        P("fsdp", None),
        P("fsdp"),
        P("fsdp"),
        P("fsdp"),
    )
    body = head_shards if mesh.shape["ctx"] == HEADS and mesh.shape["fsdp"] == 4 else shards
    return jax.shard_map(body, mesh=mesh, in_specs=in_specs, out_specs=out_specs, check_vma=False)
```

```python
import math
import jax
import jax.numpy as jnp
from jax import lax
from jax.experimental import pallas as pl
from jax.experimental.pallas import tpu as pltpu
from jax.sharding import PartitionSpec as P

HEADS = 8
NEG = -1e30
bf16 = jnp.bfloat16
f32 = jnp.float32
MESH = pl.DeviceIdType.MESH
VMEM_LIMIT = 62 << 20


def dots(left, right, left_dim, right_dim):
    return lax.dot_general(
        left, right, (((left_dim,), (right_dim,)), ((), ())), preferred_element_type=f32
    )


def turned(block):
    return jnp.transpose(block.astype(f32)).astype(bf16)


class Place:
    def __init__(self):
        self.c = lax.axis_index("ctx")
        self.z = lax.axis_index("fsdp")
        self.core = lax.rem(self.c, 2)
        self.x = lax.rem(lax.div(self.c, 2), 2)
        self.y = lax.div(self.c, 4)
        self.sibling = self.c + 1 - 2 * self.core
        self.x_next = self.c + 2 - 4 * self.x
        self.y_next = self.c + 4 - 8 * self.y
        self.middle = lax.rem(self.z + 1, 4) > 1

    def ring(self, k):
        return lax.rem(self.c + k, 8)

    def source(self, k):
        return lax.rem(self.c + 8 - k, 8)

    def up(self, d):
        return lax.rem(self.z + d, 4)

    def down(self, d):
        return lax.rem(self.z + 4 - d, 4)


def knock(place):
    barrier = pltpu.get_barrier_semaphore()
    for k in range(1, 8):
        pl.semaphore_signal(barrier, inc=1, device_id=(place.ring(k), place.z), device_id_type=MESH)
    for d in range(1, 4):
        pl.semaphore_signal(barrier, inc=1, device_id=(place.c, place.up(d)), device_id_type=MESH)


def enter():
    pl.semaphore_wait(pltpu.get_barrier_semaphore(), 10)


def remote(src, dst, send_sem, recv_sem, device):
    return pltpu.make_async_remote_copy(
        src_ref=src, dst_ref=dst, send_sem=send_sem, recv_sem=recv_sem,
        device_id=device, device_id_type=MESH,
    )


def aligned(start, size, unit):
    return pl.ds(pl.multiple_of(start, unit), size)


neg_big = -1e30
norm_eps = 1e-05
root_half = 0.7071067811865476
inv_root_tau = 0.3989422804014327


def swapped(block, axis, stride):
    count = lax.axis_size(axis)
    route = []
    for low in range(count):
        high = low | 1 << stride
        if high != low and high < count:
            route += [(low, high), (high, low)]
    return lax.ppermute(block, axis, route)


def matmul(left, right):
    return jnp.dot(left, right, preferred_element_type=jnp.float32)


def matmul_left_t(left, right):
    return lax.dot_general(
        left, right, (((0,), (0,)), ((), ())), preferred_element_type=jnp.float32
    )


def matmul_right_t(left, right):
    return lax.dot_general(
        left, right, (((1,), (1,)), ((), ())), preferred_element_type=jnp.float32
    )


def gelu_value(hidden):
    return hidden * 0.5 * (1.0 + jax.scipy.special.erf(hidden * root_half))


def gelu_slope(hidden):
    return 0.5 * (
        1.0 + jax.scipy.special.erf(hidden * root_half)
    ) + hidden * inv_root_tau * jnp.exp(-0.5 * hidden * hidden)


def norm_forward(total, gain, shift):
    mean_val = jnp.mean(total, axis=-1, keepdims=True)
    centered = total - mean_val
    inv_std = lax.rsqrt(jnp.mean(centered * centered, axis=-1, keepdims=True) + norm_eps)
    normed = centered * inv_std
    return (normed * gain + shift, normed, inv_std)


def norm_backward(upstream, normed, inv_std, gain):
    scaled = upstream * gain
    first_mean = jnp.mean(scaled, axis=-1, keepdims=True)
    second_mean = jnp.mean(scaled * normed, axis=-1, keepdims=True)
    return inv_std * (scaled - first_mean - normed * second_mean)


def allowed_pairs(query_pos, query_start, key_pos):
    return (key_pos[None, :] <= query_pos[:, None]) & (key_pos[None, :] >= query_start[:, None])


def pair_needed(key_lo, query_lo, span):
    needed = key_lo <= query_lo + span - 1
    return needed


def half_firsts(device, seq_dev, cycle_size):
    half = seq_dev // 2
    first = device * seq_dev
    second = (cycle_size - 1 - device) * seq_dev + half
    return (first, second)


def mirror_inputs(members, cycle_size):
    moved = members
    for bit in range(cycle_size.bit_length() - 1):
        moved = swapped((moved[0], moved[1], moved[2], moved[3]), "ctx", bit)
    return moved


def mirror_outputs(members, cycle_size):
    moved = members
    for bit in range(cycle_size.bit_length() - 1):
        moved = swapped((moved[0], moved[1], moved[2]), "ctx", bit)
    return moved


def block_scores(query_three, key_three, allowed, scale_factor):
    scores = (
        jnp.einsum("qhd,khd->hqk", query_three, key_three, preferred_element_type=jnp.float32)
        * scale_factor
    )
    return jnp.where(allowed[None], scores, neg_big)


def forward_update(state_mb, query_three, key_three, value_three, allowed, scale_factor):
    run_max, run_sum, run_acc = state_mb
    scores = block_scores(query_three, key_three, allowed, scale_factor)
    new_max = jnp.maximum(run_max, jnp.max(scores, axis=-1))
    rescale = jnp.exp(run_max - new_max)
    weights = jnp.where(allowed[None], jnp.exp(scores - new_max[:, :, None]), 0.0)
    new_sum = run_sum * rescale + jnp.sum(weights, axis=-1)
    mixed_sum = jnp.einsum(
        "hqk,khd->qhd",
        weights.astype(jnp.bfloat16),
        value_three,
        preferred_element_type=jnp.float32,
    )
    new_acc = run_acc * jnp.transpose(rescale)[:, :, None] + mixed_sum
    return (new_max, new_sum, new_acc)


def pair_grads(
    query_three, dout_three, key_three, value_three, allowed, log_total, row_delta, scale_factor
):
    scores = block_scores(query_three, key_three, allowed, scale_factor)
    prob_table = jnp.where(allowed[None], jnp.exp(scores - log_total[:, :, None]), 0.0)
    dprobs = jnp.einsum("qhd,khd->hqk", dout_three, value_three, preferred_element_type=jnp.float32)
    score_grad = (prob_table * (dprobs - row_delta[:, :, None])).astype(jnp.bfloat16)
    return (prob_table, score_grad)


def fold_blocks(pieces, state_all, update, base_rows):
    rows_in = pieces[0].shape[1]
    step_rows = min(rows_in, base_rows)

    def one_step(block_index, state_inner):
        offset = block_index * step_rows
        sliced = tuple(
            (lax.dynamic_slice_in_dim(member, offset, step_rows, 1) for member in pieces)
        )
        return update(state_inner, sliced, offset)

    return lax.fori_loop(0, rows_in // step_rows, one_step, state_all)


def shards(
    x_stream,
    y_stream,
    grad_x,
    grad_y,
    doc_start,
    query_weight,
    query_bias,
    key_weight,
    value_weight,
    value_bias,
    output_weight,
    output_bias,
    first_gain,
    first_shift,
    hidden_weight,
    hidden_bias,
    reduce_weight,
    reduce_bias,
    second_gain,
    second_shift,
):
    gathered = (
        lax.all_gather(query_weight, "fsdp", axis=0, tiled=True),
        lax.all_gather(query_bias, "fsdp", axis=0, tiled=True),
        lax.all_gather(key_weight, "fsdp", axis=0, tiled=True),
        lax.all_gather(value_weight, "fsdp", axis=0, tiled=True),
        lax.all_gather(value_bias, "fsdp", axis=0, tiled=True),
        lax.all_gather(output_weight, "fsdp", axis=0, tiled=True),
        lax.all_gather(output_bias, "fsdp", axis=0, tiled=True),
        lax.all_gather(first_gain, "fsdp", axis=0, tiled=True),
        lax.all_gather(first_shift, "fsdp", axis=0, tiled=True),
        lax.all_gather(hidden_weight, "fsdp", axis=0, tiled=True),
        lax.all_gather(hidden_bias, "fsdp", axis=0, tiled=True),
        lax.all_gather(reduce_weight, "fsdp", axis=0, tiled=True),
        lax.all_gather(reduce_bias, "fsdp", axis=0, tiled=True),
        lax.all_gather(second_gain, "fsdp", axis=0, tiled=True),
        lax.all_gather(second_shift, "fsdp", axis=0, tiled=True),
    )
    (
        w_query,
        b_query,
        w_key,
        w_value,
        b_value,
        w_output,
        b_output,
        gain_one,
        shift_one,
        w_hidden,
        b_hidden,
        w_reduce,
        b_reduce,
        gain_two,
        shift_two,
    ) = gathered
    b_query = b_query.astype(jnp.float32)
    b_value = b_value.astype(jnp.float32)
    b_output = b_output.astype(jnp.float32)
    gain_one = gain_one.astype(jnp.float32)
    shift_one = shift_one.astype(jnp.float32)
    b_hidden = b_hidden.astype(jnp.float32)
    b_reduce = b_reduce.astype(jnp.float32)
    gain_two = gain_two.astype(jnp.float32)
    shift_two = shift_two.astype(jnp.float32)
    micro_count, seq_dev, model_width = (x_stream.shape[1], x_stream.shape[2], x_stream.shape[3])
    half = seq_dev // 2
    head_count = HEADS
    head_dim = model_width // head_count
    scale_factor = 1.0 / math.sqrt(head_dim)
    token_rows = micro_count * seq_dev
    cycle_size = lax.axis_size("ctx")
    my_index = lax.axis_index("ctx")
    half_range = jnp.arange(half, dtype=jnp.int32)
    own_firsts = half_firsts(my_index, seq_dev, cycle_size)
    own_pos = [own_firsts[0] + half_range, own_firsts[1] + half_range]
    positions_own = jnp.concatenate(own_pos)
    doc_all = doc_start[0]
    starts_own = jnp.take(doc_all, positions_own, axis=1)
    own_starts = [
        [starts_own[micro_index, part * half : (part + 1) * half] for part in range(2)]
        for micro_index in range(micro_count)
    ]
    x_mb, y_mb, gx_mb, gy_mb = (x_stream[0], y_stream[0], grad_x[0], grad_y[0])
    moved = mirror_inputs(
        (x_mb[:, half:], y_mb[:, half:], gx_mb[:, half:], gy_mb[:, half:]), cycle_size
    )
    x_mb = jnp.concatenate([x_mb[:, :half], moved[0]], axis=1)
    y_mb = jnp.concatenate([y_mb[:, :half], moved[1]], axis=1)
    gx_mb = jnp.concatenate([gx_mb[:, :half], moved[2]], axis=1)
    gy_mb = jnp.concatenate([gy_mb[:, :half], moved[3]], axis=1)
    x_rows = x_mb.reshape(token_rows, model_width)
    y_rows = y_mb.reshape(token_rows, model_width)
    gx_rows = gx_mb.reshape(token_rows, model_width)
    gy_rows = gy_mb.reshape(token_rows, model_width)
    x_low = x_rows.astype(jnp.bfloat16)
    query_low = (matmul(x_low, w_query) + b_query).astype(jnp.bfloat16)
    key_low = matmul(x_low, w_key).astype(jnp.bfloat16)
    value_low = (matmul(x_low, w_value) + b_value).astype(jnp.bfloat16)
    query_mb = query_low.reshape(micro_count, seq_dev, model_width)
    key_mb = key_low.reshape(micro_count, seq_dev, model_width)
    value_mb = value_low.reshape(micro_count, seq_dev, model_width)
    query_three = [
        query_mb[micro_index].reshape(seq_dev, head_count, head_dim)
        for micro_index in range(micro_count)
    ]
    key_own = [
        key_mb[micro_index].reshape(seq_dev, head_count, head_dim)
        for micro_index in range(micro_count)
    ]
    value_own = [
        value_mb[micro_index].reshape(seq_dev, head_count, head_dim)
        for micro_index in range(micro_count)
    ]

    def forward_step(state_inner, sliced, key_first):
        key_block, value_block = sliced
        source = key_first // seq_dev
        key_firsts = half_firsts(source, seq_dev, cycle_size)
        updated = []
        for micro_index in range(micro_count):
            key_three = key_block[micro_index].reshape(seq_dev, head_count, head_dim)
            value_three = value_block[micro_index].reshape(seq_dev, head_count, head_dim)
            states = list(state_inner[micro_index])
            for query_part in range(2):
                query_piece = query_three[micro_index][query_part * half : (query_part + 1) * half]
                for key_part in range(2):
                    key_piece = key_three[key_part * half : (key_part + 1) * half]
                    value_piece = value_three[key_part * half : (key_part + 1) * half]
                    allowed = allowed_pairs(
                        own_pos[query_part],
                        own_starts[micro_index][query_part],
                        key_firsts[key_part] + half_range,
                    )
                    needed = pair_needed(key_firsts[key_part], own_firsts[query_part], half)

                    def forward_compute(state_mb):
                        return forward_update(
                            state_mb, query_piece, key_piece, value_piece, allowed, scale_factor
                        )

                    def forward_unchanged(state_mb):
                        return state_mb

                    states[query_part] = lax.cond(
                        needed, forward_compute, forward_unchanged, states[query_part]
                    )
            updated.append(tuple(states))
        return tuple(updated)

    def empty_state():
        return (
            jnp.full((head_count, half), neg_big, jnp.float32),
            jnp.zeros((head_count, half), jnp.float32),
            jnp.zeros((half, head_count, head_dim), jnp.float32),
        )

    forward_init = tuple(((empty_state(), empty_state()) for micro_index in range(micro_count)))
    attend_state = fold_blocks(
        (
            lax.all_gather(key_mb, "ctx", axis=1, tiled=True),
            lax.all_gather(value_mb, "ctx", axis=1, tiled=True),
        ),
        forward_init,
        forward_step,
        seq_dev,
    )
    out_parts = []
    log_parts = []
    for micro_index in range(micro_count):
        out_halves = []
        log_halves = []
        for query_part in range(2):
            run_max, run_sum, run_acc = attend_state[micro_index][query_part]
            out_halves.append(run_acc / jnp.transpose(run_sum)[:, :, None])
            log_halves.append(run_max + jnp.log(run_sum))
        out_parts.append(jnp.concatenate(out_halves, axis=0))
        log_parts.append(jnp.concatenate(log_halves, axis=1))
    out_raw = jnp.stack(out_parts)
    log_total_all = jnp.stack(log_parts)
    out_low = out_raw.reshape(token_rows, model_width).astype(jnp.bfloat16)
    branch = matmul(out_low, w_output) + b_output
    x_first, normed_one, inv_one = norm_forward(x_rows + branch, gain_one, shift_one)
    y_first = y_rows + branch
    x_first_low = x_first.astype(jnp.bfloat16)
    hidden_pre = matmul(x_first_low, w_hidden) + b_hidden
    hidden_low = gelu_value(hidden_pre).astype(jnp.bfloat16)
    second = matmul(hidden_low, w_reduce) + b_reduce
    x_next, normed_two, inv_two = norm_forward(x_first + second, gain_two, shift_two)
    y_next = y_first + second
    total_two_grad = norm_backward(gx_rows, normed_two, inv_two, gain_two)
    second_gain_grad = jnp.sum(gx_rows * normed_two, axis=0)
    second_shift_grad = jnp.sum(gx_rows, axis=0)
    second_grad = (total_two_grad + gy_rows).astype(jnp.bfloat16)
    reduce_weight_grad = matmul_left_t(hidden_low, second_grad)
    reduce_bias_grad = jnp.sum(second_grad.astype(jnp.float32), axis=0)
    hidden_grad = (matmul_right_t(second_grad, w_reduce) * gelu_slope(hidden_pre)).astype(
        jnp.bfloat16
    )
    hidden_weight_grad = matmul_left_t(x_first_low, hidden_grad)
    hidden_bias_grad = jnp.sum(hidden_grad.astype(jnp.float32), axis=0)
    first_up = total_two_grad + matmul_right_t(hidden_grad, w_hidden)
    total_one_grad = norm_backward(first_up, normed_one, inv_one, gain_one)
    first_gain_grad = jnp.sum(first_up * normed_one, axis=0)
    first_shift_grad = jnp.sum(first_up, axis=0)
    branch_grad = (total_one_grad + gy_rows).astype(jnp.bfloat16)
    output_weight_grad = matmul_left_t(out_low, branch_grad)
    output_bias_grad = jnp.sum(branch_grad.astype(jnp.float32), axis=0)
    dout_low = matmul_right_t(branch_grad, w_output).astype(jnp.bfloat16)
    dout_mb = dout_low.reshape(micro_count, seq_dev, head_count, head_dim)
    delta_all = jnp.einsum("bqhd,bqhd->bhq", dout_mb.astype(jnp.float32), out_raw)
    dout_three = [dout_mb[micro_index] for micro_index in range(micro_count)]
    dout_rows = dout_low.reshape(micro_count, seq_dev, model_width)

    def zero_query():
        return jnp.zeros((half, head_count, head_dim), jnp.float32)

    query_init = tuple(((zero_query(), zero_query()) for micro_index in range(micro_count)))

    def query_step(state_inner, sliced, key_first):
        key_block, value_block = sliced
        source = key_first // seq_dev
        key_firsts = half_firsts(source, seq_dev, cycle_size)
        updated = []
        for micro_index in range(micro_count):
            key_three = key_block[micro_index].reshape(seq_dev, head_count, head_dim)
            value_three = value_block[micro_index].reshape(seq_dev, head_count, head_dim)
            query_accs = list(state_inner[micro_index])
            for query_part in range(2):
                rows = slice(query_part * half, (query_part + 1) * half)
                query_piece = query_three[micro_index][rows]
                dout_piece = dout_three[micro_index][rows]
                log_piece = log_total_all[micro_index][:, rows]
                delta_piece = delta_all[micro_index][:, rows]
                for key_part in range(2):
                    key_piece = key_three[key_part * half : (key_part + 1) * half]
                    value_piece = value_three[key_part * half : (key_part + 1) * half]
                    allowed = allowed_pairs(
                        own_pos[query_part],
                        own_starts[micro_index][query_part],
                        key_firsts[key_part] + half_range,
                    )
                    needed = pair_needed(key_firsts[key_part], own_firsts[query_part], half)

                    def query_compute(query_acc):
                        prob_table, score_grad = pair_grads(
                            query_piece,
                            dout_piece,
                            key_piece,
                            value_piece,
                            allowed,
                            log_piece,
                            delta_piece,
                            scale_factor,
                        )
                        return (
                            query_acc
                            + jnp.einsum(
                                "hqk,khd->qhd",
                                score_grad,
                                key_piece,
                                preferred_element_type=jnp.float32,
                            )
                            * scale_factor
                        )

                    def query_unchanged(query_acc):
                        return query_acc

                    query_accs[query_part] = lax.cond(
                        needed, query_compute, query_unchanged, query_accs[query_part]
                    )
            updated.append(tuple(query_accs))
        return tuple(updated)

    query_parts = fold_blocks(
        (
            lax.all_gather(key_mb, "ctx", axis=1, tiled=True),
            lax.all_gather(value_mb, "ctx", axis=1, tiled=True),
        ),
        query_init,
        query_step,
        seq_dev,
    )
    stats_all = (
        lax.all_gather(log_total_all, "ctx", axis=2, tiled=True),
        lax.all_gather(delta_all, "ctx", axis=2, tiled=True),
    )

    def key_step(state_inner, sliced, query_begin):
        query_block, dout_block = sliced
        source = query_begin // seq_dev
        query_firsts = half_firsts(source, seq_dev, cycle_size)
        updated = []
        for micro_index in range(micro_count):
            log_block = lax.dynamic_slice_in_dim(stats_all[0][micro_index], query_begin, seq_dev, 1)
            delta_block = lax.dynamic_slice_in_dim(
                stats_all[1][micro_index], query_begin, seq_dev, 1
            )
            query_whole = query_block[micro_index].reshape(seq_dev, head_count, head_dim)
            dout_whole = dout_block[micro_index].reshape(seq_dev, head_count, head_dim)
            key_accs = [
                state_inner[micro_index][0][part * half : (part + 1) * half] for part in range(2)
            ]
            value_accs = [
                state_inner[micro_index][1][part * half : (part + 1) * half] for part in range(2)
            ]
            for query_part in range(2):
                rows = slice(query_part * half, (query_part + 1) * half)
                query_pos = query_firsts[query_part] + half_range
                starts_block = jnp.take(doc_all[micro_index], query_pos)
                query_piece = query_whole[rows]
                dout_piece = dout_whole[rows]
                log_piece = log_block[:, rows]
                delta_piece = delta_block[:, rows]
                for key_part in range(2):
                    key_piece = key_own[micro_index][key_part * half : (key_part + 1) * half]
                    value_piece = value_own[micro_index][key_part * half : (key_part + 1) * half]
                    allowed = allowed_pairs(query_pos, starts_block, own_pos[key_part])
                    needed = pair_needed(own_firsts[key_part], query_firsts[query_part], half)

                    def key_compute(operands):
                        key_acc, value_acc = operands
                        prob_table, score_grad = pair_grads(
                            query_piece,
                            dout_piece,
                            key_piece,
                            value_piece,
                            allowed,
                            log_piece,
                            delta_piece,
                            scale_factor,
                        )
                        key_add = (
                            jnp.einsum(
                                "hqk,qhd->khd",
                                score_grad,
                                query_piece,
                                preferred_element_type=jnp.float32,
                            )
                            * scale_factor
                        )
                        value_add = jnp.einsum(
                            "hqk,qhd->khd",
                            prob_table.astype(jnp.bfloat16),
                            dout_piece,
                            preferred_element_type=jnp.float32,
                        )
                        return (
                            key_acc + key_add.reshape(half, model_width),
                            value_acc + value_add.reshape(half, model_width),
                        )

                    def key_unchanged(operands):
                        return operands

                    result = lax.cond(
                        needed,
                        key_compute,
                        key_unchanged,
                        (key_accs[key_part], value_accs[key_part]),
                    )
                    key_accs[key_part] = result[0]
                    value_accs[key_part] = result[1]
            updated.append((jnp.concatenate(key_accs, axis=0), jnp.concatenate(value_accs, axis=0)))
        return tuple(updated)

    key_init = tuple(
        (
            (
                jnp.zeros((seq_dev, model_width), jnp.float32),
                jnp.zeros((seq_dev, model_width), jnp.float32),
            )
            for micro_index in range(micro_count)
        )
    )
    key_state = fold_blocks(
        (
            lax.all_gather(query_mb, "ctx", axis=1, tiled=True),
            lax.all_gather(dout_rows, "ctx", axis=1, tiled=True),
        ),
        key_init,
        key_step,
        seq_dev,
    )
    key_grad_sum = jnp.stack([key_state[micro_index][0] for micro_index in range(micro_count)])
    value_grad_sum = jnp.stack([key_state[micro_index][1] for micro_index in range(micro_count)])
    query_whole_parts = [
        jnp.concatenate([query_parts[micro_index][0], query_parts[micro_index][1]], axis=0)
        for micro_index in range(micro_count)
    ]
    query_grad_low = (
        jnp.stack(query_whole_parts).reshape(token_rows, model_width).astype(jnp.bfloat16)
    )
    key_grad_low = key_grad_sum.reshape(token_rows, model_width).astype(jnp.bfloat16)
    value_grad_low = value_grad_sum.reshape(token_rows, model_width).astype(jnp.bfloat16)
    query_weight_grad = matmul_left_t(x_low, query_grad_low)
    query_bias_grad = jnp.sum(query_grad_low.astype(jnp.float32), axis=0)
    key_weight_grad = matmul_left_t(x_low, key_grad_low)
    value_weight_grad = matmul_left_t(x_low, value_grad_low)
    value_bias_grad = jnp.sum(value_grad_low.astype(jnp.float32), axis=0)
    x_grad = (
        total_one_grad
        + matmul_right_t(query_grad_low, w_query)
        + matmul_right_t(key_grad_low, w_key)
        + matmul_right_t(value_grad_low, w_value)
    )
    shard_grads = (
        lax.psum_scatter(query_weight_grad, "fsdp", scatter_dimension=0, tiled=True),
        lax.psum_scatter(query_bias_grad, "fsdp", scatter_dimension=0, tiled=True),
        lax.psum_scatter(key_weight_grad, "fsdp", scatter_dimension=0, tiled=True),
        lax.psum_scatter(value_weight_grad, "fsdp", scatter_dimension=0, tiled=True),
        lax.psum_scatter(value_bias_grad, "fsdp", scatter_dimension=0, tiled=True),
        lax.psum_scatter(output_weight_grad, "fsdp", scatter_dimension=0, tiled=True),
        lax.psum_scatter(output_bias_grad, "fsdp", scatter_dimension=0, tiled=True),
        lax.psum_scatter(first_gain_grad, "fsdp", scatter_dimension=0, tiled=True),
        lax.psum_scatter(first_shift_grad, "fsdp", scatter_dimension=0, tiled=True),
        lax.psum_scatter(hidden_weight_grad, "fsdp", scatter_dimension=0, tiled=True),
        lax.psum_scatter(hidden_bias_grad, "fsdp", scatter_dimension=0, tiled=True),
        lax.psum_scatter(reduce_weight_grad, "fsdp", scatter_dimension=0, tiled=True),
        lax.psum_scatter(reduce_bias_grad, "fsdp", scatter_dimension=0, tiled=True),
        lax.psum_scatter(second_gain_grad, "fsdp", scatter_dimension=0, tiled=True),
        lax.psum_scatter(second_shift_grad, "fsdp", scatter_dimension=0, tiled=True),
    )
    summed = lax.psum(
        (
            shard_grads[0],
            shard_grads[1],
            shard_grads[2],
            shard_grads[3],
            shard_grads[4],
            shard_grads[5],
            shard_grads[6],
            shard_grads[7],
            shard_grads[8],
            shard_grads[9],
            shard_grads[10],
            shard_grads[11],
            shard_grads[12],
            shard_grads[13],
            shard_grads[14],
        ),
        "ctx",
    )
    mb_shape = (micro_count, seq_dev, model_width)
    x_next_mb = x_next.reshape(mb_shape)
    y_next_mb = y_next.reshape(mb_shape)
    x_grad_mb = x_grad.reshape(mb_shape)
    back = mirror_outputs(
        (x_next_mb[:, half:], y_next_mb[:, half:], x_grad_mb[:, half:]), cycle_size
    )
    x_next_mb = jnp.concatenate([x_next_mb[:, :half], back[0]], axis=1)
    y_next_mb = jnp.concatenate([y_next_mb[:, :half], back[1]], axis=1)
    x_grad_mb = jnp.concatenate([x_grad_mb[:, :half], back[2]], axis=1)
    out_shape = (1, micro_count, seq_dev, model_width)
    return (
        x_next_mb.reshape(out_shape),
        y_next_mb.reshape(out_shape),
        x_grad_mb.reshape(out_shape),
        summed[0],
        summed[1],
        summed[2],
        summed[3],
        summed[4],
        summed[5],
        summed[6],
        summed[7],
        summed[8],
        summed[9],
        summed[10],
        summed[11],
        summed[12],
        summed[13],
        summed[14],
    )


class Gather:
    def __init__(self, place, mine, at, sems, pair=None, side=None):
        self.place, self.mine, self.at, self.pair, self.side = place, mine, at, pair, side
        self.zs, self.zr, self.ps, self.pr, self.cs, self.cr = sems
        self.moved = []

    def held(self, zz, across=False, other=False):
        core = self.place.core
        core = 1 - core if other else core
        if self.pair is None:
            return self.at(zz, core)
        return self.at(zz, 2 * (1 - self.side if across else self.side) + core)

    def go(self, copy):
        copy.start()
        self.moved.append(copy)

    def start(self):
        place = self.place
        for d in (2, 1, 3):
            self.go(remote(self.mine, self.held(place.z), self.zs.at[d - 1], self.zr.at[d - 1], (place.c, place.up(d))))

    def arrive(self):
        place = self.place
        for d in (1, 3, 2):
            block = self.held(place.down(d))
            remote(block, block, self.zs.at[d - 1], self.zr.at[d - 1], (place.c, place.up(d))).wait_recv()
            if self.pair is not None:
                self.go(remote(block, block, self.ps.at[d - 1], self.pr.at[d - 1], (self.pair, place.z)))
            self.go(remote(block, block, self.cs.at[0, d - 1], self.cr.at[0, d - 1], (place.sibling, place.z)))

    def relay(self):
        place = self.place
        for d in (1, 3, 2):
            block = self.held(place.down(d), across=True)
            remote(block, block, self.ps.at[d - 1], self.pr.at[d - 1], (self.pair, place.z)).wait_recv()
            self.go(remote(block, block, self.cs.at[1, d - 1], self.cr.at[1, d - 1], (place.sibling, place.z)))

    def ready(self):
        place = self.place
        for d in (1, 3, 2):
            for across in (False, True)[:1 if self.pair is None else 2]:
                block = self.held(place.down(d), across=across, other=True)
                i = 1 if across else 0
                remote(block, block, self.cs.at[i, d - 1], self.cr.at[i, d - 1], (place.sibling, place.z)).wait_recv()

    def finish(self):
        for copy in self.moved:
            copy.wait_send()


class Reduction:
    def __init__(self, place, part, pair, comb, slots, total, plane, out, sems):
        self.place = place
        self.part, self.pair, self.comb, self.slots = part, pair, comb, slots
        self.total, self.plane, self.out = total, plane, out
        (self.pair_s, self.pair_r, self.col_s, self.col_r, self.comb_r, self.plane_s, self.plane_r,
         self.back_s, self.back_r, self.core_s, self.core_r) = sems
        self.sent = []
        self.chip = lax.div(place.c, 2)

    def peer(self, k):
        return (2 * lax.rem(self.chip + k, 4) + self.place.core, self.place.z)

    def go(self, copy):
        copy.start()
        self.sent.append(copy)

    def pair_start(self):
        place = self.place
        self.go(remote(self.part.at[1 - place.core], self.pair, self.pair_s.at[0], self.pair_r.at[0], (place.sibling, place.z)))

    def own(self, zz):
        return self.part.at[self.place.core, zz]

    def end_copy(self, i):
        place = self.place
        upper = lax.div(place.z, 3)
        near, far = 1 + upper, 2 - upper
        goal = (3 - place.z, near, far)[i]
        target = (self.comb, self.slots.at[0], self.slots.at[2])[i]
        arrival = (self.comb_r.at[0], self.col_r.at[0], self.col_r.at[2])[i]
        return remote(self.own(goal), target, self.col_s.at[i], arrival, (place.c, far if i == 2 else near))

    def middle_copy(self, i):
        place = self.place
        end = 3 * (place.z - 1)
        goal = (end, 3 - place.z, 3 - end)[i]
        return remote(self.own(goal), self.slots.at[i], self.col_s.at[i], self.col_r.at[i], (place.c, goal))

    def column_start(self):
        place = self.place
        core = place.core
        remote(self.pair, self.pair, self.pair_s.at[0], self.pair_r.at[0], (place.sibling, place.z)).wait_recv()

        def add(zz, carry):
            for chip in range(4):
                self.part[core, zz, chip] = (
                    self.part[core, zz, chip].astype(f32) + self.pair[zz, chip].astype(f32)
                ).astype(bf16)
            return carry

        lax.fori_loop(0, 4, add, 0)

        @pl.when(place.middle)
        def inner():
            self.middle_copy(0).start()
            self.middle_copy(1).start()

        @pl.when(jnp.logical_not(place.middle))
        def outer():
            for i in range(3):
                self.end_copy(i).start()

    def column_combine(self):
        place = self.place
        core = place.core

        @pl.when(place.middle)
        def inner():
            self.end_copy(0).wait_recv()
            goal = 3 - 3 * (place.z - 1)
            for chip in range(4):
                self.part[core, goal, chip] = (
                    self.part[core, goal, chip].astype(f32) + self.comb[chip].astype(f32)
                ).astype(bf16)
            self.middle_copy(2).start()

    def plane_start(self):
        place = self.place
        core, z = place.core, place.z
        self.end_copy(1).wait_recv()
        self.end_copy(2).wait_recv()

        @pl.when(place.middle)
        def inner():
            self.middle_copy(1).wait_recv()
            for chip in range(4):
                self.total[chip] = (
                    self.part[core, z, chip].astype(f32) + self.slots[0, chip].astype(f32)
                    + self.slots[1, chip].astype(f32) + self.slots[2, chip].astype(f32)
                ).astype(bf16)

        @pl.when(jnp.logical_not(place.middle))
        def outer():
            for chip in range(4):
                self.total[chip] = (
                    self.part[core, z, chip].astype(f32) + self.slots[0, chip].astype(f32)
                    + self.slots[2, chip].astype(f32)
                ).astype(bf16)

        for k in range(1, 4):
            self.go(remote(
                self.total.at[lax.rem(self.chip + k, 4)], self.plane.at[k - 1],
                self.plane_s.at[k - 1], self.plane_r.at[k - 1], self.peer(k),
            ))

    def back_start(self):
        place = self.place
        for k in range(1, 4):
            slot = self.plane.at[k - 1]
            remote(slot, slot, self.plane_s.at[k - 1], self.plane_r.at[k - 1], self.peer(k)).wait_recv()
        total = self.total[self.chip].astype(f32)
        for k in range(3):
            total = total + self.plane[k].astype(f32)
        self.out[place.c] = total.astype(bf16)
        mine = self.out.at[place.c]
        for k in range(1, 4):
            self.go(remote(mine, mine, self.back_s.at[k - 1], self.back_r.at[k - 1], self.peer(k)))
        self.go(remote(mine, mine, self.core_s.at[0], self.core_r.at[0], (place.sibling, place.z)))

    def relay(self):
        place = self.place
        for k in range(1, 4):
            slot = self.out.at[2 * lax.rem(self.chip + 4 - k, 4) + place.core]
            remote(slot, slot, self.back_s.at[k - 1], self.back_r.at[k - 1], self.peer(k)).wait_recv()
            self.go(remote(slot, slot, self.core_s.at[k], self.core_r.at[k], (place.sibling, place.z)))

    def finish(self):
        place = self.place
        for k in range(4):
            slot = self.out.at[2 * lax.rem(self.chip + 4 - k, 4) + 1 - place.core]
            remote(slot, slot, self.core_s.at[k], self.core_r.at[k], (place.sibling, place.z)).wait_recv()
        for copy in self.sent:
            copy.wait_send()

        @pl.when(place.middle)
        def inner():
            for i in range(3):
                self.middle_copy(i).wait_send()

        @pl.when(jnp.logical_not(place.middle))
        def outer():
            for i in range(3):
                self.end_copy(i).wait_send()


class Exchange:
    def __init__(self, place, pool, send, recv):
        self.place, self.pool, self.send, self.recv = place, pool, send, recv
        self.sent = []
        shift = place.sibling - place.c
        self.across = place.x_next + place.y_next - place.c
        self.from_sibling = (place.sibling, place.x_next + shift, place.y_next + shift, self.across + shift)

    def go(self, mb, i, j, owner, target, rows=None):
        block = self.pool.at[mb * 8 + owner]
        if rows is not None:
            block = block.at[rows]
        copy = remote(block, block, self.send.at[mb, i], self.recv.at[mb, j], (target, self.place.z))
        copy.start()
        self.sent.append(copy)

    def take(self, mb, j, owner, rows=None):
        block = self.pool.at[mb * 8 + owner]
        if rows is not None:
            block = block.at[rows]
        remote(block, block, self.send.at[mb, 0], self.recv.at[mb, j], (self.place.sibling, self.place.z)).wait_recv()

    def start(self, mb):
        place = self.place
        self.go(mb, 0, 0, place.c, place.x_next)
        self.go(mb, 1, 1, place.c, place.y_next)
        self.go(mb, 2, 4, place.c, place.sibling)

    def relay(self, mb):
        place = self.place
        half = self.pool.shape[1] // 2
        self.take(mb, 0, place.x_next)
        self.go(mb, 3, 2, place.x_next, place.y_next, pl.ds(0, half))
        self.take(mb, 1, place.y_next)
        self.go(mb, 4, 3, place.y_next, place.x_next, pl.ds(half, half))
        self.go(mb, 5, 5, place.x_next, place.sibling)
        self.go(mb, 6, 6, place.y_next, place.sibling)

    def last(self, mb):
        half = self.pool.shape[1] // 2
        self.take(mb, 2, self.across, pl.ds(0, half))
        self.take(mb, 3, self.across, pl.ds(half, half))
        self.go(mb, 7, 7, self.across, self.place.sibling)

    def ready(self, mb):
        for k, owner in enumerate(self.from_sibling):
            self.take(mb, 4 + k, owner)

    def finish(self):
        for copy in self.sent:
            copy.wait_send()


class ColumnSum:
    def __init__(self, place, part, column, out, sems):
        self.place, self.part, self.column, self.out = place, part, column, out
        self.col_s, self.col_r, self.back_s, self.back_r, self.core_s, self.core_r = sems
        self.sent = []
        self.chip = lax.div(place.c, 2)

    def peer(self, k):
        return (2 * lax.rem(self.chip + k, 4) + self.place.core, self.place.z)

    def go(self, copy):
        copy.start()
        self.sent.append(copy)

    def column_copy(self, d):
        place = self.place
        return remote(
            self.part.at[place.up(d)], self.column.at[d - 1], self.col_s.at[d - 1], self.col_r.at[d - 1],
            (place.c, place.up(d)),
        )

    def column_start(self):
        for d in (2, 1, 3):
            self.go(self.column_copy(d))

    def back_start(self):
        place = self.place
        for d in (1, 3, 2):
            self.column_copy(d).wait_recv()
        total = self.part[place.z].astype(f32)
        for d in range(3):
            total = total + self.column[d].astype(f32)
        self.out[place.c] = total.astype(bf16)
        mine = self.out.at[place.c]
        for k in range(1, 4):
            self.go(remote(mine, mine, self.back_s.at[k - 1], self.back_r.at[k - 1], self.peer(k)))
        self.go(remote(mine, mine, self.core_s.at[0], self.core_r.at[0], (place.sibling, place.z)))

    def relay(self):
        place = self.place
        for k in range(1, 4):
            slot = self.out.at[2 * lax.rem(self.chip + 4 - k, 4) + place.core]
            remote(slot, slot, self.back_s.at[k - 1], self.back_r.at[k - 1], self.peer(k)).wait_recv()
            self.go(remote(slot, slot, self.core_s.at[k], self.core_r.at[k], (place.sibling, place.z)))

    def finish(self):
        place = self.place
        for k in range(4):
            slot = self.out.at[2 * lax.rem(self.chip + 4 - k, 4) + 1 - place.core]
            remote(slot, slot, self.core_s.at[k], self.core_r.at[k], (place.sibling, place.z)).wait_recv()
        for copy in self.sent:
            copy.wait_send()


def layer_kernel(
    starts_ref, wq_ref, wk_ref, wv_ref, qb_ref, vb_ref, ob_ref, fg_ref, fs_ref, rb_ref, sg_ref, ss_ref, hb_ref, x_hbm, y_hbm, gx_hbm, gy_hbm, wo_hbm, wh_hbm, wr_hbm,
    xn_hbm, yn_hbm, xg_hbm, keep_hbm, red_out, hid_out, thin_out, vec_out,
    x_buf, y_buf, gx_buf, gy_buf, wt, wo, wh, wr, vecs, bias_cols, head_w, made, qkv, rows_a, rows_b,
    head, mixed, log_total, pool, first_low, second_grad, branch_grad, slope, dstage, dhead, two_grad, inv_one,
    dq_turned, delta, got,
    red_part, red_pair, red_comb, red_slots, red_total, red_plane,
    wide_part, wide_pair, wide_comb, wide_slots, wide_total, wide_plane,
    thin_total, thin_part, thin_column,
    vec_part, vec_column, vec_plane, sums,
    load_sems, store_sems, own_sems, keep_sems, vz_s, vz_r, ex_s, ex_r, hw_s, hw_r,
    gz_s, gz_r, gp_s, gp_r, gc_s, gc_r,
    o_s, o_r, d_s, d_r, kv_s, kv_r,
    pair_s, pair_r, col_s, col_r, comb_r, plane_s, plane_r, back_s, back_r, core_s, core_r,
    vc_s, vc_r, vp_s, vp_r,
):
    place = Place()
    c, z, core = place.c, place.z, place.core
    mbs, seq, width = x_buf.shape
    hidden = wh.shape[1]
    feat = width // HEADS
    shard = width // 4
    sends = []

    def go(copy):
        copy.start()
        sends.append(copy)

    loads = [
        [pltpu.make_async_copy(src.at[mb], dst.at[mb], load_sems.at[i, mb]) for mb in range(mbs)]
        for i, (src, dst) in enumerate(((x_hbm, x_buf), (y_hbm, y_buf), (gx_hbm, gx_buf), (gy_hbm, gy_buf)))
    ]
    knock(place)
    for copy in loads[0]:
        copy.start()
    own_column = aligned(z * shard, shard, 128)
    for m, w_ref in enumerate((wq_ref, wk_ref, wv_ref)):
        wt[m, :, :, own_column] = turned(w_ref[...]).reshape(8, feat, shard)
    head_w[:, :, own_column] = wt[:, c, :, own_column]
    shorts = [ref[...].reshape(1, shard) for ref in (qb_ref, vb_ref, ob_ref, fg_ref, fs_ref, rb_ref, sg_ref, ss_ref)]
    shorts += [hb_ref[r * 128:(r + 1) * 128].reshape(1, 128) for r in range(4)]
    for row, short in enumerate(shorts):
        vecs[z, row:row + 1, :] = short.astype(f32)
    vecs[z, 12:16, :] = jnp.zeros((4, 128), f32)
    for copy in loads[0]:
        copy.wait()
    for mb in range(mbs):
        pool[mb * 8 + c] = x_buf[mb].astype(bf16)
    enter()

    exchange = Exchange(place, pool, ex_s, ex_r)

    def head_copy(d):
        return remote(
            wt.at[:, c, :, own_column], head_w.at[:, :, own_column], hw_s.at[d - 1], hw_r.at[d - 1], (c, place.up(d))
        )

    exchange.start(0)
    for d in (2, 1, 3):
        go(head_copy(d))
    for d in (2, 1, 3):
        go(remote(vecs.at[z], vecs.at[z], vz_s.at[d - 1], vz_r.at[d - 1], (c, place.up(d))))
    exchange.start(1)

    def sems_of(i):
        return tuple(sem.at[i] for sem in (gz_s, gz_r, gp_s, gp_r, gc_s, gc_r))

    def turned_at(zz, part):
        return wt.at[:, pl.ds(part * 4, 4), :, aligned(zz * shard, shard, 128)]

    def rows_at(full, count, begin, rows):
        def at(zz, part):
            return full.at[aligned(zz * count + begin + part * rows, rows, 16)]
        return at

    along_x, along_y, alone = (place.x_next, place.x), (place.y_next, place.y), (None, 0)
    gathers = []
    owned = []
    plans = ((wo_hbm, wo, (along_x,)), (wh_hbm, wh, (along_x, along_y)), (wr_hbm, wr, (along_x, along_y)))
    for i, (src, full, chunks) in enumerate(plans):
        count = src.shape[0]
        for chunk, (pair, side) in enumerate(chunks):
            rows = count // len(chunks) // 4
            begin = chunk * (count // len(chunks))
            mine = src.at[aligned(begin + (2 * side + core) * rows, rows, 16)]
            gathers.append(Gather(place, mine, rows_at(full, count, begin, rows), sems_of(len(gathers)), pair, side))
        owned.append(pltpu.make_async_copy(src, full.at[aligned(z * count, count, 16)], own_sems.at[i]))
    gathers.append(Gather(place, turned_at(z, core), turned_at, sems_of(5)))
    g_out, g_in_a, g_in_b, g_red_a, g_red_b, g_proj = gathers
    for gather in gathers:
        gather.start()
    for copy in owned:
        copy.start()
    for group in loads[1:]:
        for copy in group:
            copy.start()
    exchange.relay(0)
    exchange.start(2)
    for d in (1, 3, 2):
        slot = vecs.at[place.down(d)]
        remote(slot, slot, vz_s.at[d - 1], vz_r.at[d - 1], (c, place.up(d))).wait_recv()
        head_copy(d).wait_recv()

    def vec(row):
        return jnp.concatenate([vecs[zz, row:row + 1, :] for zz in range(4)], axis=1)

    for i in range(2):
        bias_cols[i] = jnp.transpose(vec(i))
    q_bias, v_bias = [bias_cols[i, aligned(c * feat, feat, 8), :] for i in range(2)]
    exchange.last(0)
    exchange.relay(1)
    g_out.arrive()
    keeps = [pltpu.make_async_copy(pool.at[i], keep_hbm.at[i], keep_sems.at[i]) for i in range(mbs * 8)]
    backs = [pltpu.make_async_copy(keep_hbm.at[i], pool.at[i], keep_sems.at[i]) for i in range(mbs * 8)]

    def project(mb):
        for j in range(8):
            out = dots(head_w[...].reshape(3 * feat, width), pool[mb * 8 + j], 1, 1)
            query = (out[0:feat] + q_bias).astype(bf16).astype(f32) * 0.125
            qkv[0, mb, j] = query.astype(bf16)
            qkv[1, mb, j] = out[feat:2 * feat].astype(bf16)
            qkv[2, mb, j] = (out[2 * feat:] + v_bias).astype(bf16)

    forward_hooks = {
        (0, 3): [lambda: exchange.last(1)],
        (0, 6): [lambda: exchange.relay(2)],
        (0, 7): [g_in_a.arrive, g_out.relay],
        (1, 3): [lambda: exchange.last(2)],
        (1, 5): [g_in_a.relay],
        (1, 7): [g_in_b.arrive],
        (2, 4): [g_red_a.arrive, g_in_b.relay],
        (2, 7): [g_red_a.relay, g_red_b.arrive],
    }
    for mb in range(mbs):
        exchange.ready(mb)
        project(mb)
        for copy in keeps[mb * 8:mb * 8 + 8]:
            copy.start()
        for j in range(8):
            rows_a[j * seq:(j + 1) * seq, :] = turned(qkv[0, mb, j])
            rows_b[j * seq:(j + 1) * seq, :] = turned(qkv[2, mb, j])
        for i in range(8):
            span = (i + 1) * seq
            keys = jnp.concatenate([qkv[1, mb, j] for j in range(i + 1)], axis=1)
            scores = jnp.dot(rows_a[i * seq:(i + 1) * seq, :], keys, preferred_element_type=f32)
            key_pos = lax.broadcasted_iota(jnp.int32, (1, span), 1)
            query_pos = lax.broadcasted_iota(jnp.int32, (seq, 1), 0) + i * seq
            first = jnp.transpose(starts_ref[mb, :, i * seq:(i + 1) * seq])
            scores = jnp.where((key_pos >= first) & (key_pos <= query_pos), scores, NEG)
            top = jnp.max(scores, axis=1, keepdims=True)
            weights = jnp.exp(scores - top)
            total = jnp.sum(weights, axis=1, keepdims=True)
            out = jnp.dot(weights.astype(bf16), rows_b[0:span, :], preferred_element_type=f32)
            head[mb, i] = jnp.transpose(out / total).astype(bf16)
            log_total[mb, :, i * seq:(i + 1) * seq] = jnp.transpose(top + jnp.log(total))
            for hook in forward_hooks.get((mb, i), []):
                hook()
        mixed[mb, c] = head[mb, c]
        for k in range(1, 8):
            go(remote(
                head.at[mb, place.ring(k)], mixed.at[mb, c], o_s.at[mb, k - 1], o_r.at[mb, k - 1], (place.ring(k), z)
            ))

    exchange.finish()
    for copy in owned + keeps:
        copy.wait()
    for group in loads[1:]:
        for copy in group:
            copy.wait()
    b_output, gain_one, shift_one, b_reduce, gain_two, shift_two = [vec(row) for row in range(2, 8)]
    b_hidden = jnp.concatenate([vecs[zz, 8 + r:9 + r, :] for zz in range(4) for r in range(4)], axis=1)
    sums[...] = jnp.zeros_like(sums)

    def add_row(row, block):
        sums[row:row + 1, :] += jnp.sum(block, axis=0, keepdims=True)

    def reduction(i, part, pair, comb, slots, total, plane, out):
        return Reduction(place, part, pair, comb, slots, total, plane, out, tuple(
            s.at[i] for s in (pair_s, pair_r, col_s, col_r, comb_r, plane_s, plane_r, back_s, back_r, core_s, core_r)
        ))

    red = reduction(0, red_part, red_pair, red_comb, red_slots, red_total, red_plane, red_out)
    wide = reduction(1, wide_part, wide_pair, wide_comb, wide_slots, wide_total, wide_plane, hid_out)
    thin = ColumnSum(
        place, thin_part, thin_column, thin_out,
        tuple(s.at[2] for s in (col_s, col_r, back_s, back_r, core_s, core_r)),
    )
    quarter = hidden // 4
    quarters = [slice(q * quarter, (q + 1) * quarter) for q in range(4)]
    spans = [slice(mb * seq, (mb + 1) * seq) for mb in range(mbs)]
    stores = []

    def store(src, dst, i, mb):
        copy = pltpu.make_async_copy(src.at[mb], dst.at[mb], store_sems.at[i, mb])
        copy.start()
        stores.append(copy)

    def dense_in(mb):
        rows = spans[mb]
        for k in range(1, 8):
            slot = mixed.at[mb, place.source(k)]
            remote(slot, slot, o_s.at[mb, k - 1], o_r.at[mb, k - 1], (place.ring(k), z)).wait_recv()
        branch = dots(mixed[mb].reshape(width, seq), wo[...], 0, 0) + b_output
        value = x_buf[mb]
        x_first, normed, inv_std = norm_forward(value + branch, gain_one, shift_one)
        x_buf[mb] = normed
        inv_one[mb] = inv_std
        y_buf[mb] = y_buf[mb] + branch
        first_low[rows, :] = x_first.astype(bf16)
        for q, cols in enumerate(quarters):
            pre = jnp.dot(first_low[rows, :], wh[:, cols], preferred_element_type=f32) + b_hidden[:, cols]
            phi = 0.5 * (1.0 + lax.erf(pre * root_half))
            pool[q * mbs + mb] = (pre * phi).astype(bf16)
            slope[rows, cols] = phi + pre * inv_root_tau * jnp.exp(-0.5 * pre * pre)

    def dense_out(mb):
        rows = spans[mb]
        hid = jnp.concatenate([pool[q * mbs + mb] for q in range(4)], axis=1)
        second = jnp.dot(hid, wr[...], preferred_element_type=f32) + b_reduce
        x_next, normed, inv_std = norm_forward(x_buf[mb] * gain_one + shift_one + second, gain_two, shift_two)
        y_buf[mb] = y_buf[mb] + second
        store(y_buf, yn_hbm, 1, mb)
        upstream = gx_buf[mb]
        up = norm_backward(upstream, normed, inv_std, gain_two)
        two_grad[mb] = up
        add_row(4, upstream * normed)
        add_row(5, upstream)
        gx_buf[mb] = x_next
        store(gx_buf, xn_hbm, 0, mb)
        second_low = (up + gy_buf[mb]).astype(bf16)
        second_grad[rows, :] = second_low
        add_row(3, second_low.astype(f32))

    def dense_back(mb):
        rows = spans[mb]
        for q, cols in enumerate(quarters):
            low = (dots(second_grad[rows, :], wr[cols, :], 1, 1) * slope[rows, cols]).astype(bf16)
            pool[(4 + q) * mbs + mb] = low
            add_row(6 + q, low.astype(f32))
        hid_grad = jnp.concatenate([pool[(4 + q) * mbs + mb] for q in range(4)], axis=1)
        first_up = two_grad[mb] + dots(hid_grad, wh[...], 1, 1)
        one_grad = norm_backward(first_up, x_buf[mb], inv_one[mb], gain_one)
        add_row(1, first_up * x_buf[mb])
        add_row(2, first_up)
        branch_low = (one_grad + gy_buf[mb]).astype(bf16)
        gy_buf[mb] = one_grad
        branch_grad[rows, :] = branch_low
        add_row(0, branch_low.astype(f32))
        dstage[mb] = dots(wo[...], branch_low, 1, 1).astype(bf16).reshape(8, feat, seq)
        dhead[mb, c] = dstage[mb, c]
        for k in range(1, 8):
            go(remote(
                dstage.at[mb, place.ring(k)], dhead.at[mb, c], d_s.at[mb, k - 1], d_r.at[mb, k - 1], (place.ring(k), z)
            ))

    g_out.ready()
    g_in_a.ready()
    g_in_b.ready()
    for mb in range(mbs):
        dense_in(mb)
        if mb == 1:
            g_red_b.relay()
    g_red_a.ready()
    g_red_b.ready()
    for mb in range(mbs):
        dense_out(mb)
    second_all = turned(second_grad[...])
    for q, cols in enumerate(quarters):
        hid = pool[q * mbs:(q + 1) * mbs].reshape(mbs * seq, quarter)
        part = jnp.dot(second_all, hid, preferred_element_type=f32).astype(bf16)
        for owner in range(8):
            red_part[owner % 2, q, owner // 2] = part[owner * 64:(owner + 1) * 64, :]
    red.pair_start()
    dense_back(0)
    red.column_start()
    for mb in range(1, mbs):
        dense_back(mb)
    first_all = turned(first_low[...])
    for q, cols in enumerate(quarters):
        hid_grad = pool[(4 + q) * mbs:(5 + q) * mbs].reshape(mbs * seq, quarter)
        part = jnp.dot(first_all, hid_grad, preferred_element_type=f32).astype(bf16)
        for zz in range(4):
            for owner in range(8):
                begin = zz * shard + owner * 16
                wide_part[owner % 2, zz, owner // 2, 16 * q:16 * q + 16, :] = part[begin:begin + 16, :]
    mixed_all = jnp.concatenate([mixed[mb].reshape(width, seq) for mb in range(mbs)], axis=1)
    part = jnp.dot(mixed_all, branch_grad[...], preferred_element_type=f32).astype(bf16)
    for zz in range(4):
        for owner in range(8):
            begin = zz * shard + owner * 16
            wide_part[owner % 2, zz, owner // 2, 64:80, :] = part[begin:begin + 16, :]
    wide.pair_start()
    for copy in backs:
        copy.start()
    red.column_combine()

    ones = jnp.ones((8, 8 * seq), bf16)
    biases = [jnp.zeros((1, feat), f32), jnp.zeros((1, feat), f32)]

    def head_gradients(mb):
        if mb == 0:
            for copy in backs:
                copy.wait()
        block = jnp.concatenate([made[:, mb, j].reshape(3 * feat, seq) for j in range(8)], axis=1)
        rows = pool[mb * 8:(mb + 1) * 8].reshape(8 * seq, width)
        total = jnp.dot(block, rows, preferred_element_type=f32)
        thin_total[...] = total if mb == 0 else thin_total[...] + total
        biases[0] = biases[0] + dots(ones, block[0:feat], 1, 1)[0:1]
        biases[1] = biases[1] + dots(ones, block[2 * feat:], 1, 1)[0:1]

    hooks = {
        (0, 0): [wide.column_start],
        (0, 3): [g_proj.arrive],
        (1, 0): [red.plane_start],
        (1, 7): [wide.column_combine],
        (2, 0): [red.back_start],
        (2, 7): [red.relay],
    }

    def grad_copy(mb, j, source):
        return remote(made.at[:, mb, j], got.at[mb, :, source], kv_s.at[mb, j], kv_r.at[mb, source], (j, z))

    for mb in range(mbs):
        for k in range(1, 8):
            slot = dhead.at[mb, place.source(k)]
            remote(slot, slot, d_s.at[mb, k - 1], d_r.at[mb, k - 1], (place.ring(k), z)).wait_recv()
        for j in range(8):
            cols = slice(j * seq, (j + 1) * seq)
            rows_a[cols, :] = turned(qkv[0, mb, j])
            rows_b[cols, :] = turned(dhead[mb, j])
            delta[:, cols] = jnp.sum(dhead[mb, j].astype(f32) * head[mb, j].astype(f32), axis=0, keepdims=True)
        dq_turned[...] = jnp.zeros_like(dq_turned)
        for j in range(8):
            begin = j * seq
            span = 8 * seq - begin
            key_turned = qkv[1, mb, j]
            queries = jnp.concatenate([qkv[0, mb, i] for i in range(j, 8)], axis=1)
            grads = jnp.concatenate([dhead[mb, i] for i in range(j, 8)], axis=1)
            scores = jnp.dot(turned(key_turned), queries, preferred_element_type=f32)
            dprobs = jnp.dot(turned(qkv[2, mb, j]), grads, preferred_element_type=f32)
            key_pos = lax.broadcasted_iota(jnp.int32, (seq, 1), 0) + begin
            query_pos = lax.broadcasted_iota(jnp.int32, (1, span), 1) + begin
            allowed = (key_pos >= starts_ref[mb, :, begin:]) & (key_pos <= query_pos)
            probs = jnp.where(allowed, jnp.exp(scores - log_total[mb, :, begin:]), 0.0)
            score_grad = (probs * (dprobs - delta[:, begin:])).astype(bf16)
            value_made = jnp.dot(probs.astype(bf16), rows_b[begin:, :], preferred_element_type=f32)
            key_made = jnp.dot(score_grad, rows_a[begin:, :], preferred_element_type=f32)
            dq_turned[:, begin:] += jnp.dot(key_turned, score_grad, preferred_element_type=f32)
            made[1, mb, j] = jnp.transpose(key_made).astype(bf16)
            made[2, mb, j] = jnp.transpose(value_made).astype(bf16)
            made[0, mb, j] = (dq_turned[:, begin:begin + seq] * 0.125).astype(bf16)

            @pl.when(c == j)
            def keep():
                for m in range(3):
                    got[mb, m, c] = made[m, mb, j]

            @pl.when(c != j)
            def send():
                grad_copy(mb, j, c).start()

            for hook in hooks.get((mb, j), []):
                hook()
        head_gradients(mb)

    def x_gradient(mb):
        x_buf[mb] = gy_buf[mb] + dots(got[mb].reshape(3 * width, seq), wt[...].reshape(3 * width, width), 0, 0)
        copy = pltpu.make_async_copy(x_buf.at[mb], xg_hbm.at[mb], store_sems.at[2, mb])
        copy.start()
        stores.append(copy)

    low = thin_total[...].astype(bf16)
    for zz in range(4):
        thin_part[zz] = low[:, zz * shard:(zz + 1) * shard]
    thin.column_start()
    lane_head = lax.div(lax.broadcasted_iota(jnp.int32, (1, width), 1), feat)
    bias_q, bias_v = [jnp.where(lane_head == c, jnp.concatenate([b] * 8, axis=1), 0.0) for b in biases]
    for zz in range(4):
        cols = slice(zz * shard, (zz + 1) * shard)
        vec_part[zz, 0:1, :] = bias_q[:, cols]
        vec_part[zz, 1:2, :] = bias_v[:, cols]
        vec_part[zz, 2:8, :] = sums[0:6, cols]
        for r in range(4):
            vec_part[zz, 8 + r:9 + r, :] = sums[6 + zz:7 + zz, r * 128:(r + 1) * 128]
        vec_part[zz, 12:16, :] = jnp.zeros((4, 128), f32)
    for d in (1, 3, 2):
        go(remote(vec_part.at[place.up(d)], vec_column.at[d - 1], vc_s.at[d - 1], vc_r.at[d - 1], (c, place.up(d))))
    g_proj.ready()

    def take_gradients(mb):
        for k in range(1, 8):
            grad_copy(mb, 0, place.source(k)).wait_recv()
        x_gradient(mb)

    take_gradients(0)
    thin.back_start()
    wide.plane_start()
    for d in (1, 3, 2):
        slot = vec_column.at[d - 1]
        remote(slot, slot, vc_s.at[d - 1], vc_r.at[d - 1], (c, place.up(d))).wait_recv()
    vec_plane[c] = vec_part[z] + vec_column[0] + vec_column[1] + vec_column[2]
    for k in range(1, 8):
        go(remote(vec_plane.at[c], vec_plane.at[c], vp_s.at[k - 1], vp_r.at[k - 1], (place.ring(k), z)))
    take_gradients(1)
    thin.relay()
    wide.back_start()
    take_gradients(2)
    for k in range(1, 8):
        slot = vec_plane.at[place.source(k)]
        remote(slot, slot, vp_s.at[k - 1], vp_r.at[k - 1], (place.ring(k), z)).wait_recv()
    total = vec_plane[0]
    for k in range(1, 8):
        total = total + vec_plane[k]
    vec_out[...] = total
    wide.relay()
    for reduced in (red, wide, thin):
        reduced.finish()
    for gather in gathers:
        gather.finish()
    for copy in sends:
        copy.wait_send()
    for copy in stores:
        copy.wait()
    for j in range(8):
        @pl.when(c != j)
        def sent():
            for mb in range(mbs):
                grad_copy(mb, j, c).wait_send()


def layer_call(starts, wq, wk, wv, vectors, x, y, gx, gy, wo, wh, wr):
    mbs, seq, width = x.shape
    hidden = wh.shape[1]
    feat = width // HEADS
    count = HEADS * seq
    tokens = mbs * seq
    vm = pl.BlockSpec(memory_space=pltpu.VMEM)
    anym = pl.BlockSpec(memory_space=pl.ANY)
    dma = pltpu.SemaphoreType.DMA
    sds = jax.ShapeDtypeStruct
    V = pltpu.VMEM
    big = sds((mbs, seq, width), f32)

    def reduce_scratch(rows, cols):
        return [
            V((2, 4, 4, rows, cols), bf16), V((4, 4, rows, cols), bf16), V((4, rows, cols), bf16),
            V((3, 4, rows, cols), bf16), V((4, rows, cols), bf16), V((3, rows, cols), bf16),
        ]

    return pl.pallas_call(
        layer_kernel,
        out_shape=(
            big, big, big, sds((mbs * 8, seq, width), bf16), sds((8, 64, 512), bf16), sds((8, 80, 512), bf16), sds((8, 192, 128), bf16), sds((16, 128), f32),
        ),
        in_specs=[vm] * 13 + [anym] * 7,
        out_specs=[anym] * 4 + [vm] * 4,
        scratch_shapes=[V((mbs, seq, width), f32)] * 4 + [
            V((3, 8, feat, width), bf16), V((width, width), bf16), V((width, hidden), bf16), V((hidden, width), bf16),
            V((4, 16, 128), f32), V((2, width, 1), f32), V((3, feat, width), bf16), V((3, mbs, 8, feat, seq), bf16), V((3, mbs, 8, feat, seq), bf16),
            V((count, feat), bf16), V((count, feat), bf16),
            V((mbs, 8, feat, seq), bf16), V((mbs, 8, feat, seq), bf16), V((mbs, 1, count), f32),
            V((mbs * 8, seq, width), bf16), V((tokens, width), bf16), V((tokens, width), bf16),
            V((tokens, width), bf16), V((tokens, hidden), f32), V((mbs, 8, feat, seq), bf16), V((mbs, 8, feat, seq), bf16),
            V((mbs, seq, width), f32), V((mbs, seq, 1), f32),
            V((feat, count), f32), V((1, count), f32), V((mbs, 3, 8, feat, seq), bf16),
        ] + reduce_scratch(64, 512) + reduce_scratch(80, 512) + [
            V((3 * feat, width), f32), V((4, 192, 128), bf16), V((3, 192, 128), bf16),
        ] + [
            V((4, 16, 128), f32), V((3, 16, 128), f32), V((8, 16, 128), f32), V((16, width), f32),
            dma((4, mbs)), dma((3, mbs)), dma((3,)), dma((mbs * 8,)), dma((3,)), dma((3,)),
            dma((mbs, 8)), dma((mbs, 8)), dma((3,)), dma((3,)),
            dma((6, 3)), dma((6, 3)), dma((6, 3)), dma((6, 3)), dma((6, 2, 3)), dma((6, 2, 3)),
            dma((mbs, 7)), dma((mbs, 7)), dma((mbs, 7)), dma((mbs, 7)),
            dma((mbs, 8)), dma((mbs, 8)),
            dma((3, 1)), dma((3, 1)), dma((3, 3)), dma((3, 3)), dma((3, 1)), dma((3, 3)), dma((3, 3)),
            dma((3, 3)), dma((3, 3)), dma((3, 4)), dma((3, 4)),
            dma((3,)), dma((3,)), dma((7,)), dma((7,)),
        ],
        compiler_params=pltpu.CompilerParams(collective_id=1, has_side_effects=True, vmem_limit_bytes=VMEM_LIMIT),
        name="layer",
    )(starts, wq, wk, wv, *vectors, x, y, gx, gy, wo, wh, wr)


def unpack_kernel(
    red_ref, hid_ref, thin_ref, vec_ref, xn_in, yn_in, xg_in,
    xn_out, yn_out, xg_out, wq_ref, wk_ref, wv_ref, wo_ref, wh_ref, wr_ref,
    qb_ref, vb_ref, ob_ref, fg_ref, fs_ref, rb_ref, sg_ref, ss_ref, hb_ref, held, sems, out_sems,
):
    mbs = held.shape[1]
    big = ((xn_in, xn_out), (yn_in, yn_out), (xg_in, xg_out))
    loads = [
        [pltpu.make_async_copy(src.at[mb], held.at[i, mb], sems.at[i, mb]) for mb in range(mbs)]
        for i, (src, _) in enumerate(big)
    ]
    stores = [
        [pltpu.make_async_copy(held.at[i, mb], dst.at[mb], out_sems.at[i, mb]) for mb in range(mbs)]
        for i, (_, dst) in enumerate(big)
    ]

    def turn_round(i):
        for mb in range(mbs):
            loads[i][mb].wait()
            stores[i][mb].start()

    for group in loads:
        for copy in group:
            copy.start()
    wr_ref[...] = jnp.transpose(jnp.concatenate([red_ref[owner] for owner in range(8)], axis=0).astype(f32))
    turn_round(0)
    for owner in range(8):
        rows = slice(owner * 16, (owner + 1) * 16)
        for q in range(4):
            wh_ref[rows, q * 512:(q + 1) * 512] = hid_ref[owner, 16 * q:16 * q + 16, :].astype(f32)
        wo_ref[rows, :] = hid_ref[owner, 64:80, :].astype(f32)
    turn_round(1)
    for m, out in enumerate((wq_ref, wk_ref, wv_ref)):
        stacked = jnp.concatenate([thin_ref[owner, m * 64:(m + 1) * 64, :] for owner in range(8)], axis=0)
        out[...] = jnp.transpose(stacked.astype(f32))
    turn_round(2)
    for row, out in enumerate((qb_ref, vb_ref, ob_ref, fg_ref, fs_ref, rb_ref, sg_ref, ss_ref)):
        out[...] = vec_ref[row]
    for r in range(4):
        hb_ref[r * 128:(r + 1) * 128] = vec_ref[8 + r]
    for group in stores:
        for copy in group:
            copy.wait()


def unpack_call(red, hid, thin, vec, xn, yn, xg):
    mbs = xn.shape[0]
    vm = pl.BlockSpec(memory_space=pltpu.VMEM)
    anym = pl.BlockSpec(memory_space=pl.ANY)
    sds = jax.ShapeDtypeStruct
    small = sds((128, 512), f32)
    big = sds(xn.shape, f32)
    dma = pltpu.SemaphoreType.DMA
    return pl.pallas_call(
        unpack_kernel,
        out_shape=(big, big, big, small, small, small, small, sds((128, 2048), f32), sds((512, 512), f32))
        + (sds((128,), f32),) * 8 + (sds((512,), f32),),
        in_specs=[vm] * 4 + [anym] * 3,
        out_specs=[anym] * 3 + [vm] * 15,
        scratch_shapes=[pltpu.VMEM((3,) + xn.shape, f32), dma((3, mbs)), dma((3, mbs))],
        compiler_params=pltpu.CompilerParams(vmem_limit_bytes=VMEM_LIMIT),
        name="unpack",
    )(red, hid, thin, vec, xn, yn, xg)


def head_shards(
    x_stream, y_stream, grad_x, grad_y, doc_start, query_weight, query_bias, key_weight, value_weight, value_bias,
    output_weight, output_bias, first_gain, first_shift, hidden_weight, hidden_bias, reduce_weight, reduce_bias,
    second_gain, second_shift,
):
    mbs = x_stream.shape[1]
    vectors = (query_bias, value_bias, output_bias, first_gain, first_shift, reduce_bias, second_gain, second_shift, hidden_bias)
    starts = doc_start.reshape(mbs, 1, -1)
    xn, yn, xg, _, red, hid, thin, small = layer_call(
        starts, query_weight, key_weight, value_weight, vectors, x_stream[0], y_stream[0], grad_x[0], grad_y[0],
        output_weight, hidden_weight, reduce_weight,
    )
    xn, yn, xg, g_q, g_k, g_v, g_o, g_h, g_r, qb, vb, ob, fg, fs, rb, sg, ss, hb = unpack_call(
        red, hid, thin, small, xn, yn, xg
    )
    return (
        xn[None], yn[None], xg[None], g_q, qb, g_k, g_v, vb, g_o, ob, fg, fs, g_h, hb, g_r, rb, sg, ss,
    )


def solution(mesh):
    in_specs = (
        P("fsdp", None, "ctx", None),
        P("fsdp", None, "ctx", None),
        P("fsdp", None, "ctx", None),
        P("fsdp", None, "ctx", None),
        P("fsdp", None, None),
        P("fsdp", None),
        P("fsdp"),
        P("fsdp", None),
        P("fsdp", None),
        P("fsdp"),
        P("fsdp", None),
        P("fsdp"),
        P("fsdp"),
        P("fsdp"),
        P("fsdp", None),
        P("fsdp"),
        P("fsdp", None),
        P("fsdp"),
        P("fsdp"),
        P("fsdp"),
    )
    out_specs = (
        P("fsdp", None, "ctx", None),
        P("fsdp", None, "ctx", None),
        P("fsdp", None, "ctx", None),
        P("fsdp", None),
        P("fsdp"),
        P("fsdp", None),
        P("fsdp", None),
        P("fsdp"),
        P("fsdp", None),
        P("fsdp"),
        P("fsdp"),
        P("fsdp"),
        P("fsdp", None),
        P("fsdp"),
        P("fsdp", None),
        P("fsdp"),
        P("fsdp"),
        P("fsdp"),
    )
    body = head_shards if mesh.shape["ctx"] == HEADS and mesh.shape["fsdp"] == 4 else shards
    return jax.shard_map(body, mesh=mesh, in_specs=in_specs, out_specs=out_specs, check_vma=False)
```

```python
import math
import jax
import jax.numpy as jnp
from jax import lax
from jax.experimental import pallas as pl
from jax.experimental.pallas import tpu as pltpu
from jax.sharding import PartitionSpec as P

HEADS = 8
NEG = -1e30
bf16 = jnp.bfloat16
f32 = jnp.float32
MESH = pl.DeviceIdType.MESH
VMEM_LIMIT = 62 << 20


def dots(left, right, left_dim, right_dim):
    return lax.dot_general(
        left, right, (((left_dim,), (right_dim,)), ((), ())), preferred_element_type=f32
    )


def turned(block):
    return jnp.transpose(block.astype(f32)).astype(bf16)


class Place:
    def __init__(self):
        self.c = lax.axis_index("ctx")
        self.z = lax.axis_index("fsdp")
        self.core = lax.rem(self.c, 2)
        self.x = lax.rem(lax.div(self.c, 2), 2)
        self.y = lax.div(self.c, 4)
        self.sibling = self.c + 1 - 2 * self.core
        self.x_next = self.c + 2 - 4 * self.x
        self.y_next = self.c + 4 - 8 * self.y
        self.middle = lax.rem(self.z + 1, 4) > 1

    def ring(self, k):
        return lax.rem(self.c + k, 8)

    def source(self, k):
        return lax.rem(self.c + 8 - k, 8)

    def up(self, d):
        return lax.rem(self.z + d, 4)

    def down(self, d):
        return lax.rem(self.z + 4 - d, 4)


def knock(place):
    barrier = pltpu.get_barrier_semaphore()
    for k in range(1, 8):
        pl.semaphore_signal(barrier, inc=1, device_id=(place.ring(k), place.z), device_id_type=MESH)
    for d in range(1, 4):
        pl.semaphore_signal(barrier, inc=1, device_id=(place.c, place.up(d)), device_id_type=MESH)


def enter():
    pl.semaphore_wait(pltpu.get_barrier_semaphore(), 10)


def remote(src, dst, send_sem, recv_sem, device):
    return pltpu.make_async_remote_copy(
        src_ref=src, dst_ref=dst, send_sem=send_sem, recv_sem=recv_sem,
        device_id=device, device_id_type=MESH,
    )


def aligned(start, size, unit):
    return pl.ds(pl.multiple_of(start, unit), size)


neg_big = -1e30
norm_eps = 1e-05
root_half = 0.7071067811865476
inv_root_tau = 0.3989422804014327


def swapped(block, axis, stride):
    count = lax.axis_size(axis)
    route = []
    for low in range(count):
        high = low | 1 << stride
        if high != low and high < count:
            route += [(low, high), (high, low)]
    return lax.ppermute(block, axis, route)


def matmul(left, right):
    return jnp.dot(left, right, preferred_element_type=jnp.float32)


def matmul_left_t(left, right):
    return lax.dot_general(
        left, right, (((0,), (0,)), ((), ())), preferred_element_type=jnp.float32
    )


def matmul_right_t(left, right):
    return lax.dot_general(
        left, right, (((1,), (1,)), ((), ())), preferred_element_type=jnp.float32
    )


def gelu_value(hidden):
    return hidden * 0.5 * (1.0 + jax.scipy.special.erf(hidden * root_half))


def gelu_slope(hidden):
    return 0.5 * (
        1.0 + jax.scipy.special.erf(hidden * root_half)
    ) + hidden * inv_root_tau * jnp.exp(-0.5 * hidden * hidden)


def norm_forward(total, gain, shift):
    mean_val = jnp.mean(total, axis=-1, keepdims=True)
    centered = total - mean_val
    inv_std = lax.rsqrt(jnp.mean(centered * centered, axis=-1, keepdims=True) + norm_eps)
    normed = centered * inv_std
    return (normed * gain + shift, normed, inv_std)


def norm_backward(upstream, normed, inv_std, gain):
    scaled = upstream * gain
    first_mean = jnp.mean(scaled, axis=-1, keepdims=True)
    second_mean = jnp.mean(scaled * normed, axis=-1, keepdims=True)
    return inv_std * (scaled - first_mean - normed * second_mean)


def allowed_pairs(query_pos, query_start, key_pos):
    return (key_pos[None, :] <= query_pos[:, None]) & (key_pos[None, :] >= query_start[:, None])


def pair_needed(key_lo, query_lo, span):
    needed = key_lo <= query_lo + span - 1
    return needed


def half_firsts(device, seq_dev, cycle_size):
    half = seq_dev // 2
    first = device * seq_dev
    second = (cycle_size - 1 - device) * seq_dev + half
    return (first, second)


def mirror_inputs(members, cycle_size):
    moved = members
    for bit in range(cycle_size.bit_length() - 1):
        moved = swapped((moved[0], moved[1], moved[2], moved[3]), "ctx", bit)
    return moved


def mirror_outputs(members, cycle_size):
    moved = members
    for bit in range(cycle_size.bit_length() - 1):
        moved = swapped((moved[0], moved[1], moved[2]), "ctx", bit)
    return moved


def block_scores(query_three, key_three, allowed, scale_factor):
    scores = (
        jnp.einsum("qhd,khd->hqk", query_three, key_three, preferred_element_type=jnp.float32)
        * scale_factor
    )
    return jnp.where(allowed[None], scores, neg_big)


def forward_update(state_mb, query_three, key_three, value_three, allowed, scale_factor):
    run_max, run_sum, run_acc = state_mb
    scores = block_scores(query_three, key_three, allowed, scale_factor)
    new_max = jnp.maximum(run_max, jnp.max(scores, axis=-1))
    rescale = jnp.exp(run_max - new_max)
    weights = jnp.where(allowed[None], jnp.exp(scores - new_max[:, :, None]), 0.0)
    new_sum = run_sum * rescale + jnp.sum(weights, axis=-1)
    mixed_sum = jnp.einsum(
        "hqk,khd->qhd",
        weights.astype(jnp.bfloat16),
        value_three,
        preferred_element_type=jnp.float32,
    )
    new_acc = run_acc * jnp.transpose(rescale)[:, :, None] + mixed_sum
    return (new_max, new_sum, new_acc)


def pair_grads(
    query_three, dout_three, key_three, value_three, allowed, log_total, row_delta, scale_factor
):
    scores = block_scores(query_three, key_three, allowed, scale_factor)
    prob_table = jnp.where(allowed[None], jnp.exp(scores - log_total[:, :, None]), 0.0)
    dprobs = jnp.einsum("qhd,khd->hqk", dout_three, value_three, preferred_element_type=jnp.float32)
    score_grad = (prob_table * (dprobs - row_delta[:, :, None])).astype(jnp.bfloat16)
    return (prob_table, score_grad)


def fold_blocks(pieces, state_all, update, base_rows):
    rows_in = pieces[0].shape[1]
    step_rows = min(rows_in, base_rows)

    def one_step(block_index, state_inner):
        offset = block_index * step_rows
        sliced = tuple(
            (lax.dynamic_slice_in_dim(member, offset, step_rows, 1) for member in pieces)
        )
        return update(state_inner, sliced, offset)

    return lax.fori_loop(0, rows_in // step_rows, one_step, state_all)


def shards(
    x_stream,
    y_stream,
    grad_x,
    grad_y,
    doc_start,
    query_weight,
    query_bias,
    key_weight,
    value_weight,
    value_bias,
    output_weight,
    output_bias,
    first_gain,
    first_shift,
    hidden_weight,
    hidden_bias,
    reduce_weight,
    reduce_bias,
    second_gain,
    second_shift,
):
    gathered = (
        lax.all_gather(query_weight, "fsdp", axis=0, tiled=True),
        lax.all_gather(query_bias, "fsdp", axis=0, tiled=True),
        lax.all_gather(key_weight, "fsdp", axis=0, tiled=True),
        lax.all_gather(value_weight, "fsdp", axis=0, tiled=True),
        lax.all_gather(value_bias, "fsdp", axis=0, tiled=True),
        lax.all_gather(output_weight, "fsdp", axis=0, tiled=True),
        lax.all_gather(output_bias, "fsdp", axis=0, tiled=True),
        lax.all_gather(first_gain, "fsdp", axis=0, tiled=True),
        lax.all_gather(first_shift, "fsdp", axis=0, tiled=True),
        lax.all_gather(hidden_weight, "fsdp", axis=0, tiled=True),
        lax.all_gather(hidden_bias, "fsdp", axis=0, tiled=True),
        lax.all_gather(reduce_weight, "fsdp", axis=0, tiled=True),
        lax.all_gather(reduce_bias, "fsdp", axis=0, tiled=True),
        lax.all_gather(second_gain, "fsdp", axis=0, tiled=True),
        lax.all_gather(second_shift, "fsdp", axis=0, tiled=True),
    )
    (
        w_query,
        b_query,
        w_key,
        w_value,
        b_value,
        w_output,
        b_output,
        gain_one,
        shift_one,
        w_hidden,
        b_hidden,
        w_reduce,
        b_reduce,
        gain_two,
        shift_two,
    ) = gathered
    b_query = b_query.astype(jnp.float32)
    b_value = b_value.astype(jnp.float32)
    b_output = b_output.astype(jnp.float32)
    gain_one = gain_one.astype(jnp.float32)
    shift_one = shift_one.astype(jnp.float32)
    b_hidden = b_hidden.astype(jnp.float32)
    b_reduce = b_reduce.astype(jnp.float32)
    gain_two = gain_two.astype(jnp.float32)
    shift_two = shift_two.astype(jnp.float32)
    micro_count, seq_dev, model_width = (x_stream.shape[1], x_stream.shape[2], x_stream.shape[3])
    half = seq_dev // 2
    head_count = HEADS
    head_dim = model_width // head_count
    scale_factor = 1.0 / math.sqrt(head_dim)
    token_rows = micro_count * seq_dev
    cycle_size = lax.axis_size("ctx")
    my_index = lax.axis_index("ctx")
    half_range = jnp.arange(half, dtype=jnp.int32)
    own_firsts = half_firsts(my_index, seq_dev, cycle_size)
    own_pos = [own_firsts[0] + half_range, own_firsts[1] + half_range]
    positions_own = jnp.concatenate(own_pos)
    doc_all = doc_start[0]
    starts_own = jnp.take(doc_all, positions_own, axis=1)
    own_starts = [
        [starts_own[micro_index, part * half : (part + 1) * half] for part in range(2)]
        for micro_index in range(micro_count)
    ]
    x_mb, y_mb, gx_mb, gy_mb = (x_stream[0], y_stream[0], grad_x[0], grad_y[0])
    moved = mirror_inputs(
        (x_mb[:, half:], y_mb[:, half:], gx_mb[:, half:], gy_mb[:, half:]), cycle_size
    )
    x_mb = jnp.concatenate([x_mb[:, :half], moved[0]], axis=1)
    y_mb = jnp.concatenate([y_mb[:, :half], moved[1]], axis=1)
    gx_mb = jnp.concatenate([gx_mb[:, :half], moved[2]], axis=1)
    gy_mb = jnp.concatenate([gy_mb[:, :half], moved[3]], axis=1)
    x_rows = x_mb.reshape(token_rows, model_width)
    y_rows = y_mb.reshape(token_rows, model_width)
    gx_rows = gx_mb.reshape(token_rows, model_width)
    gy_rows = gy_mb.reshape(token_rows, model_width)
    x_low = x_rows.astype(jnp.bfloat16)
    query_low = (matmul(x_low, w_query) + b_query).astype(jnp.bfloat16)
    key_low = matmul(x_low, w_key).astype(jnp.bfloat16)
    value_low = (matmul(x_low, w_value) + b_value).astype(jnp.bfloat16)
    query_mb = query_low.reshape(micro_count, seq_dev, model_width)
    key_mb = key_low.reshape(micro_count, seq_dev, model_width)
    value_mb = value_low.reshape(micro_count, seq_dev, model_width)
    query_three = [
        query_mb[micro_index].reshape(seq_dev, head_count, head_dim)
        for micro_index in range(micro_count)
    ]
    key_own = [
        key_mb[micro_index].reshape(seq_dev, head_count, head_dim)
        for micro_index in range(micro_count)
    ]
    value_own = [
        value_mb[micro_index].reshape(seq_dev, head_count, head_dim)
        for micro_index in range(micro_count)
    ]

    def forward_step(state_inner, sliced, key_first):
        key_block, value_block = sliced
        source = key_first // seq_dev
        key_firsts = half_firsts(source, seq_dev, cycle_size)
        updated = []
        for micro_index in range(micro_count):
            key_three = key_block[micro_index].reshape(seq_dev, head_count, head_dim)
            value_three = value_block[micro_index].reshape(seq_dev, head_count, head_dim)
            states = list(state_inner[micro_index])
            for query_part in range(2):
                query_piece = query_three[micro_index][query_part * half : (query_part + 1) * half]
                for key_part in range(2):
                    key_piece = key_three[key_part * half : (key_part + 1) * half]
                    value_piece = value_three[key_part * half : (key_part + 1) * half]
                    allowed = allowed_pairs(
                        own_pos[query_part],
                        own_starts[micro_index][query_part],
                        key_firsts[key_part] + half_range,
                    )
                    needed = pair_needed(key_firsts[key_part], own_firsts[query_part], half)

                    def forward_compute(state_mb):
                        return forward_update(
                            state_mb, query_piece, key_piece, value_piece, allowed, scale_factor
                        )

                    def forward_unchanged(state_mb):
                        return state_mb

                    states[query_part] = lax.cond(
                        needed, forward_compute, forward_unchanged, states[query_part]
                    )
            updated.append(tuple(states))
        return tuple(updated)

    def empty_state():
        return (
            jnp.full((head_count, half), neg_big, jnp.float32),
            jnp.zeros((head_count, half), jnp.float32),
            jnp.zeros((half, head_count, head_dim), jnp.float32),
        )

    forward_init = tuple(((empty_state(), empty_state()) for micro_index in range(micro_count)))
    attend_state = fold_blocks(
        (
            lax.all_gather(key_mb, "ctx", axis=1, tiled=True),
            lax.all_gather(value_mb, "ctx", axis=1, tiled=True),
        ),
        forward_init,
        forward_step,
        seq_dev,
    )
    out_parts = []
    log_parts = []
    for micro_index in range(micro_count):
        out_halves = []
        log_halves = []
        for query_part in range(2):
            run_max, run_sum, run_acc = attend_state[micro_index][query_part]
            out_halves.append(run_acc / jnp.transpose(run_sum)[:, :, None])
            log_halves.append(run_max + jnp.log(run_sum))
        out_parts.append(jnp.concatenate(out_halves, axis=0))
        log_parts.append(jnp.concatenate(log_halves, axis=1))
    out_raw = jnp.stack(out_parts)
    log_total_all = jnp.stack(log_parts)
    out_low = out_raw.reshape(token_rows, model_width).astype(jnp.bfloat16)
    branch = matmul(out_low, w_output) + b_output
    x_first, normed_one, inv_one = norm_forward(x_rows + branch, gain_one, shift_one)
    y_first = y_rows + branch
    x_first_low = x_first.astype(jnp.bfloat16)
    hidden_pre = matmul(x_first_low, w_hidden) + b_hidden
    hidden_low = gelu_value(hidden_pre).astype(jnp.bfloat16)
    second = matmul(hidden_low, w_reduce) + b_reduce
    x_next, normed_two, inv_two = norm_forward(x_first + second, gain_two, shift_two)
    y_next = y_first + second
    total_two_grad = norm_backward(gx_rows, normed_two, inv_two, gain_two)
    second_gain_grad = jnp.sum(gx_rows * normed_two, axis=0)
    second_shift_grad = jnp.sum(gx_rows, axis=0)
    second_grad = (total_two_grad + gy_rows).astype(jnp.bfloat16)
    reduce_weight_grad = matmul_left_t(hidden_low, second_grad)
    reduce_bias_grad = jnp.sum(second_grad.astype(jnp.float32), axis=0)
    hidden_grad = (matmul_right_t(second_grad, w_reduce) * gelu_slope(hidden_pre)).astype(
        jnp.bfloat16
    )
    hidden_weight_grad = matmul_left_t(x_first_low, hidden_grad)
    hidden_bias_grad = jnp.sum(hidden_grad.astype(jnp.float32), axis=0)
    first_up = total_two_grad + matmul_right_t(hidden_grad, w_hidden)
    total_one_grad = norm_backward(first_up, normed_one, inv_one, gain_one)
    first_gain_grad = jnp.sum(first_up * normed_one, axis=0)
    first_shift_grad = jnp.sum(first_up, axis=0)
    branch_grad = (total_one_grad + gy_rows).astype(jnp.bfloat16)
    output_weight_grad = matmul_left_t(out_low, branch_grad)
    output_bias_grad = jnp.sum(branch_grad.astype(jnp.float32), axis=0)
    dout_low = matmul_right_t(branch_grad, w_output).astype(jnp.bfloat16)
    dout_mb = dout_low.reshape(micro_count, seq_dev, head_count, head_dim)
    delta_all = jnp.einsum("bqhd,bqhd->bhq", dout_mb.astype(jnp.float32), out_raw)
    dout_three = [dout_mb[micro_index] for micro_index in range(micro_count)]
    dout_rows = dout_low.reshape(micro_count, seq_dev, model_width)

    def zero_query():
        return jnp.zeros((half, head_count, head_dim), jnp.float32)

    query_init = tuple(((zero_query(), zero_query()) for micro_index in range(micro_count)))

    def query_step(state_inner, sliced, key_first):
        key_block, value_block = sliced
        source = key_first // seq_dev
        key_firsts = half_firsts(source, seq_dev, cycle_size)
        updated = []
        for micro_index in range(micro_count):
            key_three = key_block[micro_index].reshape(seq_dev, head_count, head_dim)
            value_three = value_block[micro_index].reshape(seq_dev, head_count, head_dim)
            query_accs = list(state_inner[micro_index])
            for query_part in range(2):
                rows = slice(query_part * half, (query_part + 1) * half)
                query_piece = query_three[micro_index][rows]
                dout_piece = dout_three[micro_index][rows]
                log_piece = log_total_all[micro_index][:, rows]
                delta_piece = delta_all[micro_index][:, rows]
                for key_part in range(2):
                    key_piece = key_three[key_part * half : (key_part + 1) * half]
                    value_piece = value_three[key_part * half : (key_part + 1) * half]
                    allowed = allowed_pairs(
                        own_pos[query_part],
                        own_starts[micro_index][query_part],
                        key_firsts[key_part] + half_range,
                    )
                    needed = pair_needed(key_firsts[key_part], own_firsts[query_part], half)

                    def query_compute(query_acc):
                        prob_table, score_grad = pair_grads(
                            query_piece,
                            dout_piece,
                            key_piece,
                            value_piece,
                            allowed,
                            log_piece,
                            delta_piece,
                            scale_factor,
                        )
                        return (
                            query_acc
                            + jnp.einsum(
                                "hqk,khd->qhd",
                                score_grad,
                                key_piece,
                                preferred_element_type=jnp.float32,
                            )
                            * scale_factor
                        )

                    def query_unchanged(query_acc):
                        return query_acc

                    query_accs[query_part] = lax.cond(
                        needed, query_compute, query_unchanged, query_accs[query_part]
                    )
            updated.append(tuple(query_accs))
        return tuple(updated)

    query_parts = fold_blocks(
        (
            lax.all_gather(key_mb, "ctx", axis=1, tiled=True),
            lax.all_gather(value_mb, "ctx", axis=1, tiled=True),
        ),
        query_init,
        query_step,
        seq_dev,
    )
    stats_all = (
        lax.all_gather(log_total_all, "ctx", axis=2, tiled=True),
        lax.all_gather(delta_all, "ctx", axis=2, tiled=True),
    )

    def key_step(state_inner, sliced, query_begin):
        query_block, dout_block = sliced
        source = query_begin // seq_dev
        query_firsts = half_firsts(source, seq_dev, cycle_size)
        updated = []
        for micro_index in range(micro_count):
            log_block = lax.dynamic_slice_in_dim(stats_all[0][micro_index], query_begin, seq_dev, 1)
            delta_block = lax.dynamic_slice_in_dim(
                stats_all[1][micro_index], query_begin, seq_dev, 1
            )
            query_whole = query_block[micro_index].reshape(seq_dev, head_count, head_dim)
            dout_whole = dout_block[micro_index].reshape(seq_dev, head_count, head_dim)
            key_accs = [
                state_inner[micro_index][0][part * half : (part + 1) * half] for part in range(2)
            ]
            value_accs = [
                state_inner[micro_index][1][part * half : (part + 1) * half] for part in range(2)
            ]
            for query_part in range(2):
                rows = slice(query_part * half, (query_part + 1) * half)
                query_pos = query_firsts[query_part] + half_range
                starts_block = jnp.take(doc_all[micro_index], query_pos)
                query_piece = query_whole[rows]
                dout_piece = dout_whole[rows]
                log_piece = log_block[:, rows]
                delta_piece = delta_block[:, rows]
                for key_part in range(2):
                    key_piece = key_own[micro_index][key_part * half : (key_part + 1) * half]
                    value_piece = value_own[micro_index][key_part * half : (key_part + 1) * half]
                    allowed = allowed_pairs(query_pos, starts_block, own_pos[key_part])
                    needed = pair_needed(own_firsts[key_part], query_firsts[query_part], half)

                    def key_compute(operands):
                        key_acc, value_acc = operands
                        prob_table, score_grad = pair_grads(
                            query_piece,
                            dout_piece,
                            key_piece,
                            value_piece,
                            allowed,
                            log_piece,
                            delta_piece,
                            scale_factor,
                        )
                        key_add = (
                            jnp.einsum(
                                "hqk,qhd->khd",
                                score_grad,
                                query_piece,
                                preferred_element_type=jnp.float32,
                            )
                            * scale_factor
                        )
                        value_add = jnp.einsum(
                            "hqk,qhd->khd",
                            prob_table.astype(jnp.bfloat16),
                            dout_piece,
                            preferred_element_type=jnp.float32,
                        )
                        return (
                            key_acc + key_add.reshape(half, model_width),
                            value_acc + value_add.reshape(half, model_width),
                        )

                    def key_unchanged(operands):
                        return operands

                    result = lax.cond(
                        needed,
                        key_compute,
                        key_unchanged,
                        (key_accs[key_part], value_accs[key_part]),
                    )
                    key_accs[key_part] = result[0]
                    value_accs[key_part] = result[1]
            updated.append((jnp.concatenate(key_accs, axis=0), jnp.concatenate(value_accs, axis=0)))
        return tuple(updated)

    key_init = tuple(
        (
            (
                jnp.zeros((seq_dev, model_width), jnp.float32),
                jnp.zeros((seq_dev, model_width), jnp.float32),
            )
            for micro_index in range(micro_count)
        )
    )
    key_state = fold_blocks(
        (
            lax.all_gather(query_mb, "ctx", axis=1, tiled=True),
            lax.all_gather(dout_rows, "ctx", axis=1, tiled=True),
        ),
        key_init,
        key_step,
        seq_dev,
    )
    key_grad_sum = jnp.stack([key_state[micro_index][0] for micro_index in range(micro_count)])
    value_grad_sum = jnp.stack([key_state[micro_index][1] for micro_index in range(micro_count)])
    query_whole_parts = [
        jnp.concatenate([query_parts[micro_index][0], query_parts[micro_index][1]], axis=0)
        for micro_index in range(micro_count)
    ]
    query_grad_low = (
        jnp.stack(query_whole_parts).reshape(token_rows, model_width).astype(jnp.bfloat16)
    )
    key_grad_low = key_grad_sum.reshape(token_rows, model_width).astype(jnp.bfloat16)
    value_grad_low = value_grad_sum.reshape(token_rows, model_width).astype(jnp.bfloat16)
    query_weight_grad = matmul_left_t(x_low, query_grad_low)
    query_bias_grad = jnp.sum(query_grad_low.astype(jnp.float32), axis=0)
    key_weight_grad = matmul_left_t(x_low, key_grad_low)
    value_weight_grad = matmul_left_t(x_low, value_grad_low)
    value_bias_grad = jnp.sum(value_grad_low.astype(jnp.float32), axis=0)
    x_grad = (
        total_one_grad
        + matmul_right_t(query_grad_low, w_query)
        + matmul_right_t(key_grad_low, w_key)
        + matmul_right_t(value_grad_low, w_value)
    )
    shard_grads = (
        lax.psum_scatter(query_weight_grad, "fsdp", scatter_dimension=0, tiled=True),
        lax.psum_scatter(query_bias_grad, "fsdp", scatter_dimension=0, tiled=True),
        lax.psum_scatter(key_weight_grad, "fsdp", scatter_dimension=0, tiled=True),
        lax.psum_scatter(value_weight_grad, "fsdp", scatter_dimension=0, tiled=True),
        lax.psum_scatter(value_bias_grad, "fsdp", scatter_dimension=0, tiled=True),
        lax.psum_scatter(output_weight_grad, "fsdp", scatter_dimension=0, tiled=True),
        lax.psum_scatter(output_bias_grad, "fsdp", scatter_dimension=0, tiled=True),
        lax.psum_scatter(first_gain_grad, "fsdp", scatter_dimension=0, tiled=True),
        lax.psum_scatter(first_shift_grad, "fsdp", scatter_dimension=0, tiled=True),
        lax.psum_scatter(hidden_weight_grad, "fsdp", scatter_dimension=0, tiled=True),
        lax.psum_scatter(hidden_bias_grad, "fsdp", scatter_dimension=0, tiled=True),
        lax.psum_scatter(reduce_weight_grad, "fsdp", scatter_dimension=0, tiled=True),
        lax.psum_scatter(reduce_bias_grad, "fsdp", scatter_dimension=0, tiled=True),
        lax.psum_scatter(second_gain_grad, "fsdp", scatter_dimension=0, tiled=True),
        lax.psum_scatter(second_shift_grad, "fsdp", scatter_dimension=0, tiled=True),
    )
    summed = lax.psum(
        (
            shard_grads[0],
            shard_grads[1],
            shard_grads[2],
            shard_grads[3],
            shard_grads[4],
            shard_grads[5],
            shard_grads[6],
            shard_grads[7],
            shard_grads[8],
            shard_grads[9],
            shard_grads[10],
            shard_grads[11],
            shard_grads[12],
            shard_grads[13],
            shard_grads[14],
        ),
        "ctx",
    )
    mb_shape = (micro_count, seq_dev, model_width)
    x_next_mb = x_next.reshape(mb_shape)
    y_next_mb = y_next.reshape(mb_shape)
    x_grad_mb = x_grad.reshape(mb_shape)
    back = mirror_outputs(
        (x_next_mb[:, half:], y_next_mb[:, half:], x_grad_mb[:, half:]), cycle_size
    )
    x_next_mb = jnp.concatenate([x_next_mb[:, :half], back[0]], axis=1)
    y_next_mb = jnp.concatenate([y_next_mb[:, :half], back[1]], axis=1)
    x_grad_mb = jnp.concatenate([x_grad_mb[:, :half], back[2]], axis=1)
    out_shape = (1, micro_count, seq_dev, model_width)
    return (
        x_next_mb.reshape(out_shape),
        y_next_mb.reshape(out_shape),
        x_grad_mb.reshape(out_shape),
        summed[0],
        summed[1],
        summed[2],
        summed[3],
        summed[4],
        summed[5],
        summed[6],
        summed[7],
        summed[8],
        summed[9],
        summed[10],
        summed[11],
        summed[12],
        summed[13],
        summed[14],
    )


class Gather:
    def __init__(self, place, mine, at, sems, pair=None, side=None):
        self.place, self.mine, self.at, self.pair, self.side = place, mine, at, pair, side
        self.zs, self.zr, self.ps, self.pr, self.cs, self.cr = sems
        self.moved = []

    def held(self, zz, across=False, other=False):
        core = self.place.core
        core = 1 - core if other else core
        if self.pair is None:
            return self.at(zz, core)
        return self.at(zz, 2 * (1 - self.side if across else self.side) + core)

    def go(self, copy):
        copy.start()
        self.moved.append(copy)

    def start(self):
        place = self.place
        for d in (2, 1, 3):
            self.go(remote(self.mine, self.held(place.z), self.zs.at[d - 1], self.zr.at[d - 1], (place.c, place.up(d))))

    def arrive(self):
        place = self.place
        for d in (1, 3, 2):
            block = self.held(place.down(d))
            remote(block, block, self.zs.at[d - 1], self.zr.at[d - 1], (place.c, place.up(d))).wait_recv()
            if self.pair is not None:
                self.go(remote(block, block, self.ps.at[d - 1], self.pr.at[d - 1], (self.pair, place.z)))
            self.go(remote(block, block, self.cs.at[0, d - 1], self.cr.at[0, d - 1], (place.sibling, place.z)))

    def relay(self):
        place = self.place
        for d in (1, 3, 2):
            block = self.held(place.down(d), across=True)
            remote(block, block, self.ps.at[d - 1], self.pr.at[d - 1], (self.pair, place.z)).wait_recv()
            self.go(remote(block, block, self.cs.at[1, d - 1], self.cr.at[1, d - 1], (place.sibling, place.z)))

    def ready(self):
        place = self.place
        for d in (1, 3, 2):
            for across in (False, True)[:1 if self.pair is None else 2]:
                block = self.held(place.down(d), across=across, other=True)
                i = 1 if across else 0
                remote(block, block, self.cs.at[i, d - 1], self.cr.at[i, d - 1], (place.sibling, place.z)).wait_recv()

    def finish(self):
        for copy in self.moved:
            copy.wait_send()


class Reduction:
    def __init__(self, place, part, pair, comb, slots, total, plane, out, sems):
        self.place = place
        self.part, self.pair, self.comb, self.slots = part, pair, comb, slots
        self.total, self.plane, self.out = total, plane, out
        (self.pair_s, self.pair_r, self.col_s, self.col_r, self.comb_r, self.plane_s, self.plane_r,
         self.back_s, self.back_r, self.core_s, self.core_r) = sems
        self.sent = []
        self.chip = lax.div(place.c, 2)

    def peer(self, k):
        return (2 * lax.rem(self.chip + k, 4) + self.place.core, self.place.z)

    def go(self, copy):
        copy.start()
        self.sent.append(copy)

    def pair_start(self):
        place = self.place
        self.go(remote(self.part.at[1 - place.core], self.pair, self.pair_s.at[0], self.pair_r.at[0], (place.sibling, place.z)))

    def own(self, zz):
        return self.part.at[self.place.core, zz]

    def end_copy(self, i):
        place = self.place
        upper = lax.div(place.z, 3)
        near, far = 1 + upper, 2 - upper
        goal = (3 - place.z, near, far)[i]
        target = (self.comb, self.slots.at[0], self.slots.at[2])[i]
        arrival = (self.comb_r.at[0], self.col_r.at[0], self.col_r.at[2])[i]
        return remote(self.own(goal), target, self.col_s.at[i], arrival, (place.c, far if i == 2 else near))

    def middle_copy(self, i):
        place = self.place
        end = 3 * (place.z - 1)
        goal = (end, 3 - place.z, 3 - end)[i]
        return remote(self.own(goal), self.slots.at[i], self.col_s.at[i], self.col_r.at[i], (place.c, goal))

    def column_start(self):
        place = self.place
        core = place.core
        remote(self.pair, self.pair, self.pair_s.at[0], self.pair_r.at[0], (place.sibling, place.z)).wait_recv()

        def add(zz, carry):
            for chip in range(4):
                self.part[core, zz, chip] = (
                    self.part[core, zz, chip].astype(f32) + self.pair[zz, chip].astype(f32)
                ).astype(bf16)
            return carry

        lax.fori_loop(0, 4, add, 0)

        @pl.when(place.middle)
        def inner():
            self.middle_copy(0).start()
            self.middle_copy(1).start()

        @pl.when(jnp.logical_not(place.middle))
        def outer():
            for i in range(3):
                self.end_copy(i).start()

    def column_combine(self):
        place = self.place
        core = place.core

        @pl.when(place.middle)
        def inner():
            self.end_copy(0).wait_recv()
            goal = 3 - 3 * (place.z - 1)
            for chip in range(4):
                self.part[core, goal, chip] = (
                    self.part[core, goal, chip].astype(f32) + self.comb[chip].astype(f32)
                ).astype(bf16)
            self.middle_copy(2).start()

    def plane_start(self):
        place = self.place
        core, z = place.core, place.z
        self.end_copy(1).wait_recv()
        self.end_copy(2).wait_recv()

        @pl.when(place.middle)
        def inner():
            self.middle_copy(1).wait_recv()
            for chip in range(4):
                self.total[chip] = (
                    self.part[core, z, chip].astype(f32) + self.slots[0, chip].astype(f32)
                    + self.slots[1, chip].astype(f32) + self.slots[2, chip].astype(f32)
                ).astype(bf16)

        @pl.when(jnp.logical_not(place.middle))
        def outer():
            for chip in range(4):
                self.total[chip] = (
                    self.part[core, z, chip].astype(f32) + self.slots[0, chip].astype(f32)
                    + self.slots[2, chip].astype(f32)
                ).astype(bf16)

        for k in range(1, 4):
            self.go(remote(
                self.total.at[lax.rem(self.chip + k, 4)], self.plane.at[k - 1],
                self.plane_s.at[k - 1], self.plane_r.at[k - 1], self.peer(k),
            ))

    def back_start(self):
        place = self.place
        for k in range(1, 4):
            slot = self.plane.at[k - 1]
            remote(slot, slot, self.plane_s.at[k - 1], self.plane_r.at[k - 1], self.peer(k)).wait_recv()
        total = self.total[self.chip].astype(f32)
        for k in range(3):
            total = total + self.plane[k].astype(f32)
        self.out[place.c] = total.astype(bf16)
        mine = self.out.at[place.c]
        for k in range(1, 4):
            self.go(remote(mine, mine, self.back_s.at[k - 1], self.back_r.at[k - 1], self.peer(k)))
        self.go(remote(mine, mine, self.core_s.at[0], self.core_r.at[0], (place.sibling, place.z)))

    def relay(self):
        place = self.place
        for k in range(1, 4):
            slot = self.out.at[2 * lax.rem(self.chip + 4 - k, 4) + place.core]
            remote(slot, slot, self.back_s.at[k - 1], self.back_r.at[k - 1], self.peer(k)).wait_recv()
            self.go(remote(slot, slot, self.core_s.at[k], self.core_r.at[k], (place.sibling, place.z)))

    def finish(self):
        place = self.place
        for k in range(4):
            slot = self.out.at[2 * lax.rem(self.chip + 4 - k, 4) + 1 - place.core]
            remote(slot, slot, self.core_s.at[k], self.core_r.at[k], (place.sibling, place.z)).wait_recv()
        for copy in self.sent:
            copy.wait_send()

        @pl.when(place.middle)
        def inner():
            for i in range(3):
                self.middle_copy(i).wait_send()

        @pl.when(jnp.logical_not(place.middle))
        def outer():
            for i in range(3):
                self.end_copy(i).wait_send()


class Exchange:
    def __init__(self, place, pool, send, recv):
        self.place, self.pool, self.send, self.recv = place, pool, send, recv
        self.sent = []
        shift = place.sibling - place.c
        self.across = place.x_next + place.y_next - place.c
        self.from_sibling = (place.sibling, place.x_next + shift, place.y_next + shift, self.across + shift)

    def go(self, mb, i, j, owner, target, rows=None):
        block = self.pool.at[mb * 8 + owner]
        if rows is not None:
            block = block.at[rows]
        copy = remote(block, block, self.send.at[mb, i], self.recv.at[mb, j], (target, self.place.z))
        copy.start()
        self.sent.append(copy)

    def take(self, mb, j, owner, rows=None):
        block = self.pool.at[mb * 8 + owner]
        if rows is not None:
            block = block.at[rows]
        remote(block, block, self.send.at[mb, 0], self.recv.at[mb, j], (self.place.sibling, self.place.z)).wait_recv()

    def start(self, mb):
        place = self.place
        self.go(mb, 0, 0, place.c, place.x_next)
        self.go(mb, 1, 1, place.c, place.y_next)
        self.go(mb, 2, 4, place.c, place.sibling)

    def relay(self, mb):
        place = self.place
        half = self.pool.shape[1] // 2
        self.take(mb, 0, place.x_next)
        self.go(mb, 3, 2, place.x_next, place.y_next, pl.ds(0, half))
        self.take(mb, 1, place.y_next)
        self.go(mb, 4, 3, place.y_next, place.x_next, pl.ds(half, half))
        self.go(mb, 5, 5, place.x_next, place.sibling)
        self.go(mb, 6, 6, place.y_next, place.sibling)

    def last(self, mb):
        half = self.pool.shape[1] // 2
        self.take(mb, 2, self.across, pl.ds(0, half))
        self.take(mb, 3, self.across, pl.ds(half, half))
        self.go(mb, 7, 7, self.across, self.place.sibling)

    def ready(self, mb):
        for k, owner in enumerate(self.from_sibling):
            self.take(mb, 4 + k, owner)

    def finish(self):
        for copy in self.sent:
            copy.wait_send()


class ColumnSum:
    def __init__(self, place, part, column, out, sems):
        self.place, self.part, self.column, self.out = place, part, column, out
        self.col_s, self.col_r, self.back_s, self.back_r, self.core_s, self.core_r = sems
        self.sent = []
        self.chip = lax.div(place.c, 2)

    def peer(self, k):
        return (2 * lax.rem(self.chip + k, 4) + self.place.core, self.place.z)

    def go(self, copy):
        copy.start()
        self.sent.append(copy)

    def column_copy(self, d):
        place = self.place
        return remote(
            self.part.at[place.up(d)], self.column.at[d - 1], self.col_s.at[d - 1], self.col_r.at[d - 1],
            (place.c, place.up(d)),
        )

    def column_start(self):
        for d in (2, 1, 3):
            self.go(self.column_copy(d))

    def back_start(self):
        place = self.place
        for d in (1, 3, 2):
            self.column_copy(d).wait_recv()
        total = self.part[place.z].astype(f32)
        for d in range(3):
            total = total + self.column[d].astype(f32)
        self.out[place.c] = total.astype(bf16)
        mine = self.out.at[place.c]
        for k in range(1, 4):
            self.go(remote(mine, mine, self.back_s.at[k - 1], self.back_r.at[k - 1], self.peer(k)))
        self.go(remote(mine, mine, self.core_s.at[0], self.core_r.at[0], (place.sibling, place.z)))

    def relay(self):
        place = self.place
        for k in range(1, 4):
            slot = self.out.at[2 * lax.rem(self.chip + 4 - k, 4) + place.core]
            remote(slot, slot, self.back_s.at[k - 1], self.back_r.at[k - 1], self.peer(k)).wait_recv()
            self.go(remote(slot, slot, self.core_s.at[k], self.core_r.at[k], (place.sibling, place.z)))

    def finish(self):
        place = self.place
        for k in range(4):
            slot = self.out.at[2 * lax.rem(self.chip + 4 - k, 4) + 1 - place.core]
            remote(slot, slot, self.core_s.at[k], self.core_r.at[k], (place.sibling, place.z)).wait_recv()
        for copy in self.sent:
            copy.wait_send()


def layer_kernel(
    starts_ref, wq_ref, wk_ref, wv_ref, qb_ref, vb_ref, ob_ref, fg_ref, fs_ref, rb_ref, sg_ref, ss_ref, hb_ref, x_hbm, y_hbm, gx_hbm, gy_hbm, wo_hbm, wh_hbm, wr_hbm,
    xn_hbm, yn_hbm, xg_hbm, keep_hbm, red_out, hid_out, thin_out, vec_out,
    x_buf, y_buf, gx_buf, gy_buf, wt, wo, wh, wr, vecs, bias_cols, head_w, made, qkv, rows_a, rows_b,
    head, mixed, log_total, pool, first_low, second_grad, branch_grad, slope, dstage, dhead, two_grad, inv_one,
    dq_turned, delta, got,
    red_part, red_pair, red_comb, red_slots, red_total, red_plane,
    wide_part, wide_pair, wide_comb, wide_slots, wide_total, wide_plane,
    thin_total, thin_part, thin_column,
    vec_part, vec_column, vec_plane, sums,
    load_sems, store_sems, own_sems, keep_sems, vz_s, vz_r, ex_s, ex_r, hw_s, hw_r,
    gz_s, gz_r, gp_s, gp_r, gc_s, gc_r,
    o_s, o_r, d_s, d_r, kv_s, kv_r,
    pair_s, pair_r, col_s, col_r, comb_r, plane_s, plane_r, back_s, back_r, core_s, core_r,
    vc_s, vc_r, vp_s, vp_r,
):
    place = Place()
    c, z, core = place.c, place.z, place.core
    mbs, seq, width = x_buf.shape
    hidden = wh.shape[1]
    feat = width // HEADS
    shard = width // 4
    sends = []

    def go(copy):
        copy.start()
        sends.append(copy)

    loads = [
        [pltpu.make_async_copy(src.at[mb], dst.at[mb], load_sems.at[i, mb]) for mb in range(mbs)]
        for i, (src, dst) in enumerate(((x_hbm, x_buf), (y_hbm, y_buf), (gx_hbm, gx_buf), (gy_hbm, gy_buf)))
    ]
    knock(place)
    for copy in loads[0]:
        copy.start()
    own_column = aligned(z * shard, shard, 128)
    for m, w_ref in enumerate((wq_ref, wk_ref, wv_ref)):
        wt[m, :, :, own_column] = turned(w_ref[...]).reshape(8, feat, shard)
    head_w[:, :, own_column] = wt[:, c, :, own_column]
    shorts = [ref[...].reshape(1, shard) for ref in (qb_ref, vb_ref, ob_ref, fg_ref, fs_ref, rb_ref, sg_ref, ss_ref)]
    shorts += [hb_ref[r * 128:(r + 1) * 128].reshape(1, 128) for r in range(4)]
    for row, short in enumerate(shorts):
        vecs[z, row:row + 1, :] = short.astype(f32)
    vecs[z, 12:16, :] = jnp.zeros((4, 128), f32)
    for copy in loads[0]:
        copy.wait()
    for mb in range(mbs):
        pool[mb * 8 + c] = x_buf[mb].astype(bf16)
    enter()

    exchange = Exchange(place, pool, ex_s, ex_r)

    def head_copy(d):
        return remote(
            wt.at[:, c, :, own_column], head_w.at[:, :, own_column], hw_s.at[d - 1], hw_r.at[d - 1], (c, place.up(d))
        )

    exchange.start(0)
    for d in (2, 1, 3):
        go(head_copy(d))
    for d in (2, 1, 3):
        go(remote(vecs.at[z], vecs.at[z], vz_s.at[d - 1], vz_r.at[d - 1], (c, place.up(d))))
    exchange.start(1)

    def sems_of(i):
        return tuple(sem.at[i] for sem in (gz_s, gz_r, gp_s, gp_r, gc_s, gc_r))

    def turned_at(zz, part):
        return wt.at[:, pl.ds(part * 4, 4), :, aligned(zz * shard, shard, 128)]

    def rows_at(full, count, begin, rows):
        def at(zz, part):
            return full.at[aligned(zz * count + begin + part * rows, rows, 16)]
        return at

    along_x, along_y, alone = (place.x_next, place.x), (place.y_next, place.y), (None, 0)
    gathers = []
    owned = []
    plans = ((wo_hbm, wo, (along_x,)), (wh_hbm, wh, (along_x, along_y)), (wr_hbm, wr, (along_x, along_y)))
    for i, (src, full, chunks) in enumerate(plans):
        count = src.shape[0]
        for chunk, (pair, side) in enumerate(chunks):
            rows = count // len(chunks) // 4
            begin = chunk * (count // len(chunks))
            mine = src.at[aligned(begin + (2 * side + core) * rows, rows, 16)]
            gathers.append(Gather(place, mine, rows_at(full, count, begin, rows), sems_of(len(gathers)), pair, side))
        owned.append(pltpu.make_async_copy(src, full.at[aligned(z * count, count, 16)], own_sems.at[i]))
    gathers.append(Gather(place, turned_at(z, core), turned_at, sems_of(5)))
    g_out, g_in_a, g_in_b, g_red_a, g_red_b, g_proj = gathers
    for gather in gathers:
        gather.start()
    for copy in owned:
        copy.start()
    for group in loads[1:]:
        for copy in group:
            copy.start()
    exchange.relay(0)
    exchange.start(2)
    for d in (1, 3, 2):
        slot = vecs.at[place.down(d)]
        remote(slot, slot, vz_s.at[d - 1], vz_r.at[d - 1], (c, place.up(d))).wait_recv()
        head_copy(d).wait_recv()

    def vec(row):
        return jnp.concatenate([vecs[zz, row:row + 1, :] for zz in range(4)], axis=1)

    for i in range(2):
        bias_cols[i] = jnp.transpose(vec(i))
    q_bias, v_bias = [bias_cols[i, aligned(c * feat, feat, 8), :] for i in range(2)]
    exchange.last(0)
    exchange.relay(1)
    g_out.arrive()
    keeps = [pltpu.make_async_copy(pool.at[i], keep_hbm.at[i], keep_sems.at[i]) for i in range(mbs * 8)]
    backs = [pltpu.make_async_copy(keep_hbm.at[i], pool.at[i], keep_sems.at[i]) for i in range(mbs * 8)]

    def project(mb):
        for j in range(8):
            out = dots(head_w[...].reshape(3 * feat, width), pool[mb * 8 + j], 1, 1)
            query = (out[0:feat] + q_bias).astype(bf16).astype(f32) * 0.125
            qkv[0, mb, j] = query.astype(bf16)
            qkv[1, mb, j] = out[feat:2 * feat].astype(bf16)
            qkv[2, mb, j] = (out[2 * feat:] + v_bias).astype(bf16)

    forward_hooks = {
        (0, 0): [g_in_a.arrive],
        (0, 3): [lambda: exchange.last(1)],
        (0, 6): [lambda: exchange.relay(2), g_out.relay],
        (0, 7): [g_in_b.arrive],
        (1, 3): [lambda: exchange.last(2)],
        (1, 7): [g_in_a.relay],
        (2, 2): [g_red_a.arrive],
        (2, 4): [g_in_b.relay],
        (2, 6): [g_red_b.arrive],
    }
    def block_scores_of(mb, i):
        begin, span = i * seq, (i + 1) * seq
        scores = jnp.dot(rows_a[0:span, :], qkv[0, mb, i], preferred_element_type=f32)
        key_pos = lax.broadcasted_iota(jnp.int32, (span, 1), 0)
        query_pos = lax.broadcasted_iota(jnp.int32, (1, seq), 1) + begin
        allowed = (key_pos >= starts_ref[mb, :, begin:span]) & (key_pos <= query_pos)
        scores = jnp.where(allowed, scores, NEG)
        return scores, jnp.max(scores, axis=0, keepdims=True)

    def attend_block(mb, i, scores, top):
        weights = jnp.exp(scores - top)
        total = jnp.sum(weights, axis=0, keepdims=True)
        values = jnp.concatenate([qkv[2, mb, j] for j in range(i + 1)], axis=1)
        out = jnp.dot(values, weights.astype(bf16), preferred_element_type=f32)
        head[mb, i] = (out / total).astype(bf16)
        log_total[mb, :, i * seq:(i + 1) * seq] = top + jnp.log(total)
        for hook in forward_hooks.get((mb, i), []):
            hook()

    for mb in range(mbs):
        exchange.ready(mb)
        project(mb)
        for copy in keeps[mb * 8:mb * 8 + 8]:
            copy.start()
        for j in range(8):
            rows_a[j * seq:(j + 1) * seq, :] = turned(qkv[1, mb, j])
        waiting = None
        for i in range(8):
            current = (i,) + block_scores_of(mb, i)
            if waiting is not None:
                attend_block(mb, *waiting)
            waiting = current
        attend_block(mb, *waiting)
        mixed[mb, c] = head[mb, c]
        for k in range(1, 8):
            go(remote(
                head.at[mb, place.ring(k)], mixed.at[mb, c], o_s.at[mb, k - 1], o_r.at[mb, k - 1], (place.ring(k), z)
            ))

    exchange.finish()
    for copy in owned + keeps:
        copy.wait()
    for group in loads[1:]:
        for copy in group:
            copy.wait()
    b_output, gain_one, shift_one, b_reduce, gain_two, shift_two = [vec(row) for row in range(2, 8)]
    b_hidden = jnp.concatenate([vecs[zz, 8 + r:9 + r, :] for zz in range(4) for r in range(4)], axis=1)
    sums[...] = jnp.zeros_like(sums)

    def add_row(row, block):
        sums[row:row + 1, :] += jnp.sum(block, axis=0, keepdims=True)

    def reduction(i, part, pair, comb, slots, total, plane, out):
        return Reduction(place, part, pair, comb, slots, total, plane, out, tuple(
            s.at[i] for s in (pair_s, pair_r, col_s, col_r, comb_r, plane_s, plane_r, back_s, back_r, core_s, core_r)
        ))

    red = reduction(0, red_part, red_pair, red_comb, red_slots, red_total, red_plane, red_out)
    wide = reduction(1, wide_part, wide_pair, wide_comb, wide_slots, wide_total, wide_plane, hid_out)
    thin = ColumnSum(
        place, thin_part, thin_column, thin_out,
        tuple(s.at[2] for s in (col_s, col_r, back_s, back_r, core_s, core_r)),
    )
    quarter = hidden // 4
    quarters = [slice(q * quarter, (q + 1) * quarter) for q in range(4)]
    spans = [slice(mb * seq, (mb + 1) * seq) for mb in range(mbs)]
    stores = []

    def store(src, dst, i, mb):
        copy = pltpu.make_async_copy(src.at[mb], dst.at[mb], store_sems.at[i, mb])
        copy.start()
        stores.append(copy)

    def dense_in(mb):
        rows = spans[mb]
        for k in range(1, 8):
            slot = mixed.at[mb, place.source(k)]
            remote(slot, slot, o_s.at[mb, k - 1], o_r.at[mb, k - 1], (place.ring(k), z)).wait_recv()
        branch = dots(mixed[mb].reshape(width, seq), wo[...], 0, 0) + b_output
        value = x_buf[mb]
        x_first, normed, inv_std = norm_forward(value + branch, gain_one, shift_one)
        x_buf[mb] = normed
        inv_one[mb] = inv_std
        y_buf[mb] = y_buf[mb] + branch
        first_low[rows, :] = x_first.astype(bf16)
        for q, cols in enumerate(quarters):
            pre = jnp.dot(first_low[rows, :], wh[:, cols], preferred_element_type=f32) + b_hidden[:, cols]
            phi = 0.5 * (1.0 + lax.erf(pre * root_half))
            pool[q * mbs + mb] = (pre * phi).astype(bf16)
            slope[rows, cols] = phi + pre * inv_root_tau * jnp.exp(-0.5 * pre * pre)

    def dense_out(mb):
        rows = spans[mb]
        hid = jnp.concatenate([pool[q * mbs + mb] for q in range(4)], axis=1)
        second = jnp.dot(hid, wr[...], preferred_element_type=f32) + b_reduce
        x_next, normed, inv_std = norm_forward(x_buf[mb] * gain_one + shift_one + second, gain_two, shift_two)
        y_buf[mb] = y_buf[mb] + second
        store(y_buf, yn_hbm, 1, mb)
        upstream = gx_buf[mb]
        up = norm_backward(upstream, normed, inv_std, gain_two)
        two_grad[mb] = up
        add_row(4, upstream * normed)
        add_row(5, upstream)
        gx_buf[mb] = x_next
        store(gx_buf, xn_hbm, 0, mb)
        second_low = (up + gy_buf[mb]).astype(bf16)
        second_grad[rows, :] = second_low
        add_row(3, second_low.astype(f32))

    def dense_back(mb):
        rows = spans[mb]
        for q, cols in enumerate(quarters):
            low = (dots(second_grad[rows, :], wr[cols, :], 1, 1) * slope[rows, cols]).astype(bf16)
            pool[(4 + q) * mbs + mb] = low
            add_row(6 + q, low.astype(f32))
        hid_grad = jnp.concatenate([pool[(4 + q) * mbs + mb] for q in range(4)], axis=1)
        first_up = two_grad[mb] + dots(hid_grad, wh[...], 1, 1)
        one_grad = norm_backward(first_up, x_buf[mb], inv_one[mb], gain_one)
        add_row(1, first_up * x_buf[mb])
        add_row(2, first_up)
        branch_low = (one_grad + gy_buf[mb]).astype(bf16)
        gy_buf[mb] = one_grad
        branch_grad[rows, :] = branch_low
        add_row(0, branch_low.astype(f32))
        dstage[mb] = dots(wo[...], branch_low, 1, 1).astype(bf16).reshape(8, feat, seq)
        dhead[mb, c] = dstage[mb, c]
        for k in range(1, 8):
            go(remote(
                dstage.at[mb, place.ring(k)], dhead.at[mb, c], d_s.at[mb, k - 1], d_r.at[mb, k - 1], (place.ring(k), z)
            ))

    g_out.ready()
    g_in_a.ready()
    g_in_b.ready()
    for mb in range(mbs):
        dense_in(mb)
        if mb == 0:
            g_red_a.relay()
        if mb == 1:
            g_red_b.relay()
    g_red_a.ready()
    g_red_b.ready()
    for mb in range(mbs):
        dense_out(mb)
    second_all = turned(second_grad[...])
    for q, cols in enumerate(quarters):
        hid = pool[q * mbs:(q + 1) * mbs].reshape(mbs * seq, quarter)
        part = jnp.dot(second_all, hid, preferred_element_type=f32).astype(bf16)
        for owner in range(8):
            red_part[owner % 2, q, owner // 2] = part[owner * 64:(owner + 1) * 64, :]
    red.pair_start()
    dense_back(0)
    red.column_start()
    for mb in range(1, mbs):
        dense_back(mb)
    first_all = turned(first_low[...])
    for q, cols in enumerate(quarters):
        hid_grad = pool[(4 + q) * mbs:(5 + q) * mbs].reshape(mbs * seq, quarter)
        part = jnp.dot(first_all, hid_grad, preferred_element_type=f32).astype(bf16)
        for zz in range(4):
            for owner in range(8):
                begin = zz * shard + owner * 16
                wide_part[owner % 2, zz, owner // 2, 16 * q:16 * q + 16, :] = part[begin:begin + 16, :]
    mixed_all = jnp.concatenate([mixed[mb].reshape(width, seq) for mb in range(mbs)], axis=1)
    part = jnp.dot(mixed_all, branch_grad[...], preferred_element_type=f32).astype(bf16)
    for zz in range(4):
        for owner in range(8):
            begin = zz * shard + owner * 16
            wide_part[owner % 2, zz, owner // 2, 64:80, :] = part[begin:begin + 16, :]
    wide.pair_start()
    for copy in backs:
        copy.start()
    red.column_combine()

    ones = jnp.ones((8, 8 * seq), bf16)
    biases = [jnp.zeros((1, feat), f32), jnp.zeros((1, feat), f32)]

    def head_gradients(mb):
        if mb == 0:
            for copy in backs:
                copy.wait()
        block = jnp.concatenate([made[:, mb, j].reshape(3 * feat, seq) for j in range(8)], axis=1)
        rows = pool[mb * 8:(mb + 1) * 8].reshape(8 * seq, width)
        total = jnp.dot(block, rows, preferred_element_type=f32)
        thin_total[...] = total if mb == 0 else thin_total[...] + total
        biases[0] = biases[0] + dots(ones, block[0:feat], 1, 1)[0:1]
        biases[1] = biases[1] + dots(ones, block[2 * feat:], 1, 1)[0:1]

    hooks = {
        (0, 0): [wide.column_start],
        (0, 3): [g_proj.arrive],
        (1, 0): [red.plane_start],
        (1, 7): [wide.column_combine],
        (2, 0): [red.back_start],
        (2, 7): [red.relay],
    }

    def grad_copy(mb, j, source):
        return remote(made.at[:, mb, j], got.at[mb, :, source], kv_s.at[mb, j], kv_r.at[mb, source], (j, z))

    for mb in range(mbs):
        for k in range(1, 8):
            slot = dhead.at[mb, place.source(k)]
            remote(slot, slot, d_s.at[mb, k - 1], d_r.at[mb, k - 1], (place.ring(k), z)).wait_recv()
        for j in range(8):
            cols = slice(j * seq, (j + 1) * seq)
            rows_a[cols, :] = turned(qkv[0, mb, j])
            rows_b[cols, :] = turned(dhead[mb, j])
            delta[:, cols] = jnp.sum(dhead[mb, j].astype(f32) * head[mb, j].astype(f32), axis=0, keepdims=True)
        dq_turned[...] = jnp.zeros_like(dq_turned)
        for j in range(8):
            begin = j * seq
            span = 8 * seq - begin
            key_turned = qkv[1, mb, j]
            queries = jnp.concatenate([qkv[0, mb, i] for i in range(j, 8)], axis=1)
            grads = jnp.concatenate([dhead[mb, i] for i in range(j, 8)], axis=1)
            scores = jnp.dot(turned(key_turned), queries, preferred_element_type=f32)
            dprobs = jnp.dot(turned(qkv[2, mb, j]), grads, preferred_element_type=f32)
            key_pos = lax.broadcasted_iota(jnp.int32, (seq, 1), 0) + begin
            query_pos = lax.broadcasted_iota(jnp.int32, (1, span), 1) + begin
            allowed = (key_pos >= starts_ref[mb, :, begin:]) & (key_pos <= query_pos)
            probs = jnp.where(allowed, jnp.exp(scores - log_total[mb, :, begin:]), 0.0)
            score_grad = (probs * (dprobs - delta[:, begin:])).astype(bf16)
            value_made = jnp.dot(probs.astype(bf16), rows_b[begin:, :], preferred_element_type=f32)
            key_made = jnp.dot(score_grad, rows_a[begin:, :], preferred_element_type=f32)
            dq_turned[:, begin:] += jnp.dot(key_turned, score_grad, preferred_element_type=f32)
            made[1, mb, j] = jnp.transpose(key_made).astype(bf16)
            made[2, mb, j] = jnp.transpose(value_made).astype(bf16)
            made[0, mb, j] = (dq_turned[:, begin:begin + seq] * 0.125).astype(bf16)

            @pl.when(c == j)
            def keep():
                for m in range(3):
                    got[mb, m, c] = made[m, mb, j]

            @pl.when(c != j)
            def send():
                grad_copy(mb, j, c).start()

            for hook in hooks.get((mb, j), []):
                hook()
        head_gradients(mb)

    def x_gradient(mb):
        x_buf[mb] = gy_buf[mb] + dots(got[mb].reshape(3 * width, seq), wt[...].reshape(3 * width, width), 0, 0)
        copy = pltpu.make_async_copy(x_buf.at[mb], xg_hbm.at[mb], store_sems.at[2, mb])
        copy.start()
        stores.append(copy)

    low = thin_total[...].astype(bf16)
    for zz in range(4):
        thin_part[zz] = low[:, zz * shard:(zz + 1) * shard]
    thin.column_start()
    lane_head = lax.div(lax.broadcasted_iota(jnp.int32, (1, width), 1), feat)
    bias_q, bias_v = [jnp.where(lane_head == c, jnp.concatenate([b] * 8, axis=1), 0.0) for b in biases]
    for zz in range(4):
        cols = slice(zz * shard, (zz + 1) * shard)
        vec_part[zz, 0:1, :] = bias_q[:, cols]
        vec_part[zz, 1:2, :] = bias_v[:, cols]
        vec_part[zz, 2:8, :] = sums[0:6, cols]
        for r in range(4):
            vec_part[zz, 8 + r:9 + r, :] = sums[6 + zz:7 + zz, r * 128:(r + 1) * 128]
        vec_part[zz, 12:16, :] = jnp.zeros((4, 128), f32)
    for d in (1, 3, 2):
        go(remote(vec_part.at[place.up(d)], vec_column.at[d - 1], vc_s.at[d - 1], vc_r.at[d - 1], (c, place.up(d))))
    g_proj.ready()

    def take_gradients(mb):
        for k in range(1, 8):
            grad_copy(mb, 0, place.source(k)).wait_recv()
        x_gradient(mb)

    take_gradients(0)
    thin.back_start()
    wide.plane_start()
    for d in (1, 3, 2):
        slot = vec_column.at[d - 1]
        remote(slot, slot, vc_s.at[d - 1], vc_r.at[d - 1], (c, place.up(d))).wait_recv()
    vec_plane[c] = vec_part[z] + vec_column[0] + vec_column[1] + vec_column[2]
    for k in range(1, 8):
        go(remote(vec_plane.at[c], vec_plane.at[c], vp_s.at[k - 1], vp_r.at[k - 1], (place.ring(k), z)))
    take_gradients(1)
    thin.relay()
    wide.back_start()
    take_gradients(2)
    for k in range(1, 8):
        slot = vec_plane.at[place.source(k)]
        remote(slot, slot, vp_s.at[k - 1], vp_r.at[k - 1], (place.ring(k), z)).wait_recv()
    total = vec_plane[0]
    for k in range(1, 8):
        total = total + vec_plane[k]
    vec_out[...] = total
    wide.relay()
    for reduced in (red, wide, thin):
        reduced.finish()
    for gather in gathers:
        gather.finish()
    for copy in sends:
        copy.wait_send()
    for copy in stores:
        copy.wait()
    for j in range(8):
        @pl.when(c != j)
        def sent():
            for mb in range(mbs):
                grad_copy(mb, j, c).wait_send()


def layer_call(starts, wq, wk, wv, vectors, x, y, gx, gy, wo, wh, wr):
    mbs, seq, width = x.shape
    hidden = wh.shape[1]
    feat = width // HEADS
    count = HEADS * seq
    tokens = mbs * seq
    vm = pl.BlockSpec(memory_space=pltpu.VMEM)
    anym = pl.BlockSpec(memory_space=pl.ANY)
    dma = pltpu.SemaphoreType.DMA
    sds = jax.ShapeDtypeStruct
    V = pltpu.VMEM
    big = sds((mbs, seq, width), f32)

    def reduce_scratch(rows, cols):
        return [
            V((2, 4, 4, rows, cols), bf16), V((4, 4, rows, cols), bf16), V((4, rows, cols), bf16),
            V((3, 4, rows, cols), bf16), V((4, rows, cols), bf16), V((3, rows, cols), bf16),
        ]

    return pl.pallas_call(
        layer_kernel,
        out_shape=(
            big, big, big, sds((mbs * 8, seq, width), bf16), sds((8, 64, 512), bf16), sds((8, 80, 512), bf16), sds((8, 192, 128), bf16), sds((16, 128), f32),
        ),
        in_specs=[vm] * 13 + [anym] * 7,
        out_specs=[anym] * 4 + [vm] * 4,
        scratch_shapes=[V((mbs, seq, width), f32)] * 4 + [
            V((3, 8, feat, width), bf16), V((width, width), bf16), V((width, hidden), bf16), V((hidden, width), bf16),
            V((4, 16, 128), f32), V((2, width, 1), f32), V((3, feat, width), bf16), V((3, mbs, 8, feat, seq), bf16), V((3, mbs, 8, feat, seq), bf16),
            V((count, feat), bf16), V((count, feat), bf16),
            V((mbs, 8, feat, seq), bf16), V((mbs, 8, feat, seq), bf16), V((mbs, 1, count), f32),
            V((mbs * 8, seq, width), bf16), V((tokens, width), bf16), V((tokens, width), bf16),
            V((tokens, width), bf16), V((tokens, hidden), f32), V((mbs, 8, feat, seq), bf16), V((mbs, 8, feat, seq), bf16),
            V((mbs, seq, width), f32), V((mbs, seq, 1), f32),
            V((feat, count), f32), V((1, count), f32), V((mbs, 3, 8, feat, seq), bf16),
        ] + reduce_scratch(64, 512) + reduce_scratch(80, 512) + [
            V((3 * feat, width), f32), V((4, 192, 128), bf16), V((3, 192, 128), bf16),
        ] + [
            V((4, 16, 128), f32), V((3, 16, 128), f32), V((8, 16, 128), f32), V((16, width), f32),
            dma((4, mbs)), dma((3, mbs)), dma((3,)), dma((mbs * 8,)), dma((3,)), dma((3,)),
            dma((mbs, 8)), dma((mbs, 8)), dma((3,)), dma((3,)),
            dma((6, 3)), dma((6, 3)), dma((6, 3)), dma((6, 3)), dma((6, 2, 3)), dma((6, 2, 3)),
            dma((mbs, 7)), dma((mbs, 7)), dma((mbs, 7)), dma((mbs, 7)),
            dma((mbs, 8)), dma((mbs, 8)),
            dma((3, 1)), dma((3, 1)), dma((3, 3)), dma((3, 3)), dma((3, 1)), dma((3, 3)), dma((3, 3)),
            dma((3, 3)), dma((3, 3)), dma((3, 4)), dma((3, 4)),
            dma((3,)), dma((3,)), dma((7,)), dma((7,)),
        ],
        compiler_params=pltpu.CompilerParams(collective_id=1, has_side_effects=True, vmem_limit_bytes=VMEM_LIMIT),
        name="layer",
    )(starts, wq, wk, wv, *vectors, x, y, gx, gy, wo, wh, wr)


def unpack_kernel(
    red_ref, hid_ref, thin_ref, vec_ref, xn_in, yn_in, xg_in,
    xn_out, yn_out, xg_out, wq_ref, wk_ref, wv_ref, wo_ref, wh_ref, wr_ref,
    qb_ref, vb_ref, ob_ref, fg_ref, fs_ref, rb_ref, sg_ref, ss_ref, hb_ref, held, sems, out_sems,
):
    mbs = held.shape[1]
    big = ((xn_in, xn_out), (yn_in, yn_out), (xg_in, xg_out))
    loads = [
        [pltpu.make_async_copy(src.at[mb], held.at[i, mb], sems.at[i, mb]) for mb in range(mbs)]
        for i, (src, _) in enumerate(big)
    ]
    stores = [
        [pltpu.make_async_copy(held.at[i, mb], dst.at[mb], out_sems.at[i, mb]) for mb in range(mbs)]
        for i, (_, dst) in enumerate(big)
    ]

    def turn_round(i):
        for mb in range(mbs):
            loads[i][mb].wait()
            stores[i][mb].start()

    for group in loads:
        for copy in group:
            copy.start()
    wr_ref[...] = jnp.transpose(jnp.concatenate([red_ref[owner] for owner in range(8)], axis=0).astype(f32))
    turn_round(0)
    for owner in range(8):
        rows = slice(owner * 16, (owner + 1) * 16)
        for q in range(4):
            wh_ref[rows, q * 512:(q + 1) * 512] = hid_ref[owner, 16 * q:16 * q + 16, :].astype(f32)
        wo_ref[rows, :] = hid_ref[owner, 64:80, :].astype(f32)
    turn_round(1)
    for m, out in enumerate((wq_ref, wk_ref, wv_ref)):
        stacked = jnp.concatenate([thin_ref[owner, m * 64:(m + 1) * 64, :] for owner in range(8)], axis=0)
        out[...] = jnp.transpose(stacked.astype(f32))
    turn_round(2)
    for row, out in enumerate((qb_ref, vb_ref, ob_ref, fg_ref, fs_ref, rb_ref, sg_ref, ss_ref)):
        out[...] = vec_ref[row]
    for r in range(4):
        hb_ref[r * 128:(r + 1) * 128] = vec_ref[8 + r]
    for group in stores:
        for copy in group:
            copy.wait()


def unpack_call(red, hid, thin, vec, xn, yn, xg):
    mbs = xn.shape[0]
    vm = pl.BlockSpec(memory_space=pltpu.VMEM)
    anym = pl.BlockSpec(memory_space=pl.ANY)
    sds = jax.ShapeDtypeStruct
    small = sds((128, 512), f32)
    big = sds(xn.shape, f32)
    dma = pltpu.SemaphoreType.DMA
    return pl.pallas_call(
        unpack_kernel,
        out_shape=(big, big, big, small, small, small, small, sds((128, 2048), f32), sds((512, 512), f32))
        + (sds((128,), f32),) * 8 + (sds((512,), f32),),
        in_specs=[vm] * 4 + [anym] * 3,
        out_specs=[anym] * 3 + [vm] * 15,
        scratch_shapes=[pltpu.VMEM((3,) + xn.shape, f32), dma((3, mbs)), dma((3, mbs))],
        compiler_params=pltpu.CompilerParams(vmem_limit_bytes=VMEM_LIMIT),
        name="unpack",
    )(red, hid, thin, vec, xn, yn, xg)


def head_shards(
    x_stream, y_stream, grad_x, grad_y, doc_start, query_weight, query_bias, key_weight, value_weight, value_bias,
    output_weight, output_bias, first_gain, first_shift, hidden_weight, hidden_bias, reduce_weight, reduce_bias,
    second_gain, second_shift,
):
    mbs = x_stream.shape[1]
    vectors = (query_bias, value_bias, output_bias, first_gain, first_shift, reduce_bias, second_gain, second_shift, hidden_bias)
    starts = doc_start.reshape(mbs, 1, -1)
    xn, yn, xg, _, red, hid, thin, small = layer_call(
        starts, query_weight, key_weight, value_weight, vectors, x_stream[0], y_stream[0], grad_x[0], grad_y[0],
        output_weight, hidden_weight, reduce_weight,
    )
    xn, yn, xg, g_q, g_k, g_v, g_o, g_h, g_r, qb, vb, ob, fg, fs, rb, sg, ss, hb = unpack_call(
        red, hid, thin, small, xn, yn, xg
    )
    return (
        xn[None], yn[None], xg[None], g_q, qb, g_k, g_v, vb, g_o, ob, fg, fs, g_h, hb, g_r, rb, sg, ss,
    )


def solution(mesh):
    in_specs = (
        P("fsdp", None, "ctx", None),
        P("fsdp", None, "ctx", None),
        P("fsdp", None, "ctx", None),
        P("fsdp", None, "ctx", None),
        P("fsdp", None, None),
        P("fsdp", None),
        P("fsdp"),
        P("fsdp", None),
        P("fsdp", None),
        P("fsdp"),
        P("fsdp", None),
        P("fsdp"),
        P("fsdp"),
        P("fsdp"),
        P("fsdp", None),
        P("fsdp"),
        P("fsdp", None),
        P("fsdp"),
        P("fsdp"),
        P("fsdp"),
    )
    out_specs = (
        P("fsdp", None, "ctx", None),
        P("fsdp", None, "ctx", None),
        P("fsdp", None, "ctx", None),
        P("fsdp", None),
        P("fsdp"),
        P("fsdp", None),
        P("fsdp", None),
        P("fsdp"),
        P("fsdp", None),
        P("fsdp"),
        P("fsdp"),
        P("fsdp"),
        P("fsdp", None),
        P("fsdp"),
        P("fsdp", None),
        P("fsdp"),
        P("fsdp"),
        P("fsdp"),
    )
    body = head_shards if mesh.shape["ctx"] == HEADS and mesh.shape["fsdp"] == 4 else shards
    return jax.shard_map(body, mesh=mesh, in_specs=in_specs, out_specs=out_specs, check_vma=False)
```

```python
import math
import jax
import jax.numpy as jnp
from jax import lax
from jax.experimental import pallas as pl
from jax.experimental.pallas import tpu as pltpu
from jax.sharding import PartitionSpec as P

HEADS = 8
NEG = -1e30
bf16 = jnp.bfloat16
f32 = jnp.float32
MESH = pl.DeviceIdType.MESH
VMEM_LIMIT = 62 << 20


def dots(left, right, left_dim, right_dim):
    return lax.dot_general(
        left, right, (((left_dim,), (right_dim,)), ((), ())), preferred_element_type=f32
    )


def turned(block):
    return jnp.transpose(block.astype(f32)).astype(bf16)


class Place:
    def __init__(self):
        self.c = lax.axis_index("ctx")
        self.z = lax.axis_index("fsdp")
        self.core = lax.rem(self.c, 2)
        self.x = lax.rem(lax.div(self.c, 2), 2)
        self.y = lax.div(self.c, 4)
        self.sibling = self.c + 1 - 2 * self.core
        self.x_next = self.c + 2 - 4 * self.x
        self.y_next = self.c + 4 - 8 * self.y
        self.middle = lax.rem(self.z + 1, 4) > 1

    def ring(self, k):
        return lax.rem(self.c + k, 8)

    def source(self, k):
        return lax.rem(self.c + 8 - k, 8)

    def up(self, d):
        return lax.rem(self.z + d, 4)

    def down(self, d):
        return lax.rem(self.z + 4 - d, 4)


def knock(place):
    barrier = pltpu.get_barrier_semaphore()
    for k in range(1, 8):
        pl.semaphore_signal(barrier, inc=1, device_id=(place.ring(k), place.z), device_id_type=MESH)
    for d in range(1, 4):
        pl.semaphore_signal(barrier, inc=1, device_id=(place.c, place.up(d)), device_id_type=MESH)


def enter():
    pl.semaphore_wait(pltpu.get_barrier_semaphore(), 10)


def remote(src, dst, send_sem, recv_sem, device):
    return pltpu.make_async_remote_copy(
        src_ref=src, dst_ref=dst, send_sem=send_sem, recv_sem=recv_sem,
        device_id=device, device_id_type=MESH,
    )


def aligned(start, size, unit):
    return pl.ds(pl.multiple_of(start, unit), size)


neg_big = -1e30
norm_eps = 1e-05
root_half = 0.7071067811865476
inv_root_tau = 0.3989422804014327


def swapped(block, axis, stride):
    count = lax.axis_size(axis)
    route = []
    for low in range(count):
        high = low | 1 << stride
        if high != low and high < count:
            route += [(low, high), (high, low)]
    return lax.ppermute(block, axis, route)


def matmul(left, right):
    return jnp.dot(left, right, preferred_element_type=jnp.float32)


def matmul_left_t(left, right):
    return lax.dot_general(
        left, right, (((0,), (0,)), ((), ())), preferred_element_type=jnp.float32
    )


def matmul_right_t(left, right):
    return lax.dot_general(
        left, right, (((1,), (1,)), ((), ())), preferred_element_type=jnp.float32
    )


def gelu_value(hidden):
    return hidden * 0.5 * (1.0 + jax.scipy.special.erf(hidden * root_half))


def gelu_slope(hidden):
    return 0.5 * (
        1.0 + jax.scipy.special.erf(hidden * root_half)
    ) + hidden * inv_root_tau * jnp.exp(-0.5 * hidden * hidden)


def norm_forward(total, gain, shift):
    mean_val = jnp.mean(total, axis=-1, keepdims=True)
    centered = total - mean_val
    inv_std = lax.rsqrt(jnp.mean(centered * centered, axis=-1, keepdims=True) + norm_eps)
    normed = centered * inv_std
    return (normed * gain + shift, normed, inv_std)


def norm_backward(upstream, normed, inv_std, gain):
    scaled = upstream * gain
    first_mean = jnp.mean(scaled, axis=-1, keepdims=True)
    second_mean = jnp.mean(scaled * normed, axis=-1, keepdims=True)
    return inv_std * (scaled - first_mean - normed * second_mean)


def allowed_pairs(query_pos, query_start, key_pos):
    return (key_pos[None, :] <= query_pos[:, None]) & (key_pos[None, :] >= query_start[:, None])


def pair_needed(key_lo, query_lo, span):
    needed = key_lo <= query_lo + span - 1
    return needed


def half_firsts(device, seq_dev, cycle_size):
    half = seq_dev // 2
    first = device * seq_dev
    second = (cycle_size - 1 - device) * seq_dev + half
    return (first, second)


def mirror_inputs(members, cycle_size):
    moved = members
    for bit in range(cycle_size.bit_length() - 1):
        moved = swapped((moved[0], moved[1], moved[2], moved[3]), "ctx", bit)
    return moved


def mirror_outputs(members, cycle_size):
    moved = members
    for bit in range(cycle_size.bit_length() - 1):
        moved = swapped((moved[0], moved[1], moved[2]), "ctx", bit)
    return moved


def block_scores(query_three, key_three, allowed, scale_factor):
    scores = (
        jnp.einsum("qhd,khd->hqk", query_three, key_three, preferred_element_type=jnp.float32)
        * scale_factor
    )
    return jnp.where(allowed[None], scores, neg_big)


def forward_update(state_mb, query_three, key_three, value_three, allowed, scale_factor):
    run_max, run_sum, run_acc = state_mb
    scores = block_scores(query_three, key_three, allowed, scale_factor)
    new_max = jnp.maximum(run_max, jnp.max(scores, axis=-1))
    rescale = jnp.exp(run_max - new_max)
    weights = jnp.where(allowed[None], jnp.exp(scores - new_max[:, :, None]), 0.0)
    new_sum = run_sum * rescale + jnp.sum(weights, axis=-1)
    mixed_sum = jnp.einsum(
        "hqk,khd->qhd",
        weights.astype(jnp.bfloat16),
        value_three,
        preferred_element_type=jnp.float32,
    )
    new_acc = run_acc * jnp.transpose(rescale)[:, :, None] + mixed_sum
    return (new_max, new_sum, new_acc)


def pair_grads(
    query_three, dout_three, key_three, value_three, allowed, log_total, row_delta, scale_factor
):
    scores = block_scores(query_three, key_three, allowed, scale_factor)
    prob_table = jnp.where(allowed[None], jnp.exp(scores - log_total[:, :, None]), 0.0)
    dprobs = jnp.einsum("qhd,khd->hqk", dout_three, value_three, preferred_element_type=jnp.float32)
    score_grad = (prob_table * (dprobs - row_delta[:, :, None])).astype(jnp.bfloat16)
    return (prob_table, score_grad)


def fold_blocks(pieces, state_all, update, base_rows):
    rows_in = pieces[0].shape[1]
    step_rows = min(rows_in, base_rows)

    def one_step(block_index, state_inner):
        offset = block_index * step_rows
        sliced = tuple(
            (lax.dynamic_slice_in_dim(member, offset, step_rows, 1) for member in pieces)
        )
        return update(state_inner, sliced, offset)

    return lax.fori_loop(0, rows_in // step_rows, one_step, state_all)


def shards(
    x_stream,
    y_stream,
    grad_x,
    grad_y,
    doc_start,
    query_weight,
    query_bias,
    key_weight,
    value_weight,
    value_bias,
    output_weight,
    output_bias,
    first_gain,
    first_shift,
    hidden_weight,
    hidden_bias,
    reduce_weight,
    reduce_bias,
    second_gain,
    second_shift,
):
    gathered = (
        lax.all_gather(query_weight, "fsdp", axis=0, tiled=True),
        lax.all_gather(query_bias, "fsdp", axis=0, tiled=True),
        lax.all_gather(key_weight, "fsdp", axis=0, tiled=True),
        lax.all_gather(value_weight, "fsdp", axis=0, tiled=True),
        lax.all_gather(value_bias, "fsdp", axis=0, tiled=True),
        lax.all_gather(output_weight, "fsdp", axis=0, tiled=True),
        lax.all_gather(output_bias, "fsdp", axis=0, tiled=True),
        lax.all_gather(first_gain, "fsdp", axis=0, tiled=True),
        lax.all_gather(first_shift, "fsdp", axis=0, tiled=True),
        lax.all_gather(hidden_weight, "fsdp", axis=0, tiled=True),
        lax.all_gather(hidden_bias, "fsdp", axis=0, tiled=True),
        lax.all_gather(reduce_weight, "fsdp", axis=0, tiled=True),
        lax.all_gather(reduce_bias, "fsdp", axis=0, tiled=True),
        lax.all_gather(second_gain, "fsdp", axis=0, tiled=True),
        lax.all_gather(second_shift, "fsdp", axis=0, tiled=True),
    )
    (
        w_query,
        b_query,
        w_key,
        w_value,
        b_value,
        w_output,
        b_output,
        gain_one,
        shift_one,
        w_hidden,
        b_hidden,
        w_reduce,
        b_reduce,
        gain_two,
        shift_two,
    ) = gathered
    b_query = b_query.astype(jnp.float32)
    b_value = b_value.astype(jnp.float32)
    b_output = b_output.astype(jnp.float32)
    gain_one = gain_one.astype(jnp.float32)
    shift_one = shift_one.astype(jnp.float32)
    b_hidden = b_hidden.astype(jnp.float32)
    b_reduce = b_reduce.astype(jnp.float32)
    gain_two = gain_two.astype(jnp.float32)
    shift_two = shift_two.astype(jnp.float32)
    micro_count, seq_dev, model_width = (x_stream.shape[1], x_stream.shape[2], x_stream.shape[3])
    half = seq_dev // 2
    head_count = HEADS
    head_dim = model_width // head_count
    scale_factor = 1.0 / math.sqrt(head_dim)
    token_rows = micro_count * seq_dev
    cycle_size = lax.axis_size("ctx")
    my_index = lax.axis_index("ctx")
    half_range = jnp.arange(half, dtype=jnp.int32)
    own_firsts = half_firsts(my_index, seq_dev, cycle_size)
    own_pos = [own_firsts[0] + half_range, own_firsts[1] + half_range]
    positions_own = jnp.concatenate(own_pos)
    doc_all = doc_start[0]
    starts_own = jnp.take(doc_all, positions_own, axis=1)
    own_starts = [
        [starts_own[micro_index, part * half : (part + 1) * half] for part in range(2)]
        for micro_index in range(micro_count)
    ]
    x_mb, y_mb, gx_mb, gy_mb = (x_stream[0], y_stream[0], grad_x[0], grad_y[0])
    moved = mirror_inputs(
        (x_mb[:, half:], y_mb[:, half:], gx_mb[:, half:], gy_mb[:, half:]), cycle_size
    )
    x_mb = jnp.concatenate([x_mb[:, :half], moved[0]], axis=1)
    y_mb = jnp.concatenate([y_mb[:, :half], moved[1]], axis=1)
    gx_mb = jnp.concatenate([gx_mb[:, :half], moved[2]], axis=1)
    gy_mb = jnp.concatenate([gy_mb[:, :half], moved[3]], axis=1)
    x_rows = x_mb.reshape(token_rows, model_width)
    y_rows = y_mb.reshape(token_rows, model_width)
    gx_rows = gx_mb.reshape(token_rows, model_width)
    gy_rows = gy_mb.reshape(token_rows, model_width)
    x_low = x_rows.astype(jnp.bfloat16)
    query_low = (matmul(x_low, w_query) + b_query).astype(jnp.bfloat16)
    key_low = matmul(x_low, w_key).astype(jnp.bfloat16)
    value_low = (matmul(x_low, w_value) + b_value).astype(jnp.bfloat16)
    query_mb = query_low.reshape(micro_count, seq_dev, model_width)
    key_mb = key_low.reshape(micro_count, seq_dev, model_width)
    value_mb = value_low.reshape(micro_count, seq_dev, model_width)
    query_three = [
        query_mb[micro_index].reshape(seq_dev, head_count, head_dim)
        for micro_index in range(micro_count)
    ]
    key_own = [
        key_mb[micro_index].reshape(seq_dev, head_count, head_dim)
        for micro_index in range(micro_count)
    ]
    value_own = [
        value_mb[micro_index].reshape(seq_dev, head_count, head_dim)
        for micro_index in range(micro_count)
    ]

    def forward_step(state_inner, sliced, key_first):
        key_block, value_block = sliced
        source = key_first // seq_dev
        key_firsts = half_firsts(source, seq_dev, cycle_size)
        updated = []
        for micro_index in range(micro_count):
            key_three = key_block[micro_index].reshape(seq_dev, head_count, head_dim)
            value_three = value_block[micro_index].reshape(seq_dev, head_count, head_dim)
            states = list(state_inner[micro_index])
            for query_part in range(2):
                query_piece = query_three[micro_index][query_part * half : (query_part + 1) * half]
                for key_part in range(2):
                    key_piece = key_three[key_part * half : (key_part + 1) * half]
                    value_piece = value_three[key_part * half : (key_part + 1) * half]
                    allowed = allowed_pairs(
                        own_pos[query_part],
                        own_starts[micro_index][query_part],
                        key_firsts[key_part] + half_range,
                    )
                    needed = pair_needed(key_firsts[key_part], own_firsts[query_part], half)

                    def forward_compute(state_mb):
                        return forward_update(
                            state_mb, query_piece, key_piece, value_piece, allowed, scale_factor
                        )

                    def forward_unchanged(state_mb):
                        return state_mb

                    states[query_part] = lax.cond(
                        needed, forward_compute, forward_unchanged, states[query_part]
                    )
            updated.append(tuple(states))
        return tuple(updated)

    def empty_state():
        return (
            jnp.full((head_count, half), neg_big, jnp.float32),
            jnp.zeros((head_count, half), jnp.float32),
            jnp.zeros((half, head_count, head_dim), jnp.float32),
        )

    forward_init = tuple(((empty_state(), empty_state()) for micro_index in range(micro_count)))
    attend_state = fold_blocks(
        (
            lax.all_gather(key_mb, "ctx", axis=1, tiled=True),
            lax.all_gather(value_mb, "ctx", axis=1, tiled=True),
        ),
        forward_init,
        forward_step,
        seq_dev,
    )
    out_parts = []
    log_parts = []
    for micro_index in range(micro_count):
        out_halves = []
        log_halves = []
        for query_part in range(2):
            run_max, run_sum, run_acc = attend_state[micro_index][query_part]
            out_halves.append(run_acc / jnp.transpose(run_sum)[:, :, None])
            log_halves.append(run_max + jnp.log(run_sum))
        out_parts.append(jnp.concatenate(out_halves, axis=0))
        log_parts.append(jnp.concatenate(log_halves, axis=1))
    out_raw = jnp.stack(out_parts)
    log_total_all = jnp.stack(log_parts)
    out_low = out_raw.reshape(token_rows, model_width).astype(jnp.bfloat16)
    branch = matmul(out_low, w_output) + b_output
    x_first, normed_one, inv_one = norm_forward(x_rows + branch, gain_one, shift_one)
    y_first = y_rows + branch
    x_first_low = x_first.astype(jnp.bfloat16)
    hidden_pre = matmul(x_first_low, w_hidden) + b_hidden
    hidden_low = gelu_value(hidden_pre).astype(jnp.bfloat16)
    second = matmul(hidden_low, w_reduce) + b_reduce
    x_next, normed_two, inv_two = norm_forward(x_first + second, gain_two, shift_two)
    y_next = y_first + second
    total_two_grad = norm_backward(gx_rows, normed_two, inv_two, gain_two)
    second_gain_grad = jnp.sum(gx_rows * normed_two, axis=0)
    second_shift_grad = jnp.sum(gx_rows, axis=0)
    second_grad = (total_two_grad + gy_rows).astype(jnp.bfloat16)
    reduce_weight_grad = matmul_left_t(hidden_low, second_grad)
    reduce_bias_grad = jnp.sum(second_grad.astype(jnp.float32), axis=0)
    hidden_grad = (matmul_right_t(second_grad, w_reduce) * gelu_slope(hidden_pre)).astype(
        jnp.bfloat16
    )
    hidden_weight_grad = matmul_left_t(x_first_low, hidden_grad)
    hidden_bias_grad = jnp.sum(hidden_grad.astype(jnp.float32), axis=0)
    first_up = total_two_grad + matmul_right_t(hidden_grad, w_hidden)
    total_one_grad = norm_backward(first_up, normed_one, inv_one, gain_one)
    first_gain_grad = jnp.sum(first_up * normed_one, axis=0)
    first_shift_grad = jnp.sum(first_up, axis=0)
    branch_grad = (total_one_grad + gy_rows).astype(jnp.bfloat16)
    output_weight_grad = matmul_left_t(out_low, branch_grad)
    output_bias_grad = jnp.sum(branch_grad.astype(jnp.float32), axis=0)
    dout_low = matmul_right_t(branch_grad, w_output).astype(jnp.bfloat16)
    dout_mb = dout_low.reshape(micro_count, seq_dev, head_count, head_dim)
    delta_all = jnp.einsum("bqhd,bqhd->bhq", dout_mb.astype(jnp.float32), out_raw)
    dout_three = [dout_mb[micro_index] for micro_index in range(micro_count)]
    dout_rows = dout_low.reshape(micro_count, seq_dev, model_width)

    def zero_query():
        return jnp.zeros((half, head_count, head_dim), jnp.float32)

    query_init = tuple(((zero_query(), zero_query()) for micro_index in range(micro_count)))

    def query_step(state_inner, sliced, key_first):
        key_block, value_block = sliced
        source = key_first // seq_dev
        key_firsts = half_firsts(source, seq_dev, cycle_size)
        updated = []
        for micro_index in range(micro_count):
            key_three = key_block[micro_index].reshape(seq_dev, head_count, head_dim)
            value_three = value_block[micro_index].reshape(seq_dev, head_count, head_dim)
            query_accs = list(state_inner[micro_index])
            for query_part in range(2):
                rows = slice(query_part * half, (query_part + 1) * half)
                query_piece = query_three[micro_index][rows]
                dout_piece = dout_three[micro_index][rows]
                log_piece = log_total_all[micro_index][:, rows]
                delta_piece = delta_all[micro_index][:, rows]
                for key_part in range(2):
                    key_piece = key_three[key_part * half : (key_part + 1) * half]
                    value_piece = value_three[key_part * half : (key_part + 1) * half]
                    allowed = allowed_pairs(
                        own_pos[query_part],
                        own_starts[micro_index][query_part],
                        key_firsts[key_part] + half_range,
                    )
                    needed = pair_needed(key_firsts[key_part], own_firsts[query_part], half)

                    def query_compute(query_acc):
                        prob_table, score_grad = pair_grads(
                            query_piece,
                            dout_piece,
                            key_piece,
                            value_piece,
                            allowed,
                            log_piece,
                            delta_piece,
                            scale_factor,
                        )
                        return (
                            query_acc
                            + jnp.einsum(
                                "hqk,khd->qhd",
                                score_grad,
                                key_piece,
                                preferred_element_type=jnp.float32,
                            )
                            * scale_factor
                        )

                    def query_unchanged(query_acc):
                        return query_acc

                    query_accs[query_part] = lax.cond(
                        needed, query_compute, query_unchanged, query_accs[query_part]
                    )
            updated.append(tuple(query_accs))
        return tuple(updated)

    query_parts = fold_blocks(
        (
            lax.all_gather(key_mb, "ctx", axis=1, tiled=True),
            lax.all_gather(value_mb, "ctx", axis=1, tiled=True),
        ),
        query_init,
        query_step,
        seq_dev,
    )
    stats_all = (
        lax.all_gather(log_total_all, "ctx", axis=2, tiled=True),
        lax.all_gather(delta_all, "ctx", axis=2, tiled=True),
    )

    def key_step(state_inner, sliced, query_begin):
        query_block, dout_block = sliced
        source = query_begin // seq_dev
        query_firsts = half_firsts(source, seq_dev, cycle_size)
        updated = []
        for micro_index in range(micro_count):
            log_block = lax.dynamic_slice_in_dim(stats_all[0][micro_index], query_begin, seq_dev, 1)
            delta_block = lax.dynamic_slice_in_dim(
                stats_all[1][micro_index], query_begin, seq_dev, 1
            )
            query_whole = query_block[micro_index].reshape(seq_dev, head_count, head_dim)
            dout_whole = dout_block[micro_index].reshape(seq_dev, head_count, head_dim)
            key_accs = [
                state_inner[micro_index][0][part * half : (part + 1) * half] for part in range(2)
            ]
            value_accs = [
                state_inner[micro_index][1][part * half : (part + 1) * half] for part in range(2)
            ]
            for query_part in range(2):
                rows = slice(query_part * half, (query_part + 1) * half)
                query_pos = query_firsts[query_part] + half_range
                starts_block = jnp.take(doc_all[micro_index], query_pos)
                query_piece = query_whole[rows]
                dout_piece = dout_whole[rows]
                log_piece = log_block[:, rows]
                delta_piece = delta_block[:, rows]
                for key_part in range(2):
                    key_piece = key_own[micro_index][key_part * half : (key_part + 1) * half]
                    value_piece = value_own[micro_index][key_part * half : (key_part + 1) * half]
                    allowed = allowed_pairs(query_pos, starts_block, own_pos[key_part])
                    needed = pair_needed(own_firsts[key_part], query_firsts[query_part], half)

                    def key_compute(operands):
                        key_acc, value_acc = operands
                        prob_table, score_grad = pair_grads(
                            query_piece,
                            dout_piece,
                            key_piece,
                            value_piece,
                            allowed,
                            log_piece,
                            delta_piece,
                            scale_factor,
                        )
                        key_add = (
                            jnp.einsum(
                                "hqk,qhd->khd",
                                score_grad,
                                query_piece,
                                preferred_element_type=jnp.float32,
                            )
                            * scale_factor
                        )
                        value_add = jnp.einsum(
                            "hqk,qhd->khd",
                            prob_table.astype(jnp.bfloat16),
                            dout_piece,
                            preferred_element_type=jnp.float32,
                        )
                        return (
                            key_acc + key_add.reshape(half, model_width),
                            value_acc + value_add.reshape(half, model_width),
                        )

                    def key_unchanged(operands):
                        return operands

                    result = lax.cond(
                        needed,
                        key_compute,
                        key_unchanged,
                        (key_accs[key_part], value_accs[key_part]),
                    )
                    key_accs[key_part] = result[0]
                    value_accs[key_part] = result[1]
            updated.append((jnp.concatenate(key_accs, axis=0), jnp.concatenate(value_accs, axis=0)))
        return tuple(updated)

    key_init = tuple(
        (
            (
                jnp.zeros((seq_dev, model_width), jnp.float32),
                jnp.zeros((seq_dev, model_width), jnp.float32),
            )
            for micro_index in range(micro_count)
        )
    )
    key_state = fold_blocks(
        (
            lax.all_gather(query_mb, "ctx", axis=1, tiled=True),
            lax.all_gather(dout_rows, "ctx", axis=1, tiled=True),
        ),
        key_init,
        key_step,
        seq_dev,
    )
    key_grad_sum = jnp.stack([key_state[micro_index][0] for micro_index in range(micro_count)])
    value_grad_sum = jnp.stack([key_state[micro_index][1] for micro_index in range(micro_count)])
    query_whole_parts = [
        jnp.concatenate([query_parts[micro_index][0], query_parts[micro_index][1]], axis=0)
        for micro_index in range(micro_count)
    ]
    query_grad_low = (
        jnp.stack(query_whole_parts).reshape(token_rows, model_width).astype(jnp.bfloat16)
    )
    key_grad_low = key_grad_sum.reshape(token_rows, model_width).astype(jnp.bfloat16)
    value_grad_low = value_grad_sum.reshape(token_rows, model_width).astype(jnp.bfloat16)
    query_weight_grad = matmul_left_t(x_low, query_grad_low)
    query_bias_grad = jnp.sum(query_grad_low.astype(jnp.float32), axis=0)
    key_weight_grad = matmul_left_t(x_low, key_grad_low)
    value_weight_grad = matmul_left_t(x_low, value_grad_low)
    value_bias_grad = jnp.sum(value_grad_low.astype(jnp.float32), axis=0)
    x_grad = (
        total_one_grad
        + matmul_right_t(query_grad_low, w_query)
        + matmul_right_t(key_grad_low, w_key)
        + matmul_right_t(value_grad_low, w_value)
    )
    shard_grads = (
        lax.psum_scatter(query_weight_grad, "fsdp", scatter_dimension=0, tiled=True),
        lax.psum_scatter(query_bias_grad, "fsdp", scatter_dimension=0, tiled=True),
        lax.psum_scatter(key_weight_grad, "fsdp", scatter_dimension=0, tiled=True),
        lax.psum_scatter(value_weight_grad, "fsdp", scatter_dimension=0, tiled=True),
        lax.psum_scatter(value_bias_grad, "fsdp", scatter_dimension=0, tiled=True),
        lax.psum_scatter(output_weight_grad, "fsdp", scatter_dimension=0, tiled=True),
        lax.psum_scatter(output_bias_grad, "fsdp", scatter_dimension=0, tiled=True),
        lax.psum_scatter(first_gain_grad, "fsdp", scatter_dimension=0, tiled=True),
        lax.psum_scatter(first_shift_grad, "fsdp", scatter_dimension=0, tiled=True),
        lax.psum_scatter(hidden_weight_grad, "fsdp", scatter_dimension=0, tiled=True),
        lax.psum_scatter(hidden_bias_grad, "fsdp", scatter_dimension=0, tiled=True),
        lax.psum_scatter(reduce_weight_grad, "fsdp", scatter_dimension=0, tiled=True),
        lax.psum_scatter(reduce_bias_grad, "fsdp", scatter_dimension=0, tiled=True),
        lax.psum_scatter(second_gain_grad, "fsdp", scatter_dimension=0, tiled=True),
        lax.psum_scatter(second_shift_grad, "fsdp", scatter_dimension=0, tiled=True),
    )
    summed = lax.psum(
        (
            shard_grads[0],
            shard_grads[1],
            shard_grads[2],
            shard_grads[3],
            shard_grads[4],
            shard_grads[5],
            shard_grads[6],
            shard_grads[7],
            shard_grads[8],
            shard_grads[9],
            shard_grads[10],
            shard_grads[11],
            shard_grads[12],
            shard_grads[13],
            shard_grads[14],
        ),
        "ctx",
    )
    mb_shape = (micro_count, seq_dev, model_width)
    x_next_mb = x_next.reshape(mb_shape)
    y_next_mb = y_next.reshape(mb_shape)
    x_grad_mb = x_grad.reshape(mb_shape)
    back = mirror_outputs(
        (x_next_mb[:, half:], y_next_mb[:, half:], x_grad_mb[:, half:]), cycle_size
    )
    x_next_mb = jnp.concatenate([x_next_mb[:, :half], back[0]], axis=1)
    y_next_mb = jnp.concatenate([y_next_mb[:, :half], back[1]], axis=1)
    x_grad_mb = jnp.concatenate([x_grad_mb[:, :half], back[2]], axis=1)
    out_shape = (1, micro_count, seq_dev, model_width)
    return (
        x_next_mb.reshape(out_shape),
        y_next_mb.reshape(out_shape),
        x_grad_mb.reshape(out_shape),
        summed[0],
        summed[1],
        summed[2],
        summed[3],
        summed[4],
        summed[5],
        summed[6],
        summed[7],
        summed[8],
        summed[9],
        summed[10],
        summed[11],
        summed[12],
        summed[13],
        summed[14],
    )


class Gather:
    def __init__(self, place, mine, at, sems, pair=None, side=None):
        self.place, self.mine, self.at, self.pair, self.side = place, mine, at, pair, side
        self.zs, self.zr, self.ps, self.pr, self.cs, self.cr = sems
        self.moved = []

    def held(self, zz, across=False, other=False):
        core = self.place.core
        core = 1 - core if other else core
        if self.pair is None:
            return self.at(zz, core)
        return self.at(zz, 2 * (1 - self.side if across else self.side) + core)

    def go(self, copy):
        copy.start()
        self.moved.append(copy)

    def start(self):
        place = self.place
        for d in (2, 1, 3):
            self.go(remote(self.mine, self.held(place.z), self.zs.at[d - 1], self.zr.at[d - 1], (place.c, place.up(d))))

    def arrive(self):
        place = self.place
        for d in (1, 3, 2):
            block = self.held(place.down(d))
            remote(block, block, self.zs.at[d - 1], self.zr.at[d - 1], (place.c, place.up(d))).wait_recv()
            if self.pair is not None:
                self.go(remote(block, block, self.ps.at[d - 1], self.pr.at[d - 1], (self.pair, place.z)))
            self.go(remote(block, block, self.cs.at[0, d - 1], self.cr.at[0, d - 1], (place.sibling, place.z)))

    def relay(self):
        place = self.place
        for d in (1, 3, 2):
            block = self.held(place.down(d), across=True)
            remote(block, block, self.ps.at[d - 1], self.pr.at[d - 1], (self.pair, place.z)).wait_recv()
            self.go(remote(block, block, self.cs.at[1, d - 1], self.cr.at[1, d - 1], (place.sibling, place.z)))

    def ready(self):
        place = self.place
        for d in (1, 3, 2):
            for across in (False, True)[:1 if self.pair is None else 2]:
                block = self.held(place.down(d), across=across, other=True)
                i = 1 if across else 0
                remote(block, block, self.cs.at[i, d - 1], self.cr.at[i, d - 1], (place.sibling, place.z)).wait_recv()

    def finish(self):
        for copy in self.moved:
            copy.wait_send()


class Reduction:
    def __init__(self, place, part, pair, comb, slots, total, plane, out, sems):
        self.place = place
        self.part, self.pair, self.comb, self.slots = part, pair, comb, slots
        self.total, self.plane, self.out = total, plane, out
        (self.pair_s, self.pair_r, self.col_s, self.col_r, self.comb_r, self.plane_s, self.plane_r,
         self.back_s, self.back_r, self.core_s, self.core_r) = sems
        self.sent = []
        self.chip = lax.div(place.c, 2)

    def peer(self, k):
        return (2 * lax.rem(self.chip + k, 4) + self.place.core, self.place.z)

    def go(self, copy):
        copy.start()
        self.sent.append(copy)

    def pair_start(self):
        place = self.place
        self.go(remote(self.part.at[1 - place.core], self.pair, self.pair_s.at[0], self.pair_r.at[0], (place.sibling, place.z)))

    def own(self, zz):
        return self.part.at[self.place.core, zz]

    def end_copy(self, i):
        place = self.place
        upper = lax.div(place.z, 3)
        near, far = 1 + upper, 2 - upper
        goal = (3 - place.z, near, far)[i]
        target = (self.comb, self.slots.at[0], self.slots.at[2])[i]
        arrival = (self.comb_r.at[0], self.col_r.at[0], self.col_r.at[2])[i]
        return remote(self.own(goal), target, self.col_s.at[i], arrival, (place.c, far if i == 2 else near))

    def middle_copy(self, i):
        place = self.place
        end = 3 * (place.z - 1)
        goal = (end, 3 - place.z, 3 - end)[i]
        return remote(self.own(goal), self.slots.at[i], self.col_s.at[i], self.col_r.at[i], (place.c, goal))

    def column_start(self):
        place = self.place
        core = place.core
        remote(self.pair, self.pair, self.pair_s.at[0], self.pair_r.at[0], (place.sibling, place.z)).wait_recv()

        def add(zz, carry):
            for chip in range(4):
                self.part[core, zz, chip] = (
                    self.part[core, zz, chip].astype(f32) + self.pair[zz, chip].astype(f32)
                ).astype(bf16)
            return carry

        lax.fori_loop(0, 4, add, 0)

        @pl.when(place.middle)
        def inner():
            self.middle_copy(0).start()
            self.middle_copy(1).start()

        @pl.when(jnp.logical_not(place.middle))
        def outer():
            for i in range(3):
                self.end_copy(i).start()

    def column_combine(self):
        place = self.place
        core = place.core

        @pl.when(place.middle)
        def inner():
            self.end_copy(0).wait_recv()
            goal = 3 - 3 * (place.z - 1)
            for chip in range(4):
                self.part[core, goal, chip] = (
                    self.part[core, goal, chip].astype(f32) + self.comb[chip].astype(f32)
                ).astype(bf16)
            self.middle_copy(2).start()

    def plane_start(self):
        place = self.place
        core, z = place.core, place.z
        self.end_copy(1).wait_recv()
        self.end_copy(2).wait_recv()

        @pl.when(place.middle)
        def inner():
            self.middle_copy(1).wait_recv()
            for chip in range(4):
                self.total[chip] = (
                    self.part[core, z, chip].astype(f32) + self.slots[0, chip].astype(f32)
                    + self.slots[1, chip].astype(f32) + self.slots[2, chip].astype(f32)
                ).astype(bf16)

        @pl.when(jnp.logical_not(place.middle))
        def outer():
            for chip in range(4):
                self.total[chip] = (
                    self.part[core, z, chip].astype(f32) + self.slots[0, chip].astype(f32)
                    + self.slots[2, chip].astype(f32)
                ).astype(bf16)

        for k in range(1, 4):
            self.go(remote(
                self.total.at[lax.rem(self.chip + k, 4)], self.plane.at[k - 1],
                self.plane_s.at[k - 1], self.plane_r.at[k - 1], self.peer(k),
            ))

    def back_start(self):
        place = self.place
        for k in range(1, 4):
            slot = self.plane.at[k - 1]
            remote(slot, slot, self.plane_s.at[k - 1], self.plane_r.at[k - 1], self.peer(k)).wait_recv()
        total = self.total[self.chip].astype(f32)
        for k in range(3):
            total = total + self.plane[k].astype(f32)
        self.out[place.c] = total.astype(bf16)
        mine = self.out.at[place.c]
        for k in range(1, 4):
            self.go(remote(mine, mine, self.back_s.at[k - 1], self.back_r.at[k - 1], self.peer(k)))
        self.go(remote(mine, mine, self.core_s.at[0], self.core_r.at[0], (place.sibling, place.z)))

    def relay(self):
        place = self.place
        for k in range(1, 4):
            slot = self.out.at[2 * lax.rem(self.chip + 4 - k, 4) + place.core]
            remote(slot, slot, self.back_s.at[k - 1], self.back_r.at[k - 1], self.peer(k)).wait_recv()
            self.go(remote(slot, slot, self.core_s.at[k], self.core_r.at[k], (place.sibling, place.z)))

    def finish(self):
        place = self.place
        for k in range(4):
            slot = self.out.at[2 * lax.rem(self.chip + 4 - k, 4) + 1 - place.core]
            remote(slot, slot, self.core_s.at[k], self.core_r.at[k], (place.sibling, place.z)).wait_recv()
        for copy in self.sent:
            copy.wait_send()

        @pl.when(place.middle)
        def inner():
            for i in range(3):
                self.middle_copy(i).wait_send()

        @pl.when(jnp.logical_not(place.middle))
        def outer():
            for i in range(3):
                self.end_copy(i).wait_send()


class PlaneFirst:
    def __init__(self, place, part, pair, plane, quarter, column, out, sems):
        self.place = place
        self.part, self.pair, self.plane = part, pair, plane
        self.quarter, self.column, self.out = quarter, column, out
        self.s1, self.r1, self.s2, self.r2, self.s3, self.r3, self.s4, self.r4, self.s5, self.r5 = sems
        self.sent = []
        self.chip = lax.div(place.c, 2)

    def other(self, k):
        return lax.rem(self.chip + k, 4)

    def before(self, k):
        return lax.rem(self.chip + 4 - k, 4)

    def peer(self, k):
        return (2 * self.other(k) + self.place.core, self.place.z)

    def go(self, copy):
        copy.start()
        self.sent.append(copy)

    def pair_start(self):
        p = self.place
        self.go(remote(self.part.at[1 - p.core], self.pair, self.s1, self.r1, (p.sibling, p.z)))

    def plane_start(self):
        p = self.place
        remote(self.pair, self.pair, self.s1, self.r1, (p.sibling, p.z)).wait_recv()

        def add(chip, carry):
            for zz in range(4):
                self.part[p.core, chip, zz] = (
                    self.part[p.core, chip, zz].astype(f32) + self.pair[chip, zz].astype(f32)
                ).astype(bf16)
            return carry

        lax.fori_loop(0, 4, add, 0)
        for k in range(1, 4):
            self.go(remote(self.part.at[p.core, self.other(k)], self.plane.at[k - 1], self.s2.at[k - 1], self.r2.at[k - 1], self.peer(k)))

    def column_start(self):
        p = self.place
        for k in range(1, 4):
            remote(self.plane.at[k - 1], self.plane.at[k - 1], self.s2.at[k - 1], self.r2.at[k - 1], self.peer(k)).wait_recv()

        def add(zz, carry):
            total = self.part[p.core, self.chip, zz].astype(f32)
            for k in range(3):
                total = total + self.plane[k, zz].astype(f32)
            self.quarter[zz] = total.astype(bf16)
            return carry

        lax.fori_loop(0, 4, add, 0)
        for d in (1, 3, 2):
            self.go(remote(self.quarter.at[p.up(d)], self.column.at[d - 1], self.s3.at[d - 1], self.r3.at[d - 1], (p.c, p.up(d))))

    def back_start(self):
        p = self.place
        for d in (1, 3, 2):
            remote(self.column.at[d - 1], self.column.at[d - 1], self.s3.at[d - 1], self.r3.at[d - 1], (p.c, p.up(d))).wait_recv()
        total = self.quarter[p.z].astype(f32)
        for d in range(3):
            total = total + self.column[d].astype(f32)
        self.out[p.c] = total.astype(bf16)
        mine = self.out.at[p.c]
        for k in range(1, 4):
            self.go(remote(mine, mine, self.s4.at[k - 1], self.r4.at[k - 1], self.peer(k)))
        self.go(remote(mine, mine, self.s5.at[0], self.r5.at[0], (p.sibling, p.z)))

    def relay(self):
        p = self.place
        for k in range(1, 4):
            slot = self.out.at[2 * self.before(k) + p.core]
            remote(slot, slot, self.s4.at[k - 1], self.r4.at[k - 1], self.peer(k)).wait_recv()
            self.go(remote(slot, slot, self.s5.at[k], self.r5.at[k], (p.sibling, p.z)))

    def finish(self):
        p = self.place
        for k in range(4):
            slot = self.out.at[2 * self.before(k) + 1 - p.core]
            remote(slot, slot, self.s5.at[k], self.r5.at[k], (p.sibling, p.z)).wait_recv()
        for copy in self.sent:
            copy.wait_send()


class Exchange:
    def __init__(self, place, pool, send, recv):
        self.place, self.pool, self.send, self.recv = place, pool, send, recv
        self.sent = []
        shift = place.sibling - place.c
        self.across = place.x_next + place.y_next - place.c
        self.from_sibling = (place.sibling, place.x_next + shift, place.y_next + shift, self.across + shift)

    def go(self, mb, i, j, owner, target, rows=None):
        block = self.pool.at[mb * 8 + owner]
        if rows is not None:
            block = block.at[rows]
        copy = remote(block, block, self.send.at[mb, i], self.recv.at[mb, j], (target, self.place.z))
        copy.start()
        self.sent.append(copy)

    def take(self, mb, j, owner, rows=None):
        block = self.pool.at[mb * 8 + owner]
        if rows is not None:
            block = block.at[rows]
        remote(block, block, self.send.at[mb, 0], self.recv.at[mb, j], (self.place.sibling, self.place.z)).wait_recv()

    def start(self, mb):
        place = self.place
        self.go(mb, 0, 0, place.c, place.x_next)
        self.go(mb, 1, 1, place.c, place.y_next)
        self.go(mb, 2, 4, place.c, place.sibling)

    def relay(self, mb):
        place = self.place
        half = self.pool.shape[1] // 2
        self.take(mb, 0, place.x_next)
        self.go(mb, 3, 2, place.x_next, place.y_next, pl.ds(0, half))
        self.take(mb, 1, place.y_next)
        self.go(mb, 4, 3, place.y_next, place.x_next, pl.ds(half, half))
        self.go(mb, 5, 5, place.x_next, place.sibling)
        self.go(mb, 6, 6, place.y_next, place.sibling)

    def last(self, mb):
        half = self.pool.shape[1] // 2
        self.take(mb, 2, self.across, pl.ds(0, half))
        self.take(mb, 3, self.across, pl.ds(half, half))
        self.go(mb, 7, 7, self.across, self.place.sibling)

    def ready(self, mb):
        for k, owner in enumerate(self.from_sibling):
            self.take(mb, 4 + k, owner)

    def finish(self):
        for copy in self.sent:
            copy.wait_send()


class ColumnSum:
    def __init__(self, place, part, column, out, sems):
        self.place, self.part, self.column, self.out = place, part, column, out
        self.col_s, self.col_r, self.back_s, self.back_r, self.core_s, self.core_r = sems
        self.sent = []
        self.chip = lax.div(place.c, 2)

    def peer(self, k):
        return (2 * lax.rem(self.chip + k, 4) + self.place.core, self.place.z)

    def go(self, copy):
        copy.start()
        self.sent.append(copy)

    def column_copy(self, d):
        place = self.place
        return remote(
            self.part.at[place.up(d)], self.column.at[d - 1], self.col_s.at[d - 1], self.col_r.at[d - 1],
            (place.c, place.up(d)),
        )

    def column_start(self):
        for d in (2, 1, 3):
            self.go(self.column_copy(d))

    def back_start(self):
        place = self.place
        for d in (1, 3, 2):
            self.column_copy(d).wait_recv()
        total = self.part[place.z].astype(f32)
        for d in range(3):
            total = total + self.column[d].astype(f32)
        self.out[place.c] = total.astype(bf16)
        mine = self.out.at[place.c]
        for k in range(1, 4):
            self.go(remote(mine, mine, self.back_s.at[k - 1], self.back_r.at[k - 1], self.peer(k)))
        self.go(remote(mine, mine, self.core_s.at[0], self.core_r.at[0], (place.sibling, place.z)))

    def relay(self):
        place = self.place
        for k in range(1, 4):
            slot = self.out.at[2 * lax.rem(self.chip + 4 - k, 4) + place.core]
            remote(slot, slot, self.back_s.at[k - 1], self.back_r.at[k - 1], self.peer(k)).wait_recv()
            self.go(remote(slot, slot, self.core_s.at[k], self.core_r.at[k], (place.sibling, place.z)))

    def finish(self):
        place = self.place
        for k in range(4):
            slot = self.out.at[2 * lax.rem(self.chip + 4 - k, 4) + 1 - place.core]
            remote(slot, slot, self.core_s.at[k], self.core_r.at[k], (place.sibling, place.z)).wait_recv()
        for copy in self.sent:
            copy.wait_send()


def layer_kernel(
    starts_ref, wq_ref, wk_ref, wv_ref, qb_ref, vb_ref, ob_ref, fg_ref, fs_ref, rb_ref, sg_ref, ss_ref, hb_ref, x_hbm, y_hbm, gx_hbm, gy_hbm, wo_hbm, wh_hbm, wr_hbm,
    xn_hbm, yn_hbm, xg_hbm, keep_hbm, red_out, hid_out, low_out, thin_out, vec_out,
    x_buf, y_buf, gx_buf, gy_buf, wt, wo, wh, wr, vecs, bias_cols, head_w, made, qkv, rows_a, rows_b,
    head, mixed, log_total, pool, first_low, second_grad, branch_grad, slope, dstage, dhead, two_grad, inv_one,
    dq_turned, delta, got,
    red_part, red_pair, red_comb, red_slots, red_total, red_plane,
    wide_part, wide_pair, wide_comb, wide_slots, wide_total, wide_plane,
    rest_part, rest_pair, rest_plane, rest_quarter, rest_column,
    thin_total, thin_part, thin_column,
    vec_part, vec_column, vec_plane, sums,
    load_sems, store_sems, own_sems, keep_sems, vz_s, vz_r, ex_s, ex_r, hw_s, hw_r,
    gz_s, gz_r, gp_s, gp_r, gc_s, gc_r,
    o_s, o_r, d_s, d_r, kv_s, kv_r,
    pair_s, pair_r, col_s, col_r, comb_r, plane_s, plane_r, back_s, back_r, core_s, core_r,
    vc_s, vc_r, vp_s, vp_r,
):
    place = Place()
    c, z, core = place.c, place.z, place.core
    mbs, seq, width = x_buf.shape
    hidden = wh.shape[1]
    feat = width // HEADS
    shard = width // 4
    sends = []

    def go(copy):
        copy.start()
        sends.append(copy)

    loads = [
        [pltpu.make_async_copy(src.at[mb], dst.at[mb], load_sems.at[i, mb]) for mb in range(mbs)]
        for i, (src, dst) in enumerate(((x_hbm, x_buf), (y_hbm, y_buf), (gx_hbm, gx_buf), (gy_hbm, gy_buf)))
    ]
    knock(place)
    for copy in loads[0]:
        copy.start()
    own_column = aligned(z * shard, shard, 128)
    for m, w_ref in enumerate((wq_ref, wk_ref, wv_ref)):
        wt[m, :, :, own_column] = turned(w_ref[...]).reshape(8, feat, shard)
    head_w[:, :, own_column] = wt[:, c, :, own_column]
    shorts = [ref[...].reshape(1, shard) for ref in (qb_ref, vb_ref, ob_ref, fg_ref, fs_ref, rb_ref, sg_ref, ss_ref)]
    shorts += [hb_ref[r * 128:(r + 1) * 128].reshape(1, 128) for r in range(4)]
    for row, short in enumerate(shorts):
        vecs[z, row:row + 1, :] = short.astype(f32)
    vecs[z, 12:16, :] = jnp.zeros((4, 128), f32)
    for copy in loads[0]:
        copy.wait()
    for mb in range(mbs):
        pool[mb * 8 + c] = x_buf[mb].astype(bf16)
    enter()

    exchange = Exchange(place, pool, ex_s, ex_r)

    def head_copy(d):
        return remote(
            wt.at[:, c, :, own_column], head_w.at[:, :, own_column], hw_s.at[d - 1], hw_r.at[d - 1], (c, place.up(d))
        )

    exchange.start(0)
    for d in (2, 1, 3):
        go(head_copy(d))
    for d in (2, 1, 3):
        go(remote(vecs.at[z], vecs.at[z], vz_s.at[d - 1], vz_r.at[d - 1], (c, place.up(d))))
    exchange.start(1)

    def sems_of(i):
        return tuple(sem.at[i] for sem in (gz_s, gz_r, gp_s, gp_r, gc_s, gc_r))

    def turned_at(zz, part):
        return wt.at[:, pl.ds(part * 4, 4), :, aligned(zz * shard, shard, 128)]

    def rows_at(full, count, begin, rows):
        def at(zz, part):
            return full.at[aligned(zz * count + begin + part * rows, rows, 16)]
        return at

    along_x, along_y, alone = (place.x_next, place.x), (place.y_next, place.y), (None, 0)
    gathers = []
    owned = []
    plans = ((wo_hbm, wo, (along_x,)), (wh_hbm, wh, (along_x, along_y)), (wr_hbm, wr, (along_x, along_y)))
    for i, (src, full, chunks) in enumerate(plans):
        count = src.shape[0]
        for chunk, (pair, side) in enumerate(chunks):
            rows = count // len(chunks) // 4
            begin = chunk * (count // len(chunks))
            mine = src.at[aligned(begin + (2 * side + core) * rows, rows, 16)]
            gathers.append(Gather(place, mine, rows_at(full, count, begin, rows), sems_of(len(gathers)), pair, side))
        owned.append(pltpu.make_async_copy(src, full.at[aligned(z * count, count, 16)], own_sems.at[i]))
    gathers.append(Gather(place, turned_at(z, core), turned_at, sems_of(5)))
    g_out, g_in_a, g_in_b, g_red_a, g_red_b, g_proj = gathers
    for gather in gathers:
        gather.start()
    for copy in owned:
        copy.start()
    for group in loads[1:]:
        for copy in group:
            copy.start()
    exchange.relay(0)
    exchange.start(2)
    for d in (1, 3, 2):
        slot = vecs.at[place.down(d)]
        remote(slot, slot, vz_s.at[d - 1], vz_r.at[d - 1], (c, place.up(d))).wait_recv()
        head_copy(d).wait_recv()

    def vec(row):
        return jnp.concatenate([vecs[zz, row:row + 1, :] for zz in range(4)], axis=1)

    for i in range(2):
        bias_cols[i] = jnp.transpose(vec(i))
    q_bias, v_bias = [bias_cols[i, aligned(c * feat, feat, 8), :] for i in range(2)]
    exchange.last(0)
    exchange.relay(1)
    g_out.arrive()
    keeps = [pltpu.make_async_copy(pool.at[i], keep_hbm.at[i], keep_sems.at[i]) for i in range(mbs * 8)]
    backs = [pltpu.make_async_copy(keep_hbm.at[i], pool.at[i], keep_sems.at[i]) for i in range(mbs * 8)]

    def project(mb):
        for j in range(8):
            out = dots(head_w[...].reshape(3 * feat, width), pool[mb * 8 + j], 1, 1)
            query = (out[0:feat] + q_bias).astype(bf16).astype(f32) * 0.125
            qkv[0, mb, j] = query.astype(bf16)
            qkv[1, mb, j] = out[feat:2 * feat].astype(bf16)
            qkv[2, mb, j] = (out[2 * feat:] + v_bias).astype(bf16)

    forward_hooks = {
        (0, 0): [g_in_a.arrive],
        (0, 3): [lambda: exchange.last(1)],
        (0, 6): [lambda: exchange.relay(2), g_out.relay],
        (0, 7): [g_in_b.arrive],
        (1, 3): [lambda: exchange.last(2)],
        (1, 7): [g_in_a.relay],
        (2, 2): [g_red_a.arrive],
        (2, 4): [g_in_b.relay],
        (2, 6): [g_red_b.arrive],
    }
    def block_scores_of(mb, i):
        begin, span = i * seq, (i + 1) * seq
        scores = jnp.dot(rows_a[0:span, :], qkv[0, mb, i], preferred_element_type=f32)
        key_pos = lax.broadcasted_iota(jnp.int32, (span, 1), 0)
        query_pos = lax.broadcasted_iota(jnp.int32, (1, seq), 1) + begin
        allowed = (key_pos >= starts_ref[mb, :, begin:span]) & (key_pos <= query_pos)
        scores = jnp.where(allowed, scores, NEG)
        return scores, jnp.max(scores, axis=0, keepdims=True)

    def attend_block(mb, i, scores, top):
        weights = jnp.exp(scores - top)
        total = jnp.sum(weights, axis=0, keepdims=True)
        values = jnp.concatenate([qkv[2, mb, j] for j in range(i + 1)], axis=1)
        out = jnp.dot(values, weights.astype(bf16), preferred_element_type=f32)
        head[mb, i] = (out / total).astype(bf16)
        log_total[mb, :, i * seq:(i + 1) * seq] = top + jnp.log(total)
        for hook in forward_hooks.get((mb, i), []):
            hook()

    for mb in range(mbs):
        exchange.ready(mb)
        project(mb)
        for copy in keeps[mb * 8:mb * 8 + 8]:
            copy.start()
        for j in range(8):
            rows_a[j * seq:(j + 1) * seq, :] = turned(qkv[1, mb, j])
        waiting = None
        for i in range(8):
            current = (i,) + block_scores_of(mb, i)
            if waiting is not None:
                attend_block(mb, *waiting)
            waiting = current
        attend_block(mb, *waiting)
        mixed[mb, c] = head[mb, c]
        for k in range(1, 8):
            go(remote(
                head.at[mb, place.ring(k)], mixed.at[mb, c], o_s.at[mb, k - 1], o_r.at[mb, k - 1], (place.ring(k), z)
            ))

    exchange.finish()
    for copy in owned + keeps:
        copy.wait()
    for group in loads[1:]:
        for copy in group:
            copy.wait()
    b_output, gain_one, shift_one, b_reduce, gain_two, shift_two = [vec(row) for row in range(2, 8)]
    b_hidden = jnp.concatenate([vecs[zz, 8 + r:9 + r, :] for zz in range(4) for r in range(4)], axis=1)
    sums[...] = jnp.zeros_like(sums)

    def add_row(row, block):
        sums[row:row + 1, :] += jnp.sum(block, axis=0, keepdims=True)

    def reduction(i, part, pair, comb, slots, total, plane, out):
        return Reduction(place, part, pair, comb, slots, total, plane, out, tuple(
            s.at[i] for s in (pair_s, pair_r, col_s, col_r, comb_r, plane_s, plane_r, back_s, back_r, core_s, core_r)
        ))

    red = reduction(0, red_part, red_pair, red_comb, red_slots, red_total, red_plane, red_out)
    wide = reduction(1, wide_part, wide_pair, wide_comb, wide_slots, wide_total, wide_plane, hid_out)
    rest = PlaneFirst(
        place, rest_part, rest_pair, rest_plane, rest_quarter, rest_column, low_out,
        (pair_s.at[2, 0], pair_r.at[2, 0]) + tuple(
            s.at[2] for s in (plane_s, plane_r, col_s, col_r, back_s, back_r, core_s, core_r)),
    )
    thin = ColumnSum(
        place, thin_part, thin_column, thin_out,
        tuple(s.at[3] for s in (col_s, col_r, back_s, back_r, core_s, core_r)),
    )
    quarter = hidden // 4
    quarters = [slice(q * quarter, (q + 1) * quarter) for q in range(4)]
    spans = [slice(mb * seq, (mb + 1) * seq) for mb in range(mbs)]
    stores = []

    def store(src, dst, i, mb):
        copy = pltpu.make_async_copy(src.at[mb], dst.at[mb], store_sems.at[i, mb])
        copy.start()
        stores.append(copy)

    def dense_in(mb):
        rows = spans[mb]
        for k in range(1, 8):
            slot = mixed.at[mb, place.source(k)]
            remote(slot, slot, o_s.at[mb, k - 1], o_r.at[mb, k - 1], (place.ring(k), z)).wait_recv()
        branch = dots(mixed[mb].reshape(width, seq), wo[...], 0, 0) + b_output
        value = x_buf[mb]
        x_first, normed, inv_std = norm_forward(value + branch, gain_one, shift_one)
        x_buf[mb] = normed
        inv_one[mb] = inv_std
        y_buf[mb] = y_buf[mb] + branch
        first_low[rows, :] = x_first.astype(bf16)
        for q, cols in enumerate(quarters):
            pre = jnp.dot(first_low[rows, :], wh[:, cols], preferred_element_type=f32) + b_hidden[:, cols]
            phi = 0.5 * (1.0 + lax.erf(pre * root_half))
            pool[q * mbs + mb] = (pre * phi).astype(bf16)
            slope[rows, cols] = phi + pre * inv_root_tau * jnp.exp(-0.5 * pre * pre)

    def dense_out(mb):
        rows = spans[mb]
        hid = jnp.concatenate([pool[q * mbs + mb] for q in range(4)], axis=1)
        second = jnp.dot(hid, wr[...], preferred_element_type=f32) + b_reduce
        x_next, normed, inv_std = norm_forward(x_buf[mb] * gain_one + shift_one + second, gain_two, shift_two)
        y_buf[mb] = y_buf[mb] + second
        store(y_buf, yn_hbm, 1, mb)
        upstream = gx_buf[mb]
        up = norm_backward(upstream, normed, inv_std, gain_two)
        two_grad[mb] = up
        add_row(4, upstream * normed)
        add_row(5, upstream)
        gx_buf[mb] = x_next
        store(gx_buf, xn_hbm, 0, mb)
        second_low = (up + gy_buf[mb]).astype(bf16)
        second_grad[rows, :] = second_low
        add_row(3, second_low.astype(f32))

    def dense_back(mb):
        rows = spans[mb]
        for q, cols in enumerate(quarters):
            low = (dots(second_grad[rows, :], wr[cols, :], 1, 1) * slope[rows, cols]).astype(bf16)
            pool[(4 + q) * mbs + mb] = low
            add_row(6 + q, low.astype(f32))
        hid_grad = jnp.concatenate([pool[(4 + q) * mbs + mb] for q in range(4)], axis=1)
        first_up = two_grad[mb] + dots(hid_grad, wh[...], 1, 1)
        one_grad = norm_backward(first_up, x_buf[mb], inv_one[mb], gain_one)
        add_row(1, first_up * x_buf[mb])
        add_row(2, first_up)
        branch_low = (one_grad + gy_buf[mb]).astype(bf16)
        gy_buf[mb] = one_grad
        branch_grad[rows, :] = branch_low
        add_row(0, branch_low.astype(f32))
        dstage[mb] = dots(wo[...], branch_low, 1, 1).astype(bf16).reshape(8, feat, seq)
        dhead[mb, c] = dstage[mb, c]
        for k in range(1, 8):
            go(remote(
                dstage.at[mb, place.ring(k)], dhead.at[mb, c], d_s.at[mb, k - 1], d_r.at[mb, k - 1], (place.ring(k), z)
            ))

    g_out.ready()
    g_in_a.ready()
    g_in_b.ready()
    for mb in range(mbs):
        dense_in(mb)
        if mb == 0:
            g_red_a.relay()
        if mb == 1:
            g_red_b.relay()
    g_red_a.ready()
    g_red_b.ready()
    for mb in range(mbs):
        dense_out(mb)
    second_all = turned(second_grad[...])
    for q, cols in enumerate(quarters):
        hid = pool[q * mbs:(q + 1) * mbs].reshape(mbs * seq, quarter)
        part = jnp.dot(second_all, hid, preferred_element_type=f32).astype(bf16)
        for owner in range(8):
            red_part[owner % 2, q, owner // 2] = part[owner * 64:(owner + 1) * 64, :]
    red.pair_start()
    dense_back(0)
    red.column_start()
    for mb in range(1, mbs):
        dense_back(mb)
    first_all = turned(first_low[...])
    for q, cols in enumerate(quarters):
        hid_grad = pool[(4 + q) * mbs:(5 + q) * mbs].reshape(mbs * seq, quarter)
        part = jnp.dot(first_all, hid_grad, preferred_element_type=f32).astype(bf16)
        for zz in range(4):
            for owner in range(8):
                begin = zz * shard + owner * 16
                wide_part[owner % 2, zz, owner // 2, 16 * q:16 * q + 16, :] = part[begin:begin + 16, :]
    wide.pair_start()
    mixed_all = jnp.concatenate([mixed[mb].reshape(width, seq) for mb in range(mbs)], axis=1)
    part = jnp.dot(mixed_all, branch_grad[...], preferred_element_type=f32).astype(bf16)
    for zz in range(4):
        for owner in range(8):
            begin = zz * shard + owner * 16
            rest_part[owner % 2, owner // 2, zz, :, :] = part[begin:begin + 16, :]
    rest.pair_start()
    for copy in backs:
        copy.start()
    red.column_combine()

    ones = jnp.ones((8, 8 * seq), bf16)
    biases = [jnp.zeros((1, feat), f32), jnp.zeros((1, feat), f32)]

    def head_gradients(mb):
        if mb == 0:
            for copy in backs:
                copy.wait()
        block = jnp.concatenate([made[:, mb, j].reshape(3 * feat, seq) for j in range(8)], axis=1)
        rows = pool[mb * 8:(mb + 1) * 8].reshape(8 * seq, width)
        total = jnp.dot(block, rows, preferred_element_type=f32)
        thin_total[...] = total if mb == 0 else thin_total[...] + total
        biases[0] = biases[0] + dots(ones, block[0:feat], 1, 1)[0:1]
        biases[1] = biases[1] + dots(ones, block[2 * feat:], 1, 1)[0:1]

    hooks = {
        (0, 0): [wide.column_start, rest.plane_start],
        (0, 6): [rest.column_start],
        (0, 3): [g_proj.arrive],
        (1, 0): [red.plane_start],
        (1, 7): [wide.column_combine],
        (2, 0): [red.back_start],
        (2, 7): [red.relay],
    }

    def grad_copy(mb, j, source):
        return remote(made.at[:, mb, j], got.at[mb, :, source], kv_s.at[mb, j], kv_r.at[mb, source], (j, z))

    for mb in range(mbs):
        for k in range(1, 8):
            slot = dhead.at[mb, place.source(k)]
            remote(slot, slot, d_s.at[mb, k - 1], d_r.at[mb, k - 1], (place.ring(k), z)).wait_recv()
        for j in range(8):
            cols = slice(j * seq, (j + 1) * seq)
            rows_a[cols, :] = turned(qkv[0, mb, j])
            rows_b[cols, :] = turned(dhead[mb, j])
            delta[:, cols] = jnp.sum(dhead[mb, j].astype(f32) * head[mb, j].astype(f32), axis=0, keepdims=True)
        dq_turned[...] = jnp.zeros_like(dq_turned)
        for j in range(8):
            begin = j * seq
            span = 8 * seq - begin
            key_turned = qkv[1, mb, j]
            queries = jnp.concatenate([qkv[0, mb, i] for i in range(j, 8)], axis=1)
            grads = jnp.concatenate([dhead[mb, i] for i in range(j, 8)], axis=1)
            scores = jnp.dot(turned(key_turned), queries, preferred_element_type=f32)
            dprobs = jnp.dot(turned(qkv[2, mb, j]), grads, preferred_element_type=f32)
            key_pos = lax.broadcasted_iota(jnp.int32, (seq, 1), 0) + begin
            query_pos = lax.broadcasted_iota(jnp.int32, (1, span), 1) + begin
            allowed = (key_pos >= starts_ref[mb, :, begin:]) & (key_pos <= query_pos)
            probs = jnp.where(allowed, jnp.exp(scores - log_total[mb, :, begin:]), 0.0)
            score_grad = (probs * (dprobs - delta[:, begin:])).astype(bf16)
            value_made = jnp.dot(probs.astype(bf16), rows_b[begin:, :], preferred_element_type=f32)
            key_made = jnp.dot(score_grad, rows_a[begin:, :], preferred_element_type=f32)
            dq_turned[:, begin:] += jnp.dot(key_turned, score_grad, preferred_element_type=f32)
            made[1, mb, j] = jnp.transpose(key_made).astype(bf16)
            made[2, mb, j] = jnp.transpose(value_made).astype(bf16)
            made[0, mb, j] = (dq_turned[:, begin:begin + seq] * 0.125).astype(bf16)

            @pl.when(c == j)
            def keep():
                for m in range(3):
                    got[mb, m, c] = made[m, mb, j]

            @pl.when(c != j)
            def send():
                grad_copy(mb, j, c).start()

            for hook in hooks.get((mb, j), []):
                hook()
        head_gradients(mb)

    def x_gradient(mb):
        x_buf[mb] = gy_buf[mb] + dots(got[mb].reshape(3 * width, seq), wt[...].reshape(3 * width, width), 0, 0)
        copy = pltpu.make_async_copy(x_buf.at[mb], xg_hbm.at[mb], store_sems.at[2, mb])
        copy.start()
        stores.append(copy)

    low = thin_total[...].astype(bf16)
    for zz in range(4):
        thin_part[zz] = low[:, zz * shard:(zz + 1) * shard]
    thin.column_start()
    wide.plane_start()
    lane_head = lax.div(lax.broadcasted_iota(jnp.int32, (1, width), 1), feat)
    bias_q, bias_v = [jnp.where(lane_head == c, jnp.concatenate([b] * 8, axis=1), 0.0) for b in biases]
    for zz in range(4):
        cols = slice(zz * shard, (zz + 1) * shard)
        vec_part[zz, 0:1, :] = bias_q[:, cols]
        vec_part[zz, 1:2, :] = bias_v[:, cols]
        vec_part[zz, 2:8, :] = sums[0:6, cols]
        for r in range(4):
            vec_part[zz, 8 + r:9 + r, :] = sums[6 + zz:7 + zz, r * 128:(r + 1) * 128]
        vec_part[zz, 12:16, :] = jnp.zeros((4, 128), f32)
    for d in (1, 3, 2):
        go(remote(vec_part.at[place.up(d)], vec_column.at[d - 1], vc_s.at[d - 1], vc_r.at[d - 1], (c, place.up(d))))
    g_proj.ready()

    def take_gradients(mb):
        for k in range(1, 8):
            grad_copy(mb, 0, place.source(k)).wait_recv()
        x_gradient(mb)

    take_gradients(0)
    rest.back_start()
    thin.back_start()
    wide.back_start()
    for d in (1, 3, 2):
        slot = vec_column.at[d - 1]
        remote(slot, slot, vc_s.at[d - 1], vc_r.at[d - 1], (c, place.up(d))).wait_recv()
    vec_plane[c] = vec_part[z] + vec_column[0] + vec_column[1] + vec_column[2]
    for k in range(1, 8):
        go(remote(vec_plane.at[c], vec_plane.at[c], vp_s.at[k - 1], vp_r.at[k - 1], (place.ring(k), z)))
    take_gradients(1)
    rest.relay()
    thin.relay()
    wide.relay()
    take_gradients(2)
    for k in range(1, 8):
        slot = vec_plane.at[place.source(k)]
        remote(slot, slot, vp_s.at[k - 1], vp_r.at[k - 1], (place.ring(k), z)).wait_recv()
    total = vec_plane[0]
    for k in range(1, 8):
        total = total + vec_plane[k]
    vec_out[...] = total
    for reduced in (red, wide, rest, thin):
        reduced.finish()
    for gather in gathers:
        gather.finish()
    for copy in sends:
        copy.wait_send()
    for copy in stores:
        copy.wait()
    for j in range(8):
        @pl.when(c != j)
        def sent():
            for mb in range(mbs):
                grad_copy(mb, j, c).wait_send()


def layer_call(starts, wq, wk, wv, vectors, x, y, gx, gy, wo, wh, wr):
    mbs, seq, width = x.shape
    hidden = wh.shape[1]
    feat = width // HEADS
    count = HEADS * seq
    tokens = mbs * seq
    vm = pl.BlockSpec(memory_space=pltpu.VMEM)
    anym = pl.BlockSpec(memory_space=pl.ANY)
    dma = pltpu.SemaphoreType.DMA
    sds = jax.ShapeDtypeStruct
    V = pltpu.VMEM
    big = sds((mbs, seq, width), f32)

    def reduce_scratch(rows, cols):
        return [
            V((2, 4, 4, rows, cols), bf16), V((4, 4, rows, cols), bf16), V((4, rows, cols), bf16),
            V((3, 4, rows, cols), bf16), V((4, rows, cols), bf16), V((3, rows, cols), bf16),
        ]

    def plane_scratch(rows, cols):
        return [
            V((2, 4, 4, rows, cols), bf16), V((4, 4, rows, cols), bf16), V((3, 4, rows, cols), bf16),
            V((4, rows, cols), bf16), V((3, rows, cols), bf16),
        ]

    return pl.pallas_call(
        layer_kernel,
        out_shape=(
            big, big, big, sds((mbs * 8, seq, width), bf16), sds((8, 64, 512), bf16), sds((8, 64, 512), bf16), sds((8, 16, 512), bf16),
            sds((8, 192, 128), bf16), sds((16, 128), f32),
        ),
        in_specs=[vm] * 13 + [anym] * 7,
        out_specs=[anym] * 4 + [vm] * 5,
        scratch_shapes=[V((mbs, seq, width), f32)] * 4 + [
            V((3, 8, feat, width), bf16), V((width, width), bf16), V((width, hidden), bf16), V((hidden, width), bf16),
            V((4, 16, 128), f32), V((2, width, 1), f32), V((3, feat, width), bf16), V((3, mbs, 8, feat, seq), bf16), V((3, mbs, 8, feat, seq), bf16),
            V((count, feat), bf16), V((count, feat), bf16),
            V((mbs, 8, feat, seq), bf16), V((mbs, 8, feat, seq), bf16), V((mbs, 1, count), f32),
            V((mbs * 8, seq, width), bf16), V((tokens, width), bf16), V((tokens, width), bf16),
            V((tokens, width), bf16), V((tokens, hidden), f32), V((mbs, 8, feat, seq), bf16), V((mbs, 8, feat, seq), bf16),
            V((mbs, seq, width), f32), V((mbs, seq, 1), f32),
            V((feat, count), f32), V((1, count), f32), V((mbs, 3, 8, feat, seq), bf16),
        ] + reduce_scratch(64, 512) + reduce_scratch(64, 512) + plane_scratch(16, 512) + [
            V((3 * feat, width), f32), V((4, 192, 128), bf16), V((3, 192, 128), bf16),
        ] + [
            V((4, 16, 128), f32), V((3, 16, 128), f32), V((8, 16, 128), f32), V((16, width), f32),
            dma((4, mbs)), dma((3, mbs)), dma((3,)), dma((mbs * 8,)), dma((3,)), dma((3,)),
            dma((mbs, 8)), dma((mbs, 8)), dma((3,)), dma((3,)),
            dma((6, 3)), dma((6, 3)), dma((6, 3)), dma((6, 3)), dma((6, 2, 3)), dma((6, 2, 3)),
            dma((mbs, 7)), dma((mbs, 7)), dma((mbs, 7)), dma((mbs, 7)),
            dma((mbs, 8)), dma((mbs, 8)),
            dma((4, 1)), dma((4, 1)), dma((4, 3)), dma((4, 3)), dma((4, 1)), dma((4, 3)), dma((4, 3)),
            dma((4, 3)), dma((4, 3)), dma((4, 4)), dma((4, 4)),
            dma((3,)), dma((3,)), dma((7,)), dma((7,)),
        ],
        compiler_params=pltpu.CompilerParams(collective_id=1, has_side_effects=True, vmem_limit_bytes=VMEM_LIMIT),
        name="layer",
    )(starts, wq, wk, wv, *vectors, x, y, gx, gy, wo, wh, wr)


def unpack_kernel(
    red_in, hid_in, low_in, thin_in, vec_ref, xn_in, yn_in, xg_in,
    xn_out, yn_out, xg_out, wq_out, wk_out, wv_out, wo_out, wh_out, wr_out,
    qb_ref, vb_ref, ob_ref, fg_ref, fs_ref, rb_ref, sg_ref, ss_ref, hb_ref,
    red, hid, low, thin, held, wq, wk, wv, wo, wh, wr, in_sems, out_sems, sems, held_sems,
):
    mbs = held.shape[1]
    big = ((xn_in, xn_out), (yn_in, yn_out), (xg_in, xg_out))
    small = [
        pltpu.make_async_copy(src, dst, in_sems.at[i])
        for i, (src, dst) in enumerate(((red_in, red), (thin_in, thin), (hid_in, hid), (low_in, low)))
    ]
    loads = [
        [pltpu.make_async_copy(src.at[mb], held.at[i, mb], sems.at[i, mb]) for mb in range(mbs)]
        for i, (src, _) in enumerate(big)
    ]
    stores = [
        [pltpu.make_async_copy(held.at[i, mb], dst.at[mb], held_sems.at[i, mb]) for mb in range(mbs)]
        for i, (_, dst) in enumerate(big)
    ]
    done = []

    def turn_round(i):
        for mb in range(mbs):
            loads[i][mb].wait()
            stores[i][mb].start()

    def put(src, dst, i):
        copy = pltpu.make_async_copy(src, dst, out_sems.at[i])
        copy.start()
        done.append(copy)

    for copy in small:
        copy.start()
    for group in loads:
        for copy in group:
            copy.start()
    small[0].wait()
    wr[...] = jnp.transpose(jnp.concatenate([red[owner] for owner in range(8)], axis=0).astype(f32))
    put(wr, wr_out, 0)
    turn_round(0)
    small[1].wait()
    for m, (out, target) in enumerate(((wq, wq_out), (wk, wk_out), (wv, wv_out))):
        stacked = jnp.concatenate([thin[owner, m * 64:(m + 1) * 64, :] for owner in range(8)], axis=0)
        out[...] = jnp.transpose(stacked.astype(f32))
        put(out, target, 1 + m)
    turn_round(1)
    small[2].wait()
    small[3].wait()
    for owner in range(8):
        rows = slice(owner * 16, (owner + 1) * 16)
        for q in range(4):
            wh[rows, q * 512:(q + 1) * 512] = hid[owner, 16 * q:16 * q + 16, :].astype(f32)
        wo[rows, :] = low[owner].astype(f32)
    put(wh, wh_out, 4)
    put(wo, wo_out, 5)
    turn_round(2)
    for row, out in enumerate((qb_ref, vb_ref, ob_ref, fg_ref, fs_ref, rb_ref, sg_ref, ss_ref)):
        out[...] = vec_ref[row]
    for r in range(4):
        hb_ref[r * 128:(r + 1) * 128] = vec_ref[8 + r]
    for group in stores:
        for copy in group:
            copy.wait()
    for copy in done:
        copy.wait()


def unpack_call(red, hid, low, thin, vec, xn, yn, xg):
    mbs = xn.shape[0]
    vm = pl.BlockSpec(memory_space=pltpu.VMEM)
    anym = pl.BlockSpec(memory_space=pl.ANY)
    sds = jax.ShapeDtypeStruct
    V = pltpu.VMEM
    big = sds(xn.shape, f32)
    weights = [(128, 512)] * 4 + [(128, 2048), (512, 512)]
    dma = pltpu.SemaphoreType.DMA
    return pl.pallas_call(
        unpack_kernel,
        out_shape=(big, big, big) + tuple(sds(w, f32) for w in weights) + (sds((128,), f32),) * 8 + (sds((512,), f32),),
        in_specs=[anym] * 4 + [vm] + [anym] * 3,
        out_specs=[anym] * 9 + [vm] * 9,
        scratch_shapes=[V(a.shape, bf16) for a in (red, hid, low, thin)] + [V((3,) + xn.shape, f32)]
        + [V(w, f32) for w in weights] + [dma((4,)), dma((6,)), dma((3, mbs)), dma((3, mbs))],
        compiler_params=pltpu.CompilerParams(vmem_limit_bytes=VMEM_LIMIT),
        name="unpack",
    )(red, hid, low, thin, vec, xn, yn, xg)


def head_shards(
    x_stream, y_stream, grad_x, grad_y, doc_start, query_weight, query_bias, key_weight, value_weight, value_bias,
    output_weight, output_bias, first_gain, first_shift, hidden_weight, hidden_bias, reduce_weight, reduce_bias,
    second_gain, second_shift,
):
    mbs = x_stream.shape[1]
    vectors = (query_bias, value_bias, output_bias, first_gain, first_shift, reduce_bias, second_gain, second_shift, hidden_bias)
    starts = doc_start.reshape(mbs, 1, -1)
    xn, yn, xg, _, red, hid, low, thin, small = layer_call(
        starts, query_weight, key_weight, value_weight, vectors, x_stream[0], y_stream[0], grad_x[0], grad_y[0],
        output_weight, hidden_weight, reduce_weight,
    )
    xn, yn, xg, g_q, g_k, g_v, g_o, g_h, g_r, qb, vb, ob, fg, fs, rb, sg, ss, hb = unpack_call(
        red, hid, low, thin, small, xn, yn, xg
    )
    return (
        xn[None], yn[None], xg[None], g_q, qb, g_k, g_v, vb, g_o, ob, fg, fs, g_h, hb, g_r, rb, sg, ss,
    )


def solution(mesh):
    in_specs = (
        P("fsdp", None, "ctx", None),
        P("fsdp", None, "ctx", None),
        P("fsdp", None, "ctx", None),
        P("fsdp", None, "ctx", None),
        P("fsdp", None, None),
        P("fsdp", None),
        P("fsdp"),
        P("fsdp", None),
        P("fsdp", None),
        P("fsdp"),
        P("fsdp", None),
        P("fsdp"),
        P("fsdp"),
        P("fsdp"),
        P("fsdp", None),
        P("fsdp"),
        P("fsdp", None),
        P("fsdp"),
        P("fsdp"),
        P("fsdp"),
    )
    out_specs = (
        P("fsdp", None, "ctx", None),
        P("fsdp", None, "ctx", None),
        P("fsdp", None, "ctx", None),
        P("fsdp", None),
        P("fsdp"),
        P("fsdp", None),
        P("fsdp", None),
        P("fsdp"),
        P("fsdp", None),
        P("fsdp"),
        P("fsdp"),
        P("fsdp"),
        P("fsdp", None),
        P("fsdp"),
        P("fsdp", None),
        P("fsdp"),
        P("fsdp"),
        P("fsdp"),
    )
    body = head_shards if mesh.shape["ctx"] == HEADS and mesh.shape["fsdp"] == 4 else shards
    return jax.shard_map(body, mesh=mesh, in_specs=in_specs, out_specs=out_specs, check_vma=False)
```
